512 devices in a mesh: region: 16 (over y, x), shard: 32 (over z, core).
Axes of the slice: x: 4, y: 4, z: 16, core: 2. Of those that a mesh axis runs over, the one named last changes fastest.
Arguments:
- tiles: bfloat16 [524288, 512], P(('region', 'shard')), may hold values from -6 to 6
- tile_block: int32 [524288], P(('region', 'shard')), may hold values from 0 to 15
- neighbors: int32 [8192, 64], P(('region', 'shard')), may hold values from 0 to 8191, as said below
- counts: int32 [8192], P(('region', 'shard')), may hold values from 1 to 64, as said below
- flows: int32 [8192, 64], P(('region', 'shard')), may hold values from 0 to 22, as said below
- w_anchor: bfloat16 [512, 1024], P('shard'), may hold values from -0.25 to 0.25
- w_dest: bfloat16 [512, 1024], P('shard'), may hold values from -0.25 to 0.25
- w_hidden: bfloat16 [1024, 1024], P('shard'), may hold values from -0.1875 to 0.1875
- w_out: bfloat16 [1024], replicated, may hold values from -0.1875 to 0.1875
Outputs:
- hidden_grad: float32 [1024, 1024], P('shard')
- out_grad: float32 [1024], replicated
- loss: float32 [], replicated
The draws below stay inside these ranges and needn't reach their ends.
Inputs may be any that keep to these rules, and one draw needn't show every extreme that they name: `neighbors`: every destination lies in the anchor's region, at most 32 blocks from the anchor in the region's order; the first counts slots hold distinct blocks, the others hold the anchor itself. `counts`: some anchor of every region has all 64 slots valid. `flows`: zero in slots at or beyond the anchor's count; the first slot holds at least one trip.
All inputs are finite; a program needn't handle non-finite values.
Results may differ from the reference program's by a relative error of at most 0.017.
Values may be sent and summed in bfloat16 or wider, within the bound.
A program may use at most 64 MiB of HBM per device.

```python
import jax
import jax.numpy as jnp
from jax import lax

D = 512
HID = 1024
NB = 64
BLK_DEV = 16
TILE_DEV = 1024
BLOCKS = 8192
TILES = 524288
N_REGION = 16
N_SHARD = 32


def neighbor_plan(key):
    reach = 2 * BLK_DEV
    width = 2 * reach + 1
    region_size = BLK_DEV * N_SHARD
    blocks = jnp.arange(BLOCKS, dtype=jnp.int32)
    local = blocks % region_size
    device = blocks // BLK_DEV
    offsets = jnp.arange(width, dtype=jnp.int32) - reach
    candidate = local[:, None] + offsets[None, :]
    inside = (candidate >= 0) & (candidate < region_size)
    available = jnp.sum(inside.astype(jnp.int32), axis=1)
    key_dense, key_count, key_order, key_flow = jax.random.split(key, 4)
    density = jax.random.randint(key_dense, (N_REGION * N_SHARD,), 1, 5)[device]
    draws = jax.random.randint(key_count, (BLOCKS,), 1, NB // 4 + 1)
    chosen_count = jnp.minimum(draws * density, available)
    chosen_count = jnp.where(local == region_size // 2, NB, chosen_count)
    chosen_count = jnp.maximum(chosen_count, 1).astype(jnp.int32)
    priority = jax.random.randint(key_order, (BLOCKS, width), 0, 2 ** 20) * width + jnp.arange(width, dtype=jnp.int32)[None, :]
    priority = jnp.where(inside, priority, 2 ** 30 + jnp.arange(width, dtype=jnp.int32)[None, :])
    order = jnp.argsort(priority, axis=1, stable=True)[:, :NB]
    picked = jnp.take_along_axis(candidate, order, axis=1)
    slot = jnp.arange(NB, dtype=jnp.int32)[None, :]
    live = slot < chosen_count[:, None]
    dest = jnp.where(live, blocks[:, None] - local[:, None] + picked, blocks[:, None]).astype(jnp.int32)
    factor = 1 + 3 * blocks // BLOCKS
    trips = jax.random.randint(key_flow, (BLOCKS, NB), 0, 8) * factor[:, None]
    trips = jnp.where((blocks[:, None] == BLOCKS - 1) & (slot == 0), 7 * factor[:, None], trips)
    trips = jnp.where(live, trips, 0)
    trips = trips + jnp.where(slot == 0, 1, 0)
    return (dest, chosen_count, trips.astype(jnp.int32))


def draw_neighbors(key, part):
    return neighbor_plan(key)[0]


def draw_counts(key, part):
    return neighbor_plan(key)[1]


def draw_flows(key, part):
    return neighbor_plan(key)[2]


def place_ends(drawn, key, least, top_value):
    extent = drawn.shape
    place = [jax.random.randint(jax.random.fold_in(key, axis), (), 0, extent[axis]) for axis in range(len(extent))]
    drawn = drawn.at[tuple(place)].set(least)
    longest = extent.index(max(extent))
    place[longest] = (place[longest] + 1) % extent[longest]
    return drawn.at[tuple(place)].set(top_value)


def level_of(key, dims, pieces, low, high):
    def one(position, parts):
        steps = jax.random.uniform(jax.random.fold_in(jax.random.fold_in(key, 6), position), (parts,), jnp.float32, low / len(pieces), high / len(pieces))
        return jnp.repeat(jnp.exp(steps), dims[position] // parts).reshape((-1,) + (1,) * (len(dims) - position - 1))

    loudness = one(*pieces[0])
    for cut in pieces[1:]:
        loudness = loudness * one(*cut)
    return loudness


def bell_draw(own_key, shape, deviation, most, shards=(), kind=jnp.bfloat16):
    entries = jax.random.normal(own_key, shape, jnp.float32) * deviation
    if len(shards) > 0:
        entries = level_of(own_key, shape, shards, -0.22, 0.18) * entries
    return jnp.clip(entries, min=-most, max=most).astype(kind)


def setup_inputs(seed: int = 0) -> dict:
    key_list = jax.random.split(jax.random.key(seed), 10)
    return {
        "tiles": bell_draw(key_list[0], (TILES, D), 1.0, 6.0, ((0, 512),)),
        "tile_block": place_ends(jax.random.randint(key_list[1], (TILES,), 0, BLK_DEV), jax.random.fold_in(key_list[1], 1), 0, BLK_DEV - 1).astype(jnp.int32),
        "neighbors": draw_neighbors(jax.random.fold_in(key_list[9], 71), 0),
        "counts": draw_counts(jax.random.fold_in(key_list[9], 71), 0),
        "flows": draw_flows(jax.random.fold_in(key_list[9], 71), 0),
        "w_anchor": bell_draw(key_list[5], (D, HID), D ** -0.5, 0.25, ((0, 32),)),
        "w_dest": bell_draw(key_list[6], (D, HID), D ** -0.5, 0.25, ((0, 32),)),
        "w_hidden": bell_draw(key_list[7], (HID, HID), HID ** -0.5, 0.1875, ((0, 32),)),
        "w_out": bell_draw(key_list[8], (HID,), HID ** -0.5, 0.1875),
    }


def reference(tiles, tile_block, neighbors, counts, flows, w_anchor, w_dest, w_hidden, w_out):
    owner = jnp.arange(TILES, dtype=jnp.int32) // TILE_DEV * BLK_DEV + tile_block
    sums = jax.ops.segment_sum(tiles.astype(jnp.float32), owner, num_segments=BLOCKS)
    scale = lax.rsqrt(lax.optimization_barrier(jnp.mean(sums * sums, axis=-1, keepdims=True)) + 1e-05)
    features = (sums * scale).astype(jnp.bfloat16)
    anchor_proj = jnp.dot(features, w_anchor, preferred_element_type=jnp.float32)
    dest_proj = jnp.dot(features, w_dest, preferred_element_type=jnp.float32)
    valid = jnp.arange(NB, dtype=jnp.int32)[None, :] < counts[:, None]
    flow_f = flows.astype(jnp.float32)
    total = jnp.sum(flow_f)
    weight_out = w_out.astype(jnp.float32)
    steps = BLOCKS // BLK_DEV
    inputs = (anchor_proj.reshape(steps, BLK_DEV, HID), neighbors.reshape(steps, BLK_DEV, NB), valid.reshape(steps, BLK_DEV, NB), flow_f.reshape(steps, BLK_DEV, NB))

    def visit(carry, item):
        grad, gout, numer = carry
        anchor_part, dest_ids, mask, flow_part = item
        first = jnp.maximum(anchor_part[:, None, :] + dest_proj[dest_ids], 0.0).astype(jnp.bfloat16)
        first = first.reshape(BLK_DEV * NB, HID)
        second = jnp.dot(first, w_hidden, preferred_element_type=jnp.float32)
        active = jnp.maximum(second, 0.0)
        scores = lax.optimization_barrier(jnp.sum(active * weight_out, axis=-1)).reshape(BLK_DEV, NB)
        masked = jnp.where(mask, scores, -jnp.inf)
        top = lax.optimization_barrier(jnp.max(masked, axis=-1, keepdims=True))
        expo = jnp.where(mask, jnp.exp(scores - top), 0.0)
        mass = lax.optimization_barrier(jnp.sum(expo, axis=-1, keepdims=True))
        probs = expo / mass
        logp = scores - top - jnp.log(mass)
        anchor_total = lax.optimization_barrier(jnp.sum(flow_part, axis=-1, keepdims=True))
        sgrad = jnp.where(mask, probs * anchor_total - flow_part, 0.0) / total
        sgrad = sgrad.reshape(BLK_DEV * NB)
        pre = (sgrad[:, None] * weight_out * (second > 0)).astype(jnp.bfloat16)
        grad = grad + jnp.dot(first.T, pre, preferred_element_type=jnp.float32)
        gout = gout + lax.optimization_barrier(jnp.sum(sgrad[:, None] * active, axis=0))
        numer = numer - jnp.sum(jnp.where(mask, flow_part * logp, 0.0))
        return ((grad, gout, numer), None)
    start = (jnp.zeros((HID, HID), jnp.float32), jnp.zeros((HID,), jnp.float32), jnp.zeros((), jnp.float32))
    (grad, gout, numer), unused = lax.scan(visit, start, inputs)
    return (grad, gout, numer / total)
```

```python
import functools

import jax
import jax.numpy as jnp
from jax import lax
from jax.experimental import pallas as pl
from jax.experimental.pallas import tpu as pltpu
from jax.sharding import PartitionSpec as P

MESH = pl.DeviceIdType.MESH
BF16 = jnp.bfloat16
F32 = jnp.float32
HALVES = 2


def remote(src, dst, send, recv, where):
    return pltpu.make_async_remote_copy(
        src_ref=src, dst_ref=dst, send_sem=send, recv_sem=recv, device_id=where, device_id_type=MESH
    )


def step_kernel(
    dims,
    tiles, tile_block, neighbors, counts, flows, w_anchor, w_dest, w_hidden, w_out,
    grad_out, gout_out, loss_out,
    pair_w, hid_w, window, proj, onehot, first_t, active, pre, grad, sib_grad, chip_grad, plane_in, plane_sum,
    z_in, own_rows, extra, extra_z, extra_zsum, extra_plane, extra_psum, extra_sib,
    ring_r_send, ring_r_recv, ring_l_send, ring_l_recv, pair_send, pair_recv, halo_send, halo_recv,
    hz_send, hz_recv, hp_send, hp_recv, hs_send, hs_recv, gs_send, gs_recv, gp_send, gp_recv, gz_send, gz_recv,
    ga_send, ga_recv, ez_send, ez_recv, ep_send, ep_recv, es_send, es_recv, local_sem,
):
    planes, depth, blk, slots, hid = dims
    pos = lax.axis_index("shard")
    mine = lax.axis_index("region")
    z, core = pos // 2, pos % 2
    shards = 2 * depth
    cols = hid // (planes // HALVES)
    feat = tiles.shape[1]
    half, block = mine // (planes // HALVES), mine % (planes // HALVES)

    def plane_peer(i):
        return lax.rem(mine + i, planes)

    def z_peer(i):
        return lax.rem(z + i, depth)

    def at_z(where):
        return {"shard": where * 2 + core}

    sibling = {"shard": z * 2 + (1 - core)}
    cross = {"shard": lax.rem(pos + shards + 2 * core - 1, shards)}

    barrier = pltpu.get_barrier_semaphore()
    pl.semaphore_signal(barrier, inc=1, device_id=sibling, device_id_type=MESH)
    pl.semaphore_signal(barrier, inc=1, device_id=cross, device_id_type=MESH)

    def greet_z(i, c):
        pl.semaphore_signal(barrier, inc=1, device_id=at_z(z_peer(i)), device_id_type=MESH)
        return c

    def greet_plane(i, c):
        pl.semaphore_signal(barrier, inc=1, device_id={"region": plane_peer(i)}, device_id_type=MESH)
        return c

    lax.fori_loop(1, depth, greet_z, 0)
    lax.fori_loop(1, planes, greet_plane, 0)

    pair_w[z, core, 0] = w_anchor[...]
    pair_w[z, core, 1] = w_dest[...]

    def hid_tile(ref, row, p):
        r = pl.multiple_of(row + (p // (planes // HALVES)) * 16, 16)
        c = pl.multiple_of((p % (planes // HALVES)) * cols, cols)
        return ref.at[:, pl.ds(r, 16), pl.ds(c, cols)]

    def hid_tile_z(ref, where, row, p):
        r = pl.multiple_of(row + (p // (planes // HALVES)) * 16, 16)
        c = pl.multiple_of((p % (planes // HALVES)) * cols, cols)
        return ref.at[where, pl.ds(r, 16), pl.ds(c, cols)]

    own_r = pl.multiple_of(half * 16, 16)
    own_c = pl.multiple_of(block * cols, cols)
    own_tile = w_hidden.at[pl.ds(own_r, 16), pl.ds(own_c, cols)]
    tile_copy = pltpu.make_async_copy(own_tile, hid_tile_z(hid_w, z, core * 32, mine), local_sem.at[0])
    tile_copy.start()

    member = tile_block[...] == lax.broadcasted_iota(jnp.int32, (blk, tile_block.shape[1]), 0)
    sums = jnp.dot(member.astype(BF16), tiles[...], preferred_element_type=F32)
    scale = lax.rsqrt(jnp.mean(sums * sums, axis=-1, keepdims=True) + 1e-05)
    window[2] = (sums * scale).astype(BF16)
    tile_copy.wait()

    pl.semaphore_wait(barrier, planes - 1 + depth - 1 + 2)

    hops_r, hops_l = depth // 2, (depth - 1) // 2

    def ring(where, to, send, recv):
        return remote(pair_w.at[where, core], pair_w.at[where, core], send, recv, at_z(to))

    def ring_right(t):
        return ring(lax.rem(z - t + 2 * depth, depth), z_peer(1), ring_r_send.at[t], ring_r_recv.at[t])

    def ring_left(t):
        return ring(z_peer(t), lax.rem(z + depth - 1, depth), ring_l_send.at[t], ring_l_recv.at[t])

    def hand_pair(where):
        return remote(
            pair_w.at[where, core], pair_w.at[where, core], pair_send.at[where], pair_recv.at[where], sibling
        )

    def take_pair(where):
        return remote(
            pair_w.at[where, 1 - core], pair_w.at[where, 1 - core], pair_send.at[where], pair_recv.at[where], sibling
        )

    ring_right(0).start()
    if hops_l:
        ring_left(0).start()

    def hid_z(i):
        return remote(
            own_tile, hid_tile_z(hid_w, z, core * 32, mine), hz_send.at[i], hz_recv.at[i], at_z(z_peer(i))
        )

    def hid_z_from(i):
        where = lax.rem(z - i + 2 * depth, depth)
        return remote(own_tile, hid_tile_z(hid_w, where, core * 32, mine), hz_send.at[i], hz_recv.at[i], at_z(where))

    lax.fori_loop(1, depth, lambda i, c: (hid_z(i).start(), c)[1], 0)
    hand_pair(z).start()

    def halo(by):
        return remote(
            window.at[2], window.at[2 - by], halo_send.at[by + 2], halo_recv.at[by + 2],
            {"shard": lax.rem(pos + by + shards, shards)},
        )

    for by in (-2, -1, 1, 2):
        halo(by).start()

    shift = mine * (blk * shards) + (pos - 2) * blk
    place = (neighbors[...] - shift).astype(F32).T
    flow = flows[...].astype(F32).T
    lane16 = lax.broadcasted_iota(jnp.int32, (slots, blk), 1)
    count = jnp.zeros((1, blk), jnp.int32)
    for b in range(blk):
        count = jnp.where(lax.broadcasted_iota(jnp.int32, (1, blk), 1) == b, counts[b], count)
    valid = lax.broadcasted_iota(jnp.int32, (slots, blk), 0) < count
    lane = lax.broadcasted_iota(jnp.int32, (slots, 128), 1).astype(F32)
    for b in range(blk):
        here = (lane == place[:, b:b + 1]) | (lane == 5 * blk + b)
        onehot[b * slots:(b + 1) * slots, :] = jnp.where(here, 1.0, 0.0).astype(BF16)
    anchor_total = jnp.sum(flow, axis=0, keepdims=True)
    proj[...] = jnp.zeros_like(proj)

    def hid_p(i):
        tile = hid_tile(hid_w, core * 32, mine)
        return remote(tile, tile, hp_send.at[i], hp_recv.at[i], {"region": plane_peer(i)})

    def hid_p_from(i):
        p = lax.rem(mine - i + 2 * planes, planes)
        tile = hid_tile(hid_w, core * 32, p)
        return remote(tile, tile, hp_send.at[i], hp_recv.at[i], {"region": p})

    def hand_hid(i):
        tile = hid_tile(hid_w, core * 32, lax.rem(mine - i + 2 * planes, planes))
        return remote(tile, tile, hs_send.at[i], hs_recv.at[i], sibling)

    def take_hid(i):
        tile = hid_tile(hid_w, (1 - core) * 32, lax.rem(mine - i + 2 * planes, planes))
        return remote(tile, tile, hs_send.at[i], hs_recv.at[i], sibling)

    def ring_step(t):
        ring_right(t - 1).wait_send()
        take = ring(lax.rem(z - t + 2 * depth, depth), z_peer(1), ring_r_send.at[t - 1], ring_r_recv.at[t - 1])
        take.wait_recv()
        if t < hops_r:
            ring_right(t).start()
        hand_pair(lax.rem(z - t + 2 * depth, depth)).start()
        if t <= hops_l:
            ring_left(t - 1).wait_send()
            take = ring(z_peer(t), z_peer(1), ring_l_send.at[t - 1], ring_l_recv.at[t - 1])
            take.wait_recv()
            if t < hops_l:
                ring_left(t).start()
            hand_pair(z_peer(t)).start()

    def hid_step(i):
        hid_p_from(i).wait_recv()
        hand_hid(i).start()

    ring_step(1)
    lax.fori_loop(1, depth, lambda i, c: (hid_z_from(i).wait_recv(), c)[1], 0)
    lax.fori_loop(1, planes, lambda i, c: (hid_p(i).start(), c)[1], 0)
    hand_hid(0).start()
    done = 1
    for t in range(2, hops_r + 1):
        ring_step(t)
        for i in range(done, min(done + 2, planes)):
            hid_step(i)
        done = min(done + 2, planes)

    lax.fori_loop(0, depth, lambda i, c: (take_pair(i).wait_recv(), c)[1], 0)
    for by in (-2, -1, 1, 2):
        halo(by).wait_recv()

    rows = 5 * blk
    dest = jnp.dot(
        window[...].reshape(rows, feat), pair_w[:, :, 1].reshape(feat, hid), preferred_element_type=F32
    )
    dest_top = dest.astype(BF16)
    proj[0:rows] = dest_top
    proj[128:128 + rows] = (dest - dest_top.astype(F32)).astype(BF16)
    anchor = jnp.dot(window[2], pair_w[:, :, 0].reshape(feat, hid), preferred_element_type=F32)
    anchor_top = anchor.astype(BF16)
    proj[rows:rows + blk] = anchor_top
    proj[128 + rows:128 + rows + blk] = (anchor - anchor_top.astype(F32)).astype(BF16)

    for i in range(done, planes):
        hid_step(i)
    lax.fori_loop(0, planes, lambda i, c: (take_hid(i).wait_recv(), c)[1], 0)

    group = 4
    size = group * slots
    weight = w_out[...].astype(F32)

    def score(i, scores):
        at = pl.multiple_of(i * size, size)
        pick = onehot[pl.ds(at, size), :]
        both = jnp.concatenate([pick, pick], axis=1)
        first = jnp.maximum(jnp.dot(both, proj[...], preferred_element_type=F32), 0.0).astype(BF16)
        first_t[:, pl.ds(at, size)] = first.T
        act = jnp.maximum(
            jnp.dot(first, hid_w[...].reshape(hid, hid), preferred_element_type=F32), 0.0
        )
        active[pl.ds(at, size), :] = act
        col = jnp.sum(act * weight, axis=1, keepdims=True)
        for a in range(group):
            scores = jnp.where(lane16 == i * group + a, col[a * slots:(a + 1) * slots], scores)
        return scores

    scores = lax.fori_loop(0, blk // group, score, jnp.zeros((slots, blk), F32))

    top = jnp.max(jnp.where(valid, scores, -jnp.inf), axis=0, keepdims=True)
    expo = jnp.where(valid, jnp.exp(scores - top), 0.0)
    mass = jnp.sum(expo, axis=0, keepdims=True)
    probs = expo / mass
    logp = scores - top - jnp.log(mass)
    sgrad = jnp.where(valid, probs * anchor_total - flow, 0.0)
    numer = -jnp.sum(jnp.where(valid, flow * logp, 0.0))
    total = jnp.sum(anchor_total)

    def back(i, gout):
        at = pl.multiple_of(i * size, size)
        col = jnp.concatenate(
            [
                jnp.sum(jnp.where(lane16 == i * group + a, sgrad, 0.0), axis=1, keepdims=True)
                for a in range(group)
            ],
            axis=0,
        )
        act = active[pl.ds(at, size), :]
        pre[pl.ds(at, size), :] = jnp.where(act > 0, col * weight, 0.0).astype(BF16)
        return gout + jnp.sum((col * act).reshape(size // 8, 8, hid), axis=0)

    gout = lax.fori_loop(0, blk // group, back, jnp.zeros((8, hid), F32))
    gout = jnp.sum(gout, axis=0, keepdims=True)

    width = hid // 8
    for r in range(8):
        extra[r:r + 1, :] = gout[:, r * width:(r + 1) * width]
    row = lax.broadcasted_iota(jnp.int32, (8, width), 0)
    extra[8:16, :] = jnp.where(row == 0, numer, jnp.where(row == 1, total, 0.0))

    def extra_to_z(i):
        return remote(extra, extra_z.at[z], ez_send.at[i], ez_recv.at[i], at_z(z_peer(i)))

    def extra_from_z(i):
        where = lax.rem(z - i + 2 * depth, depth)
        return remote(extra, extra_z.at[where], ez_send.at[i], ez_recv.at[i], at_z(where))

    def extra_to_plane(i):
        return remote(extra_zsum, extra_plane.at[mine], ep_send.at[i], ep_recv.at[i], {"region": plane_peer(i)})

    def extra_from_plane(i):
        p = lax.rem(mine - i + 2 * planes, planes)
        return remote(extra_zsum, extra_plane.at[p], ep_send.at[i], ep_recv.at[i], {"region": p})

    lax.fori_loop(1, depth, lambda i, c: (extra_to_z(i).start(), c)[1], 0)
    extra_z[z] = extra[...]

    wide = 2 * cols
    turns = hid // wide

    def turn(n):
        return pl.multiple_of(lax.rem(block // 2 + 1 + n, turns) * wide, wide)

    def to_sibling(n):
        rows_of = pl.ds(pl.multiple_of((1 - core) * 32, 32), 32)
        return remote(
            grad.at[:, rows_of, pl.ds(turn(n), wide)], sib_grad.at[:, :, pl.ds(turn(n), wide)],
            gs_send.at[n], gs_recv.at[n], sibling,
        )

    def grads(n, c):
        part = jnp.dot(first_t[...], pre[:, pl.ds(turn(n), wide)], preferred_element_type=F32)
        grad[:, :, pl.ds(turn(n), wide)] = part.reshape(depth, hid // depth, wide).astype(BF16)
        to_sibling(n).start()
        return c

    lax.fori_loop(0, turns, grads, 0)

    lax.fori_loop(1, depth, lambda i, c: (extra_from_z(i).wait_recv(), c)[1], 0)
    extra_zsum[...] = jnp.sum(extra_z[...], axis=0)
    lax.fori_loop(1, planes, lambda i, c: (extra_to_plane(i).start(), c)[1], 0)
    extra_plane[mine] = extra_zsum[...]

    def to_plane(p):
        return remote(
            hid_tile(chip_grad, 0, p), plane_in.at[mine], gp_send.at[p], gp_recv.at[mine], {"region": p}
        )

    def from_plane(p):
        return remote(hid_tile(chip_grad, 0, mine), plane_in.at[p], gp_send.at[p], gp_recv.at[p], {"region": p})

    def join(n, c):
        to_sibling(n).wait_recv()
        at = turn(n)
        mine_part = grad[:, pl.ds(pl.multiple_of(core * 32, 32), 32), pl.ds(at, wide)].astype(F32)
        chip_grad[:, :, pl.ds(at, wide)] = (mine_part + sib_grad[:, :, pl.ds(at, wide)].astype(F32)).astype(BF16)
        for h in range(HALVES):
            for b in range(2):
                p = h * (planes // HALVES) + at // cols + b

                @pl.when(p != mine)
                def _():
                    to_plane(p).start()
        return c

    lax.fori_loop(0, turns, join, 0)
    own_part = pltpu.make_async_copy(hid_tile(chip_grad, 0, mine), plane_in.at[mine], local_sem.at[1])
    own_part.start()
    own_part.wait()

    lax.fori_loop(1, planes, lambda i, c: (extra_from_plane(i).wait_recv(), c)[1], 0)
    extra_psum[...] = jnp.sum(extra_plane[...], axis=0)
    extra_swap = remote(extra_psum, extra_sib, es_send, es_recv, sibling)
    extra_swap.start()

    lax.fori_loop(1, planes, lambda i, c: (from_plane(plane_peer(i)).wait_recv(), c)[1], 0)

    def to_z(i):
        return remote(plane_sum.at[z_peer(i)], z_in.at[z], gz_send.at[i], gz_recv.at[i], at_z(z_peer(i)))

    def from_z(i):
        where = lax.rem(z - i + 2 * depth, depth)
        return remote(plane_sum.at[where], z_in.at[where], gz_send.at[i], gz_recv.at[i], at_z(where))

    def plane_total(where):
        acc = plane_in[0, where].astype(F32)
        for p in range(1, planes):
            acc = acc + plane_in[p, where].astype(F32)
        return acc.astype(BF16)

    def spread(i, c):
        plane_sum[z_peer(i)] = plane_total(z_peer(i))
        to_z(i).start()
        return c

    lax.fori_loop(1, depth, spread, 0)
    z_in[z] = plane_total(z)

    extra_swap.wait_recv()
    sums_all = extra_psum[...] + extra_sib[...]
    inverse = 1.0 / sums_all[9:10, :]
    gout_out[...] = sums_all[0:8, :] * inverse
    loss_out[...] = sums_all[8:9, 0:1] * inverse[:, 0:1]

    lax.fori_loop(1, depth, lambda i, c: (from_z(i).wait_recv(), c)[1], 0)
    acc = z_in[0].astype(F32)
    for i in range(1, depth):
        acc = acc + z_in[i].astype(F32)
    own_rows[...] = acc * inverse[0:1, 0:1]

    def out_tile(p):
        r = pl.multiple_of((p // (planes // HALVES)) * 16, 16)
        c = pl.multiple_of((p % (planes // HALVES)) * cols, cols)
        return grad_out.at[pl.ds(r, 16), pl.ds(c, cols)]

    def share(i):
        return remote(own_rows, out_tile(mine), ga_send.at[i], ga_recv.at[i], {"region": plane_peer(i)})

    def shared(i):
        p = lax.rem(mine - i + 2 * planes, planes)
        return remote(own_rows, out_tile(p), ga_send.at[i], ga_recv.at[i], {"region": p})

    lax.fori_loop(1, planes, lambda i, c: (share(i).start(), c)[1], 0)
    own_out = pltpu.make_async_copy(own_rows, out_tile(mine), local_sem.at[2])
    own_out.start()

    lax.fori_loop(0, depth, lambda i, c: (hand_pair(i).wait_send(), c)[1], 0)
    for by in (-2, -1, 1, 2):
        halo(by).wait_send()
    lax.fori_loop(1, depth, lambda i, c: (hid_z(i).wait_send(), c)[1], 0)
    lax.fori_loop(1, planes, lambda i, c: (hid_p(i).wait_send(), c)[1], 0)
    lax.fori_loop(0, planes, lambda i, c: (hand_hid(i).wait_send(), c)[1], 0)
    lax.fori_loop(1, depth, lambda i, c: (extra_to_z(i).wait_send(), c)[1], 0)
    lax.fori_loop(1, planes, lambda i, c: (extra_to_plane(i).wait_send(), c)[1], 0)
    extra_swap.wait_send()
    lax.fori_loop(0, turns, lambda n, c: (to_sibling(n).wait_send(), c)[1], 0)
    lax.fori_loop(1, planes, lambda i, c: (to_plane(plane_peer(i)).wait_send(), c)[1], 0)
    lax.fori_loop(1, depth, lambda i, c: (to_z(i).wait_send(), c)[1], 0)
    own_out.wait()
    lax.fori_loop(1, planes, lambda i, c: (shared(i).wait_recv(), c)[1], 0)
    lax.fori_loop(1, planes, lambda i, c: (share(i).wait_send(), c)[1], 0)


def shards(tiles, tile_block, neighbors, counts, flows, w_anchor, w_dest, w_hidden, w_out):
    planes, shard_count = lax.axis_size("region"), lax.axis_size("shard")
    depth = shard_count // 2
    blk, slots = neighbors.shape
    feat, hid = tiles.shape[1], w_hidden.shape[1]
    pairs = blk * slots
    cols = hid // (planes // HALVES)
    turns = hid // (2 * cols)
    vmem = pl.BlockSpec(memory_space=pltpu.VMEM)
    dma = lambda n: pltpu.SemaphoreType.DMA((n,))
    scratch = [
        pltpu.VMEM((depth, 2, 2, w_anchor.shape[0], hid), BF16),
        pltpu.VMEM((depth, 64, hid), BF16),
        pltpu.VMEM((5, blk, feat), BF16),
        pltpu.VMEM((256, hid), BF16),
        pltpu.VMEM((pairs, 128), BF16),
        pltpu.VMEM((hid, pairs), BF16),
        pltpu.VMEM((pairs, hid), F32),
        pltpu.VMEM((pairs, hid), BF16),
        pltpu.VMEM((depth, 64, hid), BF16),
        pltpu.VMEM((depth, 32, hid), BF16),
        pltpu.VMEM((depth, 32, hid), BF16),
        pltpu.VMEM((planes, depth, 16, cols), BF16),
        pltpu.VMEM((depth, 16, cols), BF16),
        pltpu.VMEM((depth, 16, cols), BF16),
        pltpu.VMEM((16, cols), F32),
        pltpu.VMEM((16, hid // 8), F32),
        pltpu.VMEM((depth, 16, hid // 8), F32),
        pltpu.VMEM((16, hid // 8), F32),
        pltpu.VMEM((planes, 16, hid // 8), F32),
        pltpu.VMEM((16, hid // 8), F32),
        pltpu.VMEM((16, hid // 8), F32),
        dma(depth), dma(depth), dma(depth), dma(depth), dma(depth), dma(depth), dma(5), dma(5),
        dma(depth), dma(depth), dma(planes), dma(planes), dma(planes), dma(planes),
        dma(turns), dma(turns), dma(planes), dma(planes), dma(depth), dma(depth),
        dma(planes), dma(planes), dma(depth), dma(depth), dma(planes), dma(planes),
        pltpu.SemaphoreType.DMA, pltpu.SemaphoreType.DMA, dma(3),
    ]
    grad, gout, loss = pl.pallas_call(
        functools.partial(step_kernel, (planes, depth, blk, slots, hid)),
        out_shape=(
            jax.ShapeDtypeStruct((w_hidden.shape[0], hid), F32),
            jax.ShapeDtypeStruct((8, hid // 8), F32),
            jax.ShapeDtypeStruct((1, 1), F32),
        ),
        in_specs=[vmem, vmem, vmem, pl.BlockSpec(memory_space=pltpu.SMEM), vmem, vmem, vmem, vmem, vmem],
        out_specs=(vmem, vmem, vmem),
        scratch_shapes=scratch,
        compiler_params=pltpu.CompilerParams(
            collective_id=0, has_side_effects=True, vmem_limit_bytes=50 * 2 ** 20
        ),
        cost_estimate=pl.CostEstimate(
            flops=4 * pairs * hid * hid, bytes_accessed=2 * tiles.size, transcendentals=pairs
        ),
    )(
        tiles, tile_block.reshape(1, -1), neighbors, counts, flows, w_anchor, w_dest, w_hidden, w_out.reshape(1, -1)
    )
    return grad, gout.reshape(hid), loss.reshape(())


def solution(mesh):
    return jax.shard_map(
        shards,
        mesh=mesh,
        in_specs=(
            P(("region", "shard"), None),
            P(("region", "shard")),
            P(("region", "shard"), None),
            P(("region", "shard")),
            P(("region", "shard"), None),
            P("shard", None),
            P("shard", None),
            P("shard", None),
            P(),
        ),
        out_specs=(P("shard", None), P(), P()),
        check_vma=False,
    )
```

```python
import functools

import jax
import jax.numpy as jnp
from jax import lax
from jax.experimental import pallas as pl
from jax.experimental.pallas import tpu as pltpu
from jax.sharding import PartitionSpec as P

MESH = pl.DeviceIdType.MESH
BF16 = jnp.bfloat16
F32 = jnp.float32


def remote(src, dst, send, recv, where):
    return pltpu.make_async_remote_copy(
        src_ref=src, dst_ref=dst, send_sem=send, recv_sem=recv, device_id=where, device_id_type=MESH
    )


def step_kernel(
    dims,
    tiles_hbm, tile_block_hbm, neighbors_hbm, counts_hbm, flows_hbm, anchor_hbm, dest_hbm, hidden_hbm, out_hbm,
    grad_out, gout_out, loss_out,
    tiles, tile_block, neighbors, counts, flows, w_out,
    own_w, weights, window, proj, onehot, first_t, active, pre, grad, sib_grad, chip_grad, u_in, u_sum, v_in,
    plane_sum, z_in, own_rows, extra, extra_z, extra_zsum, extra_plane, extra_psum, extra_sib,
    halo_send, halo_recv, az_send, az_recv, p1_send, p1_recv, p2_send, p2_recv, sb_send, sb_recv,
    gs_send, gs_recv, gu_send, gu_recv, gv_send, gv_recv, gz_send, gz_recv,
    ga_send, ga_recv, ez_send, ez_recv, ep_send, ep_recv, es_send, es_recv, load_sem, local_sem,
):
    side, depth, blk, slots, hid = dims
    planes = side * side
    pos = lax.axis_index("shard")
    mine = lax.axis_index("region")
    z, core = pos // 2, pos % 2
    shards = 2 * depth
    feat = tiles.shape[1]
    y, x = mine // side, mine % side
    u = y + core * (x - y)
    v = x + core * (y - x)
    per_half = side // 2
    group_cols = hid // per_half
    tile_cols = group_cols // side

    def wrap(i, n):
        return lax.rem(i + 2 * n, n)

    def at_z(where):
        return {"shard": where * 2 + core}

    def at_uv(uu, vv):
        return {"region": (uu * side + vv) * (1 - core) + (vv * side + uu) * core}

    sibling = {"shard": z * 2 + (1 - core)}
    cross = {"shard": wrap(pos + 2 * core - 1, shards)}

    def each(first, last, act):
        def body(i, c):
            act(i)
            return c

        lax.fori_loop(first, last, body, 0)

    loads = [
        pltpu.make_async_copy(anchor_hbm, own_w.at[0, 0], load_sem.at[0]),
        pltpu.make_async_copy(dest_hbm, own_w.at[1, 0], load_sem.at[1]),
        pltpu.make_async_copy(hidden_hbm.at[0:16], own_w.at[0, 1], load_sem.at[2]),
        pltpu.make_async_copy(hidden_hbm.at[16:32], own_w.at[1, 1], load_sem.at[3]),
        pltpu.make_async_copy(tiles_hbm, tiles, load_sem.at[4]),
        pltpu.make_async_copy(tile_block_hbm, tile_block, load_sem.at[5]),
        pltpu.make_async_copy(neighbors_hbm, neighbors, load_sem.at[6]),
        pltpu.make_async_copy(counts_hbm, counts, load_sem.at[7]),
        pltpu.make_async_copy(flows_hbm, flows, load_sem.at[8]),
        pltpu.make_async_copy(out_hbm, w_out, load_sem.at[9]),
    ]
    for copy in loads:
        copy.start()
    barrier = pltpu.get_barrier_semaphore()

    def greet(where):
        pl.semaphore_signal(barrier, inc=1, device_id=where, device_id_type=MESH)

    greet(sibling)
    greet(cross)
    each(1, depth, lambda i: greet(at_z(wrap(z + i, depth))))
    each(1, planes, lambda i: greet({"region": wrap(mine + i, planes)}))

    def span(ref, uu, first, count):
        at = (uu % per_half) * group_cols + first * tile_cols
        return pl.ds(pl.multiple_of(at, tile_cols), count * tile_cols)

    def weight_tile(where, zs):
        return weights.at[pl.ds(where, zs), core, u // per_half, :, :, span(weights, u, v, 1)]

    def weight_group(where, zs, uu, cc):
        return weights.at[pl.ds(where, zs), cc, uu // per_half, :, :, span(weights, uu, 0, side)]

    own_tile = own_w.at[u // per_half, :, :, span(own_w, u, v, 1)]

    def weight_slot(where):
        return weights.at[where, core, u // per_half, :, :, span(weights, u, v, 1)]

    def to_z_weights(i):
        to = wrap(z + i, depth)
        return remote(own_tile, weight_slot(z), az_send.at[to], az_recv.at[z], at_z(to))

    def from_z_weights(where):
        return remote(own_tile, weight_slot(where), az_send.at[where], az_recv.at[where], at_z(where))

    for copy in loads[0:4]:
        copy.wait()
    keep_tile = pltpu.make_async_copy(own_tile, weight_slot(z), local_sem.at[0])
    keep_tile.start()
    pl.semaphore_wait(barrier, planes - 1 + depth - 1 + 2)

    def both_ways(i):
        to_z_weights(i).start()
        to_z_weights(depth - i).start()

    each(1, depth // 2, both_ways)
    to_z_weights(depth // 2).start()

    for copy in loads[4:]:
        copy.wait()
    member = tile_block[...] == lax.broadcasted_iota(jnp.int32, (blk, tile_block.shape[1]), 0)
    sums = jnp.dot(member.astype(BF16), tiles[...], preferred_element_type=F32)
    scale = lax.rsqrt(jnp.mean(sums * sums, axis=-1, keepdims=True) + 1e-05)
    window[2] = (sums * scale).astype(BF16)

    def halo(by):
        return remote(
            window.at[2], window.at[2 - by], halo_send.at[by + 2], halo_recv.at[by + 2],
            {"shard": wrap(pos + by, shards)},
        )

    for by in (-2, -1, 1, 2):
        halo(by).start()

    shift = mine * (blk * shards) + (pos - 2) * blk
    place = (neighbors[...] - shift).astype(F32).T
    flow = flows[...].astype(F32).T
    lane16 = lax.broadcasted_iota(jnp.int32, (slots, blk), 1)
    count = jnp.zeros((1, blk), jnp.int32)
    for b in range(blk):
        count = jnp.where(lax.broadcasted_iota(jnp.int32, (1, blk), 1) == b, counts[b], count)
    valid = lax.broadcasted_iota(jnp.int32, (slots, blk), 0) < count
    lane = lax.broadcasted_iota(jnp.int32, (slots, 128), 1).astype(F32)
    for b in range(blk):
        here = (lane == place[:, b:b + 1]) | (lane == 5 * blk + b)
        onehot[b * slots:(b + 1) * slots, :] = jnp.where(here, 1.0, 0.0).astype(BF16)
    anchor_total = jnp.sum(flow, axis=0, keepdims=True)
    proj[...] = jnp.zeros_like(proj)
    keep_tile.wait()

    zs = depth // 4
    first_block = z // zs

    def block_at(n):
        return wrap(first_block + (0, 1, -1, 2)[n], 4)

    def along_v(b, i):
        tile = weight_tile(b * zs, zs)
        return remote(
            tile, tile, p1_send.at[b * side + i], p1_recv.at[b * side + i], at_uv(u, wrap(v + i, side))
        )

    def from_v(b, i):
        vv = wrap(v - i, side)
        tile = weights.at[pl.ds(b * zs, zs), core, u // per_half, :, :, span(weights, u, vv, 1)]
        return remote(tile, tile, p1_send.at[b * side + i], p1_recv.at[b * side + i], at_uv(u, vv))

    def along_u(b, i):
        part = weight_group(b * zs, zs, u, core)
        return remote(
            part, part, p2_send.at[b * side + i], p2_recv.at[b * side + i], at_uv(wrap(u + i, side), v)
        )

    def from_u(b, i):
        uu = wrap(u - i, side)
        part = weight_group(b * zs, zs, uu, core)
        return remote(part, part, p2_send.at[b * side + i], p2_recv.at[b * side + i], at_uv(uu, v))

    def hand(b, i):
        part = weight_group(b * zs, zs, wrap(u - i, side), core)
        return remote(part, part, sb_send.at[b * side + i], sb_recv.at[b * side + i], sibling)

    def take(b, i):
        part = weight_group(b * zs, zs, wrap(v - i, side), 1 - core)
        return remote(part, part, sb_send.at[b * side + i], sb_recv.at[b * side + i], sibling)

    for n in range(6):
        if 1 <= n <= 4:
            b = block_at(n - 1)
            for i in range(1, side):
                from_v(b, i).wait_recv()
            for i in range(1, side):
                along_u(b, i).start()
            hand(b, 0).start()
        if n < 4:
            b = block_at(n)
            for k in range(zs):

                @pl.when(b * zs + k != z)
                def _():
                    from_z_weights(b * zs + k).wait_recv()

            for i in range(1, side):
                along_v(b, i).start()
        if n >= 2:
            b = block_at(n - 2)
            for i in range(1, side):
                from_u(b, i).wait_recv()
                hand(b, i).start()

    for by in (-2, -1, 1, 2):
        halo(by).wait_recv()
    each(0, 4 * side, lambda i: take(i // side, i % side).wait_recv())

    rows = 5 * blk
    dest = jnp.dot(
        window[...].reshape(rows, feat), weights[:, :, 1, 0].reshape(feat, hid), preferred_element_type=F32
    )
    dest_top = dest.astype(BF16)
    proj[0:rows] = dest_top
    proj[128:128 + rows] = (dest - dest_top.astype(F32)).astype(BF16)
    anchor = jnp.dot(window[2], weights[:, :, 0, 0].reshape(feat, hid), preferred_element_type=F32)
    anchor_top = anchor.astype(BF16)
    proj[rows:rows + blk] = anchor_top
    proj[128 + rows:128 + rows + blk] = (anchor - anchor_top.astype(F32)).astype(BF16)

    group = 4
    size = group * slots
    weight = w_out[...].astype(F32).reshape(1, hid)

    def score(i, scores):
        at = pl.multiple_of(i * size, size)
        pick = onehot[pl.ds(at, size), :]
        both = jnp.concatenate([pick, pick], axis=1)
        first = jnp.maximum(jnp.dot(both, proj[...], preferred_element_type=F32), 0.0).astype(BF16)
        first_t[:, pl.ds(at, size)] = first.T
        act = jnp.maximum(
            jnp.dot(first, weights[:, :, :, 1].reshape(hid, hid), preferred_element_type=F32), 0.0
        )
        active[pl.ds(at, size), :] = act
        col = jnp.sum(act * weight, axis=1, keepdims=True)
        for a in range(group):
            scores = jnp.where(lane16 == i * group + a, col[a * slots:(a + 1) * slots], scores)
        return scores

    scores = lax.fori_loop(0, blk // group, score, jnp.zeros((slots, blk), F32))

    top = jnp.max(jnp.where(valid, scores, -jnp.inf), axis=0, keepdims=True)
    expo = jnp.where(valid, jnp.exp(scores - top), 0.0)
    mass = jnp.sum(expo, axis=0, keepdims=True)
    probs = expo / mass
    logp = scores - top - jnp.log(mass)
    sgrad = jnp.where(valid, probs * anchor_total - flow, 0.0)
    numer = -jnp.sum(jnp.where(valid, flow * logp, 0.0))
    total = jnp.sum(anchor_total)

    def back(i, gout):
        at = pl.multiple_of(i * size, size)
        col = jnp.concatenate(
            [
                jnp.sum(jnp.where(lane16 == i * group + a, sgrad, 0.0), axis=1, keepdims=True)
                for a in range(group)
            ],
            axis=0,
        )
        act = active[pl.ds(at, size), :]
        pre[pl.ds(at, size), :] = jnp.where(act > 0, col * weight, 0.0).astype(BF16)
        return gout + jnp.sum((col * act).reshape(size // 8, 8, hid), axis=0)

    gout = lax.fori_loop(0, blk // group, back, jnp.zeros((8, hid), F32))
    gout = jnp.sum(gout, axis=0, keepdims=True)

    width = hid // 8
    for r in range(8):
        extra[r:r + 1, :] = gout[:, r * width:(r + 1) * width]
    row = lax.broadcasted_iota(jnp.int32, (8, width), 0)
    extra[8:16, :] = jnp.where(row == 0, numer, jnp.where(row == 1, total, 0.0))

    def extra_to_z(i):
        return remote(extra, extra_z.at[z], ez_send.at[i], ez_recv.at[i], at_z(wrap(z + i, depth)))

    def extra_from_z(i):
        where = wrap(z - i, depth)
        return remote(extra, extra_z.at[where], ez_send.at[i], ez_recv.at[i], at_z(where))

    def extra_to_plane(i):
        to = {"region": wrap(mine + i, planes)}
        return remote(extra_zsum, extra_plane.at[mine], ep_send.at[i], ep_recv.at[i], to)

    def extra_from_plane(i):
        p = wrap(mine - i, planes)
        return remote(extra_zsum, extra_plane.at[p], ep_send.at[i], ep_recv.at[i], {"region": p})

    each(1, depth, lambda i: extra_to_z(i).start())
    extra_z[z] = extra[...]

    wide = group_cols // 2
    turns = hid // wide

    def turn(n):
        return pl.ds(pl.multiple_of(n * wide, wide), wide)

    def to_sibling(n):
        return remote(
            grad.at[:, 1 - core, :, :, turn(n)], sib_grad.at[:, :, :, turn(n)], gs_send.at[n], gs_recv.at[n], sibling
        )

    def grads(n):
        part = jnp.dot(first_t[...], pre[:, turn(n)], preferred_element_type=F32)
        grad[:, :, :, :, turn(n)] = part.reshape(depth, 2, 2, 16, wide).astype(BF16)
        to_sibling(n).start()

    each(0, turns, grads)

    def to_u(n, h):
        uu = h * per_half + n // 2
        inside = pl.ds(pl.multiple_of((n % 2) * wide, wide), wide)
        return remote(
            chip_grad.at[:, h, :, turn(n)], u_in.at[u, :, :, inside],
            gu_send.at[n * 2 + h], gu_recv.at[u * 2 + n % 2], at_uv(uu, v),
        )

    def from_u_grad(uu, k):
        inside = pl.ds(pl.multiple_of(k * wide, wide), wide)
        return remote(
            chip_grad.at[:, 0, :, 0:wide], u_in.at[uu, :, :, inside],
            gu_send.at[0], gu_recv.at[uu * 2 + k], at_uv(uu, v),
        )

    def join(n):
        to_sibling(n).wait_recv()
        mine_part = grad[:, core, :, :, turn(n)].astype(F32)
        chip_grad[:, :, :, turn(n)] = (mine_part + sib_grad[:, :, :, turn(n)].astype(F32)).astype(BF16)
        for h in range(2):

            @pl.when(h * per_half + n // 2 != u)
            def _():
                to_u(n, h).start()

    each(0, turns, join)

    each(1, depth, lambda i: extra_from_z(i).wait_recv())
    extra_zsum[...] = jnp.sum(extra_z[...], axis=0)
    each(1, planes, lambda i: extra_to_plane(i).start())
    extra_plane[mine] = extra_zsum[...]

    def to_v(i):
        vv = wrap(v + i, side)
        part = u_sum.at[:, :, pl.ds(pl.multiple_of(vv * tile_cols, tile_cols), tile_cols)]
        return remote(part, v_in.at[v], gv_send.at[i], gv_recv.at[i], at_uv(u, vv))

    def from_v_grad(i):
        vv = wrap(v - i, side)
        part = u_sum.at[:, :, 0:tile_cols]
        return remote(part, v_in.at[vv], gv_send.at[i], gv_recv.at[i], at_uv(u, vv))

    for i in range(1, side):
        for k in range(2):
            from_u_grad(wrap(u + i, side), k).wait_recv()

    own_group = span(chip_grad, u, 0, side)

    def sum_u(i):
        acc = chip_grad[pl.ds(i * zs, zs), u // per_half, :, own_group].astype(F32)
        for k in range(1, side):
            acc = acc + u_in[wrap(u + k, side), pl.ds(i * zs, zs)].astype(F32)
        u_sum[pl.ds(i * zs, zs)] = acc.astype(BF16)

    each(0, 4, sum_u)
    for i in range(1, side):
        to_v(i).start()

    each(1, planes, lambda i: extra_from_plane(i).wait_recv())
    extra_psum[...] = jnp.sum(extra_plane[...], axis=0)
    extra_swap = remote(extra_psum, extra_sib, es_send, es_recv, sibling)
    extra_swap.start()

    def to_z(i):
        where = wrap(z + i, depth)
        return remote(plane_sum.at[where], z_in.at[z], gz_send.at[i], gz_recv.at[i], at_z(where))

    def from_z(i):
        where = wrap(z - i, depth)
        return remote(plane_sum.at[where], z_in.at[where], gz_send.at[i], gz_recv.at[i], at_z(where))

    for i in range(1, side):
        from_v_grad(i).wait_recv()
    own_cols = pl.ds(pl.multiple_of(v * tile_cols, tile_cols), tile_cols)
    acc = u_sum[:, :, own_cols].astype(F32)
    for k in range(1, side):
        acc = acc + v_in[wrap(v + k, side)].astype(F32)
    plane_sum[...] = acc.astype(BF16)
    each(1, depth, lambda i: to_z(i).start())
    z_in[z] = plane_sum[z]

    extra_swap.wait_recv()
    sums_all = extra_psum[...] + extra_sib[...]
    inverse = 1.0 / sums_all[9:10, :]
    gout_out[...] = sums_all[0:8, :] * inverse
    loss_out[...] = sums_all[8:9, 0:1] * inverse[:, 0:1]

    each(1, depth, lambda i: from_z(i).wait_recv())
    own_rows[...] = jnp.sum(z_in[...].astype(F32), axis=0) * inverse[0:1, 0:1]

    def out_tile(p):
        py, px = p // side, p % side
        uu = py + core * (px - py)
        vv = px + core * (py - px)
        return grad_out.at[pl.ds(pl.multiple_of((uu // per_half) * 16, 16), 16), span(grad_out, uu, vv, 1)]

    def share(i):
        to = {"region": wrap(mine + i, planes)}
        return remote(own_rows, out_tile(mine), ga_send.at[i], ga_recv.at[i], to)

    def shared(i):
        p = wrap(mine - i, planes)
        return remote(own_rows, out_tile(p), ga_send.at[i], ga_recv.at[i], {"region": p})

    each(1, planes, lambda i: share(i).start())
    own_out = pltpu.make_async_copy(own_rows, out_tile(mine), local_sem.at[1])
    own_out.start()

    for by in (-2, -1, 1, 2):
        halo(by).wait_send()
    each(1, depth, lambda i: to_z_weights(i).wait_send())

    def weights_left(b):
        for i in range(1, side):
            along_v(b, i).wait_send()
            along_u(b, i).wait_send()
        for i in range(side):
            hand(b, i).wait_send()

    each(0, 4, weights_left)
    each(1, depth, lambda i: extra_to_z(i).wait_send())
    each(1, planes, lambda i: extra_to_plane(i).wait_send())
    extra_swap.wait_send()
    each(0, turns, lambda n: to_sibling(n).wait_send())

    def u_left(n):
        for h in range(2):

            @pl.when(h * per_half + n // 2 != u)
            def _():
                to_u(n, h).wait_send()

    each(0, turns, u_left)
    for i in range(1, side):
        to_v(i).wait_send()
    each(1, depth, lambda i: to_z(i).wait_send())
    own_out.wait()
    each(1, planes, lambda i: shared(i).wait_recv())
    each(1, planes, lambda i: share(i).wait_send())


def shards(tiles, tile_block, neighbors, counts, flows, w_anchor, w_dest, w_hidden, w_out):
    planes, shard_count = lax.axis_size("region"), lax.axis_size("shard")
    side = 4 if planes == 16 else 2
    depth = shard_count // 2
    blk, slots = neighbors.shape
    feat, hid = tiles.shape[1], w_hidden.shape[1]
    pairs = blk * slots
    group_cols = hid // (side // 2)
    tile_cols = group_cols // side
    turns = hid // (group_cols // 2)
    width = hid // 8
    vmem = pl.BlockSpec(memory_space=pltpu.VMEM)
    hbm = pl.BlockSpec(memory_space=pltpu.HBM)
    dma = lambda n: pltpu.SemaphoreType.DMA((n,))
    scratch = [
        pltpu.VMEM(tiles.shape, BF16),
        pltpu.VMEM((1, tile_block.shape[0]), jnp.int32),
        pltpu.VMEM((blk, slots), jnp.int32),
        pltpu.SMEM((blk,), jnp.int32),
        pltpu.VMEM((blk, slots), jnp.int32),
        pltpu.VMEM((hid,), BF16),
        pltpu.VMEM((2, 2, 16, hid), BF16),
        pltpu.VMEM((depth, 2, 2, 2, 16, hid), BF16),
        pltpu.VMEM((5, blk, feat), BF16),
        pltpu.VMEM((256, hid), BF16),
        pltpu.VMEM((pairs, 128), BF16),
        pltpu.VMEM((hid, pairs), BF16),
        pltpu.VMEM((pairs, hid), F32),
        pltpu.VMEM((pairs, hid), BF16),
        pltpu.VMEM((depth, 2, 2, 16, hid), BF16),
        pltpu.VMEM((depth, 2, 16, hid), BF16),
        pltpu.VMEM((depth, 2, 16, hid), BF16),
        pltpu.VMEM((side, depth, 16, group_cols), BF16),
        pltpu.VMEM((depth, 16, group_cols), BF16),
        pltpu.VMEM((side, depth, 16, tile_cols), BF16),
        pltpu.VMEM((depth, 16, tile_cols), BF16),
        pltpu.VMEM((depth, 16, tile_cols), BF16),
        pltpu.VMEM((16, tile_cols), F32),
        pltpu.VMEM((16, width), F32),
        pltpu.VMEM((depth, 16, width), F32),
        pltpu.VMEM((16, width), F32),
        pltpu.VMEM((planes, 16, width), F32),
        pltpu.VMEM((16, width), F32),
        pltpu.VMEM((16, width), F32),
        dma(5), dma(5), dma(depth), dma(depth), dma(4 * side), dma(4 * side), dma(4 * side), dma(4 * side),
        dma(4 * side), dma(4 * side), dma(turns), dma(turns), dma(2 * turns), dma(2 * side), dma(side), dma(side),
        dma(depth), dma(depth), dma(planes), dma(planes), dma(depth), dma(depth), dma(planes), dma(planes),
        pltpu.SemaphoreType.DMA, pltpu.SemaphoreType.DMA, dma(10), dma(2),
    ]
    grad, gout, loss = pl.pallas_call(
        functools.partial(step_kernel, (side, depth, blk, slots, hid)),
        out_shape=(
            jax.ShapeDtypeStruct((w_hidden.shape[0], hid), F32),
            jax.ShapeDtypeStruct((8, width), F32),
            jax.ShapeDtypeStruct((1, 1), F32),
        ),
        in_specs=[hbm] * 9,
        out_specs=(vmem, vmem, vmem),
        scratch_shapes=scratch,
        compiler_params=pltpu.CompilerParams(
            collective_id=0, has_side_effects=True, vmem_limit_bytes=62 * 2 ** 20
        ),
        cost_estimate=pl.CostEstimate(
            flops=4 * pairs * hid * hid, bytes_accessed=2 * tiles.size, transcendentals=pairs
        ),
    )(tiles, tile_block.reshape(1, -1), neighbors, counts, flows, w_anchor, w_dest, w_hidden, w_out)
    return grad, gout.reshape(hid), loss.reshape(())


def solution(mesh):
    return jax.shard_map(
        shards,
        mesh=mesh,
        in_specs=(
            P(("region", "shard"), None),
            P(("region", "shard")),
            P(("region", "shard"), None),
            P(("region", "shard")),
            P(("region", "shard"), None),
            P("shard", None),
            P("shard", None),
            P("shard", None),
            P(),
        ),
        out_specs=(P("shard", None), P(), P()),
        check_vma=False,
    )
```

```python
import functools

import jax
import jax.numpy as jnp
from jax import lax
from jax.experimental import pallas as pl
from jax.experimental.pallas import tpu as pltpu
from jax.sharding import PartitionSpec as P

MESH = pl.DeviceIdType.MESH
BF16 = jnp.bfloat16
F32 = jnp.float32


def remote(src, dst, send, recv, where):
    return pltpu.make_async_remote_copy(
        src_ref=src, dst_ref=dst, send_sem=send, recv_sem=recv, device_id=where, device_id_type=MESH
    )


def step_kernel(
    dims,
    tiles_hbm, tile_block_hbm, neighbors_hbm, counts_hbm, flows_hbm, anchor_hbm, dest_hbm, hidden_hbm, out_hbm,
    grad_out, gout_out, loss_out,
    tiles, tile_block, neighbors, counts, flows, w_out,
    weights, features, tile_w, plane_feats, part_proj, own_proj, window, proj, onehot, first_t, active, pre, grad, sib_grad, chip_grad, u_in, u_sum, v_in,
    plane_sum, z_in, own_rows, extra, extra_z, extra_zsum, extra_plane, extra_psum, extra_sib,
    halo_send, halo_recv, fz_send, fz_recv, fs_send, fs_recv, fp_send, fp_recv, pp_send, pp_recv,
    az_send, az_recv, p1_send, p1_recv, p2_send, p2_recv, sb_send, sb_recv,
    gs_send, gs_recv, gu_send, gu_recv, gv_send, gv_recv, gz_send, gz_recv,
    ga_send, ga_recv, ez_send, ez_recv, ep_send, ep_recv, es_send, es_recv, load_sem, local_sem,
):
    side, depth, blk, slots, hid = dims
    planes = side * side
    pos = lax.axis_index("shard")
    mine = lax.axis_index("region")
    z, core = pos // 2, pos % 2
    shards = 2 * depth
    feat = tiles.shape[1]
    y, x = mine // side, mine % side
    u = y + core * (x - y)
    v = x + core * (y - x)
    per_half = side // 2
    group_cols = hid // per_half
    tile_cols = group_cols // side

    def wrap(i, n):
        return lax.rem(i + 2 * n, n)

    def at_z(where):
        return {"shard": where * 2 + core}

    def at_uv(uu, vv):
        return {"region": (uu * side + vv) * (1 - core) + (vv * side + uu) * core}

    sibling = {"shard": z * 2 + (1 - core)}
    cross = {"shard": wrap(pos + 2 * core - 1, shards)}

    def each(first, last, act):
        def body(i, c):
            act(i)
            return c

        lax.fori_loop(first, last, body, 0)

    loads = [
        pltpu.make_async_copy(tiles_hbm, tiles, load_sem.at[0]),
        pltpu.make_async_copy(tile_block_hbm, tile_block, load_sem.at[1]),
        pltpu.make_async_copy(neighbors_hbm, neighbors, load_sem.at[2]),
        pltpu.make_async_copy(counts_hbm, counts, load_sem.at[3]),
        pltpu.make_async_copy(flows_hbm, flows, load_sem.at[4]),
        pltpu.make_async_copy(out_hbm, w_out, load_sem.at[5]),
    ]
    barrier = pltpu.get_barrier_semaphore()

    def greet(where):
        pl.semaphore_signal(barrier, inc=1, device_id=where, device_id_type=MESH)

    greet(sibling)
    greet(cross)
    each(1, depth, lambda i: greet(at_z(wrap(z + i, depth))))
    each(1, planes, lambda i: greet({"region": wrap(mine + i, planes)}))

    for copy in loads:
        copy.start()

    def span(uu, first, count):
        at = (uu % per_half) * group_cols + first * tile_cols
        return pl.ds(pl.multiple_of(at, tile_cols), count * tile_cols)

    def weight_part(where, count, cc, uu, first, tiles_of):
        return weights.at[pl.ds(where, count), cc, uu // per_half, :, span(uu, first, tiles_of)]

    half_planes = planes // 2
    matrix = mine // half_planes
    first_cols = pl.ds(pl.multiple_of((mine % half_planes) * tile_cols, tile_cols), tile_cols)
    hid_tile = hidden_hbm.at[pl.ds(pl.multiple_of((u // per_half) * 16, 16), 16), span(u, v, 1)]

    def weight_slot(where):
        return weights.at[where, core, u // per_half, :, span(u, v, 1)]

    def first_to_z(i, source):
        to = wrap(z + i, depth)
        return remote(source.at[:, first_cols], tile_w.at[z, core], fz_send.at[to], fz_recv.at[z], at_z(to))

    def first_from_z(where):
        return remote(
            anchor_hbm.at[:, first_cols], tile_w.at[where, core], fz_send.at[where], fz_recv.at[where], at_z(where)
        )

    def hid_to_z(i):
        to = wrap(z + i, depth)
        return remote(hid_tile, weight_slot(z), az_send.at[to], az_recv.at[z], at_z(to))

    def hid_from_z(where):
        return remote(hid_tile, weight_slot(where), az_send.at[where], az_recv.at[where], at_z(where))

    def keep_first(source):
        return pltpu.make_async_copy(source.at[:, first_cols], tile_w.at[z, core], local_sem.at[2])

    def near_first(start):
        def both_ways(i):
            start(i)
            start(depth - i)

        each(1, depth // 2, both_ways)
        start(depth // 2)

    pl.semaphore_wait(barrier, planes - 1 + depth - 1 + 2)
    for k, source in enumerate((anchor_hbm, dest_hbm)):

        @pl.when(matrix == k)
        def _():
            near_first(lambda i: first_to_z(i, source).start())
            keep_first(source).start()

    near_first(lambda i: hid_to_z(i).start())
    keep_tile = pltpu.make_async_copy(hid_tile, weight_slot(z), local_sem.at[0])
    keep_tile.start()

    loads[0].wait()
    loads[1].wait()
    member = tile_block[...] == lax.broadcasted_iota(jnp.int32, (blk, tile_block.shape[1]), 0)
    sums = jnp.dot(member.astype(BF16), tiles[...], preferred_element_type=F32)
    scale = lax.rsqrt(jnp.mean(sums * sums, axis=-1, keepdims=True) + 1e-05)
    features[...] = (sums * scale).astype(BF16)
    plane_feats[mine] = features[...]

    def feats_to(i):
        p = wrap(mine + i, planes)
        return remote(features, plane_feats.at[mine], fp_send.at[i], fp_recv.at[i], {"region": p})

    def feats_from(i):
        p = wrap(mine - i, planes)
        return remote(features, plane_feats.at[p], fp_send.at[i], fp_recv.at[i], {"region": p})

    each(1, planes, lambda i: feats_to(i).start())

    shift = mine * (blk * shards) + (pos - 2) * blk
    for copy in loads[2:]:
        copy.wait()
    place = (neighbors[...] - shift).astype(F32).T
    flow = flows[...].astype(F32).T
    lane16 = lax.broadcasted_iota(jnp.int32, (slots, blk), 1)
    count = jnp.zeros((1, blk), jnp.int32)
    for b in range(blk):
        count = jnp.where(lax.broadcasted_iota(jnp.int32, (1, blk), 1) == b, counts[b], count)
    valid = lax.broadcasted_iota(jnp.int32, (slots, blk), 0) < count
    lane = lax.broadcasted_iota(jnp.int32, (slots, 128), 1).astype(F32)
    for b in range(blk):
        here = (lane == place[:, b:b + 1]) | (lane == 5 * blk + b)
        onehot[b * slots:(b + 1) * slots, :] = jnp.where(here, 1.0, 0.0).astype(BF16)
    anchor_total = jnp.sum(flow, axis=0, keepdims=True)
    proj[...] = jnp.zeros_like(proj)
    keep_tile.wait()

    keep_first(anchor_hbm).wait()

    zs = depth // 4
    first_block = z // zs

    def block_at(n):
        return wrap(first_block + (0, 1, -1, 2)[n], 4)

    def along_v(b, i):
        tile = weight_part(b * zs, zs, core, u, v, 1)
        return remote(
            tile, tile, p1_send.at[b * side + i], p1_recv.at[b * side + i], at_uv(u, wrap(v + i, side))
        )

    def from_v(b, i):
        vv = wrap(v - i, side)
        tile = weight_part(b * zs, zs, core, u, vv, 1)
        return remote(tile, tile, p1_send.at[b * side + i], p1_recv.at[b * side + i], at_uv(u, vv))

    def along_u(b, i):
        part = weight_part(b * zs, zs, core, u, 0, side)
        return remote(
            part, part, p2_send.at[b * side + i], p2_recv.at[b * side + i], at_uv(wrap(u + i, side), v)
        )

    def from_u(b, i):
        uu = wrap(u - i, side)
        part = weight_part(b * zs, zs, core, uu, 0, side)
        return remote(part, part, p2_send.at[b * side + i], p2_recv.at[b * side + i], at_uv(uu, v))

    def hand(b, i):
        part = weight_part(b * zs, zs, core, wrap(u - i, side), 0, side)
        return remote(part, part, sb_send.at[b * side + i], sb_recv.at[b * side + i], sibling)

    def take(b, i):
        part = weight_part(b * zs, zs, 1 - core, wrap(v - i, side), 0, side)
        return remote(part, part, sb_send.at[b * side + i], sb_recv.at[b * side + i], sibling)

    def hand_first(b, cc):
        part = tile_w.at[pl.ds(b * zs, zs), cc]
        return remote(part, part, fs_send.at[b], fs_recv.at[b], sibling)

    def first_block_in(n):
        b = block_at(n)
        for k in range(zs):

            @pl.when(b * zs + k != z)
            def _():
                first_from_z(b * zs + k).wait_recv()

        hand_first(b, core).start()

    def hid_block_in(n):
        b = block_at(n)
        for k in range(zs):

            @pl.when(b * zs + k != z)
            def _():
                hid_from_z(b * zs + k).wait_recv()

        for i in range(1, side):
            along_v(b, i).start()

    def v_in_block(n):
        b = block_at(n)
        for i in range(1, side):
            from_v(b, i).wait_recv()
        for i in range(1, side):
            along_u(b, i).start()
        hand(b, 0).start()

    def u_in_block(n):
        b = block_at(n)
        for i in range(1, side):
            from_u(b, i).wait_recv()
            hand(b, i).start()

    first_block_in(0)
    hid_block_in(0)
    first_block_in(1)
    first_block_in(2)
    first_block_in(3)
    v_in_block(0)

    each(1, planes, lambda i: feats_from(i).wait_recv())
    each(0, 4, lambda b: hand_first(b, 1 - core).wait_recv())
    part_proj[...] = jnp.dot(
        plane_feats[...].reshape(planes * blk, feat), tile_w[...].reshape(feat, tile_cols),
        preferred_element_type=F32,
    ).reshape(planes, blk, tile_cols)

    def proj_tile(p):
        at = pl.multiple_of((p % half_planes) * tile_cols, tile_cols)
        return own_proj.at[p // half_planes, :, pl.ds(at, tile_cols)]

    def proj_to(i):
        p = wrap(mine + i, planes)
        return remote(part_proj.at[p], proj_tile(mine), pp_send.at[i], pp_recv.at[i], {"region": p})

    def proj_from(i):
        p = wrap(mine - i, planes)
        return remote(part_proj.at[p], proj_tile(p), pp_send.at[i], pp_recv.at[i], {"region": p})

    each(1, planes, lambda i: proj_to(i).start())
    keep_proj = pltpu.make_async_copy(part_proj.at[mine], proj_tile(mine), local_sem.at[3])
    keep_proj.start()

    hid_block_in(1)
    hid_block_in(2)
    v_in_block(1)
    hid_block_in(3)
    v_in_block(2)
    u_in_block(0)
    keep_proj.wait()
    each(1, planes, lambda i: proj_from(i).wait_recv())

    def halo(by):
        return remote(
            own_proj.at[1], window.at[2 - by], halo_send.at[by + 2], halo_recv.at[by + 2],
            {"shard": wrap(pos + by, shards)},
        )

    for by in (-2, -1, 1, 2):
        halo(by).start()
    window[2] = own_proj[1]
    v_in_block(3)
    u_in_block(1)
    u_in_block(2)
    u_in_block(3)
    for by in (-2, -1, 1, 2):
        halo(by).wait_recv()

    rows = 5 * blk
    dest = window[...].reshape(rows, hid)
    dest_top = dest.astype(BF16)
    proj[0:rows] = dest_top
    proj[128:128 + rows] = (dest - dest_top.astype(F32)).astype(BF16)
    anchor = own_proj[0]
    anchor_top = anchor.astype(BF16)
    proj[rows:rows + blk] = anchor_top
    proj[128 + rows:128 + rows + blk] = (anchor - anchor_top.astype(F32)).astype(BF16)
    each(0, 4 * side, lambda i: take(i // side, i % side).wait_recv())

    group = 4
    size = group * slots
    weight = w_out[...].astype(F32).reshape(1, hid)

    def score(i, scores):
        at = pl.multiple_of(i * size, size)
        pick = onehot[pl.ds(at, size), :]
        both = jnp.concatenate([pick, pick], axis=1)
        first = jnp.maximum(jnp.dot(both, proj[...], preferred_element_type=F32), 0.0).astype(BF16)
        first_t[:, pl.ds(at, size)] = first.T
        act = jnp.maximum(
            jnp.dot(first, weights[...].reshape(hid, hid), preferred_element_type=F32), 0.0
        )
        active[pl.ds(at, size), :] = act
        col = jnp.sum(act * weight, axis=1, keepdims=True)
        for a in range(group):
            scores = jnp.where(lane16 == i * group + a, col[a * slots:(a + 1) * slots], scores)
        return scores

    scores = lax.fori_loop(0, blk // group, score, jnp.zeros((slots, blk), F32))

    top = jnp.max(jnp.where(valid, scores, -jnp.inf), axis=0, keepdims=True)
    expo = jnp.where(valid, jnp.exp(scores - top), 0.0)
    mass = jnp.sum(expo, axis=0, keepdims=True)
    probs = expo / mass
    logp = scores - top - jnp.log(mass)
    sgrad = jnp.where(valid, probs * anchor_total - flow, 0.0)
    numer = -jnp.sum(jnp.where(valid, flow * logp, 0.0))
    total = jnp.sum(anchor_total)

    def back(i, gout):
        at = pl.multiple_of(i * size, size)
        col = jnp.concatenate(
            [
                jnp.sum(jnp.where(lane16 == i * group + a, sgrad, 0.0), axis=1, keepdims=True)
                for a in range(group)
            ],
            axis=0,
        )
        act = active[pl.ds(at, size), :]
        pre[pl.ds(at, size), :] = jnp.where(act > 0, col * weight, 0.0).astype(BF16)
        return gout + jnp.sum((col * act).reshape(size // 8, 8, hid), axis=0)

    gout = lax.fori_loop(0, blk // group, back, jnp.zeros((8, hid), F32))
    gout = jnp.sum(gout, axis=0, keepdims=True)

    width = hid // 8
    for r in range(8):
        extra[r:r + 1, :] = gout[:, r * width:(r + 1) * width]
    row = lax.broadcasted_iota(jnp.int32, (8, width), 0)
    extra[8:16, :] = jnp.where(row == 0, numer, jnp.where(row == 1, total, 0.0))

    def extra_to_z(i):
        return remote(extra, extra_z.at[z], ez_send.at[i], ez_recv.at[i], at_z(wrap(z + i, depth)))

    def extra_from_z(i):
        where = wrap(z - i, depth)
        return remote(extra, extra_z.at[where], ez_send.at[i], ez_recv.at[i], at_z(where))

    def extra_to_plane(i):
        to = {"region": wrap(mine + i, planes)}
        return remote(extra_zsum, extra_plane.at[mine], ep_send.at[i], ep_recv.at[i], to)

    def extra_from_plane(i):
        p = wrap(mine - i, planes)
        return remote(extra_zsum, extra_plane.at[p], ep_send.at[i], ep_recv.at[i], {"region": p})

    each(1, depth, lambda i: extra_to_z(i).start())
    extra_z[z] = extra[...]

    wide = group_cols // 2
    turns = hid // wide

    def turn(n):
        return pl.ds(pl.multiple_of(n * wide, wide), wide)

    def to_sibling(n):
        return remote(
            grad.at[:, 1 - core, :, :, turn(n)], sib_grad.at[:, :, :, turn(n)], gs_send.at[n], gs_recv.at[n], sibling
        )

    def grads(n):
        part = jnp.dot(first_t[...], pre[:, turn(n)], preferred_element_type=F32)
        grad[:, :, :, :, turn(n)] = part.reshape(depth, 2, 2, 16, wide).astype(BF16)
        to_sibling(n).start()

    each(0, turns, grads)

    def to_u(n, h):
        uu = h * per_half + n // 2
        inside = pl.ds(pl.multiple_of((n % 2) * wide, wide), wide)
        return remote(
            chip_grad.at[:, h, :, turn(n)], u_in.at[u, :, :, inside],
            gu_send.at[n * 2 + h], gu_recv.at[u * 2 + n % 2], at_uv(uu, v),
        )

    def from_u_grad(uu, k):
        inside = pl.ds(pl.multiple_of(k * wide, wide), wide)
        return remote(
            chip_grad.at[:, 0, :, 0:wide], u_in.at[uu, :, :, inside],
            gu_send.at[0], gu_recv.at[uu * 2 + k], at_uv(uu, v),
        )

    def join(n):
        to_sibling(n).wait_recv()
        mine_part = grad[:, core, :, :, turn(n)].astype(F32)
        chip_grad[:, :, :, turn(n)] = (mine_part + sib_grad[:, :, :, turn(n)].astype(F32)).astype(BF16)
        for h in range(2):

            @pl.when(h * per_half + n // 2 != u)
            def _():
                to_u(n, h).start()

    each(0, turns, join)

    def to_v(i):
        vv = wrap(v + i, side)
        part = u_sum.at[:, :, pl.ds(pl.multiple_of(vv * tile_cols, tile_cols), tile_cols)]
        return remote(part, v_in.at[v], gv_send.at[i], gv_recv.at[i], at_uv(u, vv))

    def from_v_grad(i):
        vv = wrap(v - i, side)
        part = u_sum.at[:, :, 0:tile_cols]
        return remote(part, v_in.at[vv], gv_send.at[i], gv_recv.at[i], at_uv(u, vv))

    for i in range(1, side):
        for k in range(2):
            from_u_grad(wrap(u + i, side), k).wait_recv()

    own_group = span(u, 0, side)

    def sum_u(i):
        acc = chip_grad[pl.ds(i * zs, zs), u // per_half, :, own_group].astype(F32)
        for k in range(1, side):
            acc = acc + u_in[wrap(u + k, side), pl.ds(i * zs, zs)].astype(F32)
        u_sum[pl.ds(i * zs, zs)] = acc.astype(BF16)

    each(0, 4, sum_u)
    for i in range(1, side):
        to_v(i).start()

    each(1, depth, lambda i: extra_from_z(i).wait_recv())
    extra_zsum[...] = jnp.sum(extra_z[...], axis=0)
    each(1, planes, lambda i: extra_to_plane(i).start())
    extra_plane[mine] = extra_zsum[...]

    def to_z(i):
        where = wrap(z + i, depth)
        return remote(plane_sum.at[where], z_in.at[z], gz_send.at[i], gz_recv.at[i], at_z(where))

    def from_z(i):
        where = wrap(z - i, depth)
        return remote(plane_sum.at[where], z_in.at[where], gz_send.at[i], gz_recv.at[i], at_z(where))

    for i in range(1, side):
        from_v_grad(i).wait_recv()
    own_cols = pl.ds(pl.multiple_of(v * tile_cols, tile_cols), tile_cols)
    acc = u_sum[:, :, own_cols].astype(F32)
    for k in range(1, side):
        acc = acc + v_in[wrap(v + k, side)].astype(F32)
    plane_sum[...] = acc.astype(BF16)
    each(1, depth, lambda i: to_z(i).start())
    z_in[z] = plane_sum[z]

    each(1, planes, lambda i: extra_from_plane(i).wait_recv())
    extra_psum[...] = jnp.sum(extra_plane[...], axis=0)
    extra_swap = remote(extra_psum, extra_sib, es_send, es_recv, sibling)
    extra_swap.start()
    extra_swap.wait_recv()
    sums_all = extra_psum[...] + extra_sib[...]
    inverse = 1.0 / sums_all[9:10, :]
    gout_out[...] = sums_all[0:8, :] * inverse
    loss_out[...] = sums_all[8:9, 0:1] * inverse[:, 0:1]

    each(1, depth, lambda i: from_z(i).wait_recv())
    own_rows[...] = jnp.sum(z_in[...].astype(F32), axis=0) * inverse[0:1, 0:1]

    def out_tile(p):
        py, px = p // side, p % side
        uu = py + core * (px - py)
        vv = px + core * (py - px)
        return grad_out.at[pl.ds(pl.multiple_of((uu // per_half) * 16, 16), 16), span(uu, vv, 1)]

    def share(i):
        to = {"region": wrap(mine + i, planes)}
        return remote(own_rows, out_tile(mine), ga_send.at[i], ga_recv.at[i], to)

    def shared(i):
        p = wrap(mine - i, planes)
        return remote(own_rows, out_tile(p), ga_send.at[i], ga_recv.at[i], {"region": p})

    each(1, planes, lambda i: share(i).start())
    own_out = pltpu.make_async_copy(own_rows, out_tile(mine), local_sem.at[1])
    own_out.start()

    for by in (-2, -1, 1, 2):
        halo(by).wait_send()
    each(1, depth, lambda i: first_to_z(i, anchor_hbm).wait_send())
    each(1, depth, lambda i: hid_to_z(i).wait_send())
    each(0, 4, lambda b: hand_first(b, core).wait_send())
    each(1, planes, lambda i: feats_to(i).wait_send())
    each(1, planes, lambda i: proj_to(i).wait_send())

    def weights_left(b):
        for i in range(1, side):
            along_v(b, i).wait_send()
            along_u(b, i).wait_send()
        for i in range(side):
            hand(b, i).wait_send()

    each(0, 4, weights_left)
    each(1, depth, lambda i: extra_to_z(i).wait_send())
    each(1, planes, lambda i: extra_to_plane(i).wait_send())
    extra_swap.wait_send()
    each(0, turns, lambda n: to_sibling(n).wait_send())

    def u_left(n):
        for h in range(2):

            @pl.when(h * per_half + n // 2 != u)
            def _():
                to_u(n, h).wait_send()

    each(0, turns, u_left)
    for i in range(1, side):
        to_v(i).wait_send()
    each(1, depth, lambda i: to_z(i).wait_send())
    own_out.wait()
    each(1, planes, lambda i: shared(i).wait_recv())
    each(1, planes, lambda i: share(i).wait_send())


def shards(tiles, tile_block, neighbors, counts, flows, w_anchor, w_dest, w_hidden, w_out):
    planes, shard_count = lax.axis_size("region"), lax.axis_size("shard")
    side = 4 if planes == 16 else 2
    depth = shard_count // 2
    blk, slots = neighbors.shape
    feat, hid = tiles.shape[1], w_hidden.shape[1]
    pairs = blk * slots
    group_cols = hid // (side // 2)
    tile_cols = group_cols // side
    turns = hid // (group_cols // 2)
    width = hid // 8
    vmem = pl.BlockSpec(memory_space=pltpu.VMEM)
    hbm = pl.BlockSpec(memory_space=pltpu.HBM)
    dma = lambda n: pltpu.SemaphoreType.DMA((n,))
    scratch = [
        pltpu.VMEM(tiles.shape, BF16),
        pltpu.VMEM((1, tile_block.shape[0]), jnp.int32),
        pltpu.VMEM((blk, slots), jnp.int32),
        pltpu.SMEM((blk,), jnp.int32),
        pltpu.VMEM((blk, slots), jnp.int32),
        pltpu.VMEM((hid,), BF16),
        pltpu.VMEM((depth, 2, 2, 16, hid), BF16),
        pltpu.VMEM((blk, feat), BF16),
        pltpu.VMEM((depth, 2, 16, tile_cols), BF16),
        pltpu.VMEM((planes, blk, feat), BF16),
        pltpu.VMEM((planes, blk, tile_cols), F32),
        pltpu.VMEM((2, blk, hid), F32),
        pltpu.VMEM((5, blk, hid), F32),
        pltpu.VMEM((256, hid), BF16),
        pltpu.VMEM((pairs, 128), BF16),
        pltpu.VMEM((hid, pairs), BF16),
        pltpu.VMEM((pairs, hid), F32),
        pltpu.VMEM((pairs, hid), BF16),
        pltpu.VMEM((depth, 2, 2, 16, hid), BF16),
        pltpu.VMEM((depth, 2, 16, hid), BF16),
        pltpu.VMEM((depth, 2, 16, hid), BF16),
        pltpu.VMEM((side, depth, 16, group_cols), BF16),
        pltpu.VMEM((depth, 16, group_cols), BF16),
        pltpu.VMEM((side, depth, 16, tile_cols), BF16),
        pltpu.VMEM((depth, 16, tile_cols), BF16),
        pltpu.VMEM((depth, 16, tile_cols), BF16),
        pltpu.VMEM((16, tile_cols), F32),
        pltpu.VMEM((16, width), F32),
        pltpu.VMEM((depth, 16, width), F32),
        pltpu.VMEM((16, width), F32),
        pltpu.VMEM((planes, 16, width), F32),
        pltpu.VMEM((16, width), F32),
        pltpu.VMEM((16, width), F32),
        dma(5), dma(5), dma(depth), dma(depth), dma(4), dma(4), dma(planes), dma(planes), dma(planes), dma(planes),
        dma(depth), dma(depth), dma(4 * side), dma(4 * side), dma(4 * side), dma(4 * side),
        dma(4 * side), dma(4 * side), dma(turns), dma(turns), dma(2 * turns), dma(2 * side), dma(side), dma(side),
        dma(depth), dma(depth), dma(planes), dma(planes), dma(depth), dma(depth), dma(planes), dma(planes),
        pltpu.SemaphoreType.DMA, pltpu.SemaphoreType.DMA, dma(6), dma(4),
    ]
    grad, gout, loss = pl.pallas_call(
        functools.partial(step_kernel, (side, depth, blk, slots, hid)),
        out_shape=(
            jax.ShapeDtypeStruct((w_hidden.shape[0], hid), F32),
            jax.ShapeDtypeStruct((8, width), F32),
            jax.ShapeDtypeStruct((1, 1), F32),
        ),
        in_specs=[hbm] * 9,
        out_specs=(vmem, vmem, vmem),
        scratch_shapes=scratch,
        compiler_params=pltpu.CompilerParams(
            collective_id=0, has_side_effects=True, vmem_limit_bytes=62 * 2 ** 20
        ),
        cost_estimate=pl.CostEstimate(
            flops=4 * pairs * hid * hid, bytes_accessed=2 * tiles.size, transcendentals=pairs
        ),
    )(tiles, tile_block.reshape(1, -1), neighbors, counts, flows, w_anchor, w_dest, w_hidden, w_out)
    return grad, gout.reshape(hid), loss.reshape(())


def solution(mesh):
    return jax.shard_map(
        shards,
        mesh=mesh,
        in_specs=(
            P(("region", "shard"), None),
            P(("region", "shard")),
            P(("region", "shard"), None),
            P(("region", "shard")),
            P(("region", "shard"), None),
            P("shard", None),
            P("shard", None),
            P("shard", None),
            P(),
        ),
        out_specs=(P("shard", None), P(), P()),
        check_vma=False,
    )
```

```python
import functools

import jax
import jax.numpy as jnp
from jax import lax
from jax.experimental import pallas as pl
from jax.experimental.pallas import tpu as pltpu
from jax.sharding import PartitionSpec as P

MESH = pl.DeviceIdType.MESH
BF16 = jnp.bfloat16
F32 = jnp.float32


def remote(src, dst, send, recv, where):
    return pltpu.make_async_remote_copy(
        src_ref=src, dst_ref=dst, send_sem=send, recv_sem=recv, device_id=where, device_id_type=MESH
    )


def arrived(ref, sem, where):
    remote(ref, ref, sem, sem, where).wait_recv()


def left(ref, sem, where):
    remote(ref, ref, sem, sem, where).wait_send()


def step_kernel(
    dims,
    tiles_hbm, tile_block_hbm, neighbors_hbm, counts_hbm, flows_hbm, anchor_hbm, dest_hbm, hidden_hbm, out_hbm,
    grad_out, gout_out, loss_out,
    tiles, tile_block, neighbors, counts, flows, w_out,
    weights, features, tile_w, plane_feats, part_proj, own_proj, window, proj, onehot, first_t, active, pre, grad, sib_grad, chip_grad, u_in, u_sum, v_in,
    plane_sum, z_in, own_rows, extra, extra_z, extra_zsum, extra_plane, extra_psum, extra_sib,
    halo_send, halo_recv, fz_send, fz_recv, fs_send, fs_recv, fp_send, fp_recv, pp_send, pp_recv,
    az_send, az_recv, p1_send, p1_recv, p2_send, p2_recv, sb_send, sb_recv,
    gs_send, gs_recv, gu_send, gu_recv, gv_send, gv_recv, gz_send, gz_recv,
    ga_send, ga_recv, ez_send, ez_recv, ep_send, ep_recv, es_send, es_recv, load_sem, local_sem,
):
    side, depth, blk, slots, hid = dims
    planes = side * side
    pos = lax.axis_index("shard")
    mine = lax.axis_index("region")
    z, core = pos // 2, pos % 2
    shards = 2 * depth
    feat = tiles.shape[1]
    y, x = mine // side, mine % side
    u = y + core * (x - y)
    v = x + core * (y - x)
    per_half = side // 2
    group_cols = hid // per_half
    tile_cols = group_cols // side

    def wrap(i, n):
        return lax.rem(i + 2 * n, n)

    def at_z(where):
        return {"shard": where * 2 + core}

    def at_uv(uu, vv):
        return {"region": (uu * side + vv) * (1 - core) + (vv * side + uu) * core}

    sibling = {"shard": z * 2 + (1 - core)}
    cross = {"shard": wrap(pos + 2 * core - 1, shards)}

    def each(first, last, act):
        def body(i, c):
            act(i)
            return c

        lax.fori_loop(first, last, body, 0)

    loads = [
        pltpu.make_async_copy(tiles_hbm, tiles, load_sem.at[0]),
        pltpu.make_async_copy(tile_block_hbm, tile_block, load_sem.at[1]),
        pltpu.make_async_copy(neighbors_hbm, neighbors, load_sem.at[2]),
        pltpu.make_async_copy(counts_hbm, counts, load_sem.at[3]),
        pltpu.make_async_copy(flows_hbm, flows, load_sem.at[4]),
        pltpu.make_async_copy(out_hbm, w_out, load_sem.at[5]),
    ]
    barrier = pltpu.get_barrier_semaphore()

    def greet(where):
        pl.semaphore_signal(barrier, inc=1, device_id=where, device_id_type=MESH)

    def greet_z(i):
        greet(at_z(wrap(z + depth // 2 + i, depth)))
        greet(at_z(wrap(z + depth // 2 - i, depth)))

    greet(at_z(wrap(z + depth // 2, depth)))
    each(1, depth // 2, greet_z)
    each(1, planes, lambda i: greet({"region": wrap(mine + i, planes)}))
    greet(cross)
    greet(sibling)
    for copy in loads:
        copy.start()

    def span(uu, first, count):
        at = (uu % per_half) * group_cols + first * tile_cols
        return pl.ds(pl.multiple_of(at, tile_cols), count * tile_cols)

    def weight_part(where, count, cc, uu, first, tiles_of):
        return weights.at[pl.ds(where, count), cc, uu // per_half, :, span(uu, first, tiles_of)]

    half_planes = planes // 2
    matrix = mine // half_planes
    first_cols = pl.ds(pl.multiple_of((mine % half_planes) * tile_cols, tile_cols), tile_cols)
    hid_tile = hidden_hbm.at[pl.ds(pl.multiple_of((u // per_half) * 16, 16), 16), span(u, v, 1)]

    def weight_slot(where):
        return weights.at[where, core, u // per_half, :, span(u, v, 1)]

    zs = depth // 4
    first_block = z // zs

    def first_to_z(i, source):
        to = at_z(wrap(z + i, depth))
        return remote(source.at[:, first_cols], tile_w.at[z, core], fz_send, fz_recv.at[first_block], to)

    def hid_to_z(i):
        to = at_z(wrap(z + i, depth))
        return remote(hid_tile, weight_slot(z), az_send, az_recv.at[first_block], to)

    def keep_first(source):
        return pltpu.make_async_copy(source.at[:, first_cols], tile_w.at[z, core], local_sem.at[2])

    def near_first(start):
        def both_ways(i):
            start(i)
            start(depth - i)

        each(1, depth // 2, both_ways)
        start(depth // 2)

    pl.semaphore_wait(barrier, planes - 1 + depth - 1 + 2)
    for k, source in enumerate((anchor_hbm, dest_hbm)):

        @pl.when(matrix == k)
        def _():
            near_first(lambda i: first_to_z(i, source).start())
            keep_first(source).start()

    near_first(lambda i: hid_to_z(i).start())
    keep_tile = pltpu.make_async_copy(hid_tile, weight_slot(z), local_sem.at[0])
    keep_tile.start()

    loads[0].wait()
    loads[1].wait()
    member = tile_block[...] == lax.broadcasted_iota(jnp.int32, (blk, tile_block.shape[1]), 0)
    sums = jnp.dot(member.astype(BF16), tiles[...], preferred_element_type=F32)
    scale = lax.rsqrt(jnp.mean(sums * sums, axis=-1, keepdims=True) + 1e-05)
    features[...] = (sums * scale).astype(BF16)
    plane_feats[mine] = features[...]

    def feats_to(i):
        p = wrap(mine + i, planes)
        return remote(features, plane_feats.at[mine], fp_send, fp_recv, {"region": p})

    each(1, planes, lambda i: feats_to(i).start())

    shift = mine * (blk * shards) + (pos - 2) * blk
    for copy in loads[2:]:
        copy.wait()
    place = (neighbors[...] - shift).astype(F32).T
    flow = flows[...].astype(F32).T
    lane16 = lax.broadcasted_iota(jnp.int32, (slots, blk), 1)
    count = jnp.zeros((1, blk), jnp.int32)
    for b in range(blk):
        count = jnp.where(lax.broadcasted_iota(jnp.int32, (1, blk), 1) == b, counts[b], count)
    valid = lax.broadcasted_iota(jnp.int32, (slots, blk), 0) < count
    lane = lax.broadcasted_iota(jnp.int32, (slots, 128), 1).astype(F32)
    for b in range(blk):
        here = (lane == place[:, b:b + 1]) | (lane == 5 * blk + b)
        onehot[b * slots:(b + 1) * slots, :] = jnp.where(here, 1.0, 0.0).astype(BF16)
    anchor_total = jnp.sum(flow, axis=0, keepdims=True)
    proj[...] = jnp.zeros_like(proj)
    keep_tile.wait()

    keep_first(anchor_hbm).wait()

    def block_at(n):
        return wrap(first_block + (0, 1, -1, 2)[n], 4)

    def along_v(b, i):
        tile = weight_part(b * zs, zs, core, u, v, 1)
        return remote(
            tile, tile, p1_send, p1_recv.at[b], at_uv(u, wrap(v + i, side))
        )

    def along_u(b, i):
        part = weight_part(b * zs, zs, core, u, 0, side)
        return remote(
            part, part, p2_send, p2_recv.at[b * side + i], at_uv(wrap(u + i, side), v)
        )

    def from_u(b, i):
        uu = wrap(u - i, side)
        part = weight_part(b * zs, zs, core, uu, 0, side)
        return remote(part, part, p2_send, p2_recv.at[b * side + i], at_uv(uu, v))

    def hand(b, i):
        part = weight_part(b * zs, zs, core, wrap(u - i, side), 0, side)
        return remote(part, part, sb_send, sb_recv, sibling)

    def hand_first(b):
        part = tile_w.at[pl.ds(b * zs, zs), core]
        return remote(part, part, fs_send, fs_recv, sibling)

    def first_block_in(n):
        b = block_at(n)
        others = zs - 1 if n == 0 else zs
        if others:
            arrived(tile_w.at[pl.ds(b * zs, others), core], fz_recv.at[b], sibling)
        hand_first(b).start()

    def hid_block_in(n):
        b = block_at(n)
        others = zs - 1 if n == 0 else zs
        if others:
            arrived(weight_part(b * zs, others, core, u, v, 1), az_recv.at[b], sibling)
        for i in range(1, side):
            along_v(b, i).start()

    def v_in_block(n):
        b = block_at(n)
        arrived(weight_part(b * zs, zs, core, u, 0, side - 1), p1_recv.at[b], sibling)
        for i in range(1, side):
            along_u(b, i).start()
        hand(b, 0).start()

    def u_in_block(n):
        b = block_at(n)
        for i in range(1, side):
            from_u(b, i).wait_recv()
            hand(b, i).start()

    first_block_in(0)
    hid_block_in(0)
    first_block_in(1)
    first_block_in(2)
    first_block_in(3)
    v_in_block(0)

    arrived(plane_feats.at[0:planes - 1], fp_recv, sibling)
    arrived(tile_w.at[:, 1 - core], fs_recv, sibling)
    part_proj[...] = jnp.dot(
        plane_feats[...].reshape(planes * blk, feat), tile_w[...].reshape(feat, tile_cols),
        preferred_element_type=F32,
    ).reshape(planes, blk, tile_cols)

    def proj_tile(p):
        at = pl.multiple_of((p % half_planes) * tile_cols, tile_cols)
        return own_proj.at[p // half_planes, :, pl.ds(at, tile_cols)]

    def proj_to(i):
        p = wrap(mine + i, planes)
        return remote(part_proj.at[p], proj_tile(mine), pp_send, pp_recv, {"region": p})

    each(1, planes, lambda i: proj_to(i).start())
    keep_proj = pltpu.make_async_copy(part_proj.at[mine], proj_tile(mine), local_sem.at[3])
    keep_proj.start()

    hid_block_in(1)
    hid_block_in(2)
    v_in_block(1)
    hid_block_in(3)
    v_in_block(2)
    u_in_block(0)
    keep_proj.wait()
    arrived(part_proj.at[0:planes - 1], pp_recv, sibling)

    def halo(by):
        return remote(
            own_proj.at[1], window.at[2 - by], halo_send, halo_recv,
            {"shard": wrap(pos + by, shards)},
        )

    for by in (-2, -1, 1, 2):
        halo(by).start()
    window[2] = own_proj[1]
    v_in_block(3)
    u_in_block(1)
    u_in_block(2)
    u_in_block(3)
    arrived(window.at[0:4], halo_recv, sibling)

    rows = 5 * blk
    dest = window[...].reshape(rows, hid)
    dest_top = dest.astype(BF16)
    proj[0:rows] = dest_top
    proj[128:128 + rows] = (dest - dest_top.astype(F32)).astype(BF16)
    anchor = own_proj[0]
    anchor_top = anchor.astype(BF16)
    proj[rows:rows + blk] = anchor_top
    proj[128 + rows:128 + rows + blk] = (anchor - anchor_top.astype(F32)).astype(BF16)
    arrived(weights.at[:, 1 - core], sb_recv, sibling)

    group = 4
    size = group * slots
    weight = w_out[...].astype(F32).reshape(1, hid)

    def score(i, scores):
        at = pl.multiple_of(i * size, size)
        pick = onehot[pl.ds(at, size), :]
        both = jnp.concatenate([pick, pick], axis=1)
        first = jnp.maximum(jnp.dot(both, proj[...], preferred_element_type=F32), 0.0).astype(BF16)
        first_t[:, pl.ds(at, size)] = first.T
        act = jnp.maximum(
            jnp.dot(first, weights[...].reshape(hid, hid), preferred_element_type=F32), 0.0
        )
        active[pl.ds(at, size), :] = act
        col = jnp.sum(act * weight, axis=1, keepdims=True)
        for a in range(group):
            scores = jnp.where(lane16 == i * group + a, col[a * slots:(a + 1) * slots], scores)
        return scores

    scores = lax.fori_loop(0, blk // group, score, jnp.zeros((slots, blk), F32))

    top = jnp.max(jnp.where(valid, scores, -jnp.inf), axis=0, keepdims=True)
    expo = jnp.where(valid, jnp.exp(scores - top), 0.0)
    mass = jnp.sum(expo, axis=0, keepdims=True)
    probs = expo / mass
    logp = scores - top - jnp.log(mass)
    sgrad = jnp.where(valid, probs * anchor_total - flow, 0.0)
    numer = -jnp.sum(jnp.where(valid, flow * logp, 0.0))
    total = jnp.sum(anchor_total)

    def back(i, gout):
        at = pl.multiple_of(i * size, size)
        col = jnp.concatenate(
            [
                jnp.sum(jnp.where(lane16 == i * group + a, sgrad, 0.0), axis=1, keepdims=True)
                for a in range(group)
            ],
            axis=0,
        )
        act = active[pl.ds(at, size), :]
        pre[pl.ds(at, size), :] = jnp.where(act > 0, col * weight, 0.0).astype(BF16)
        return gout + jnp.sum((col * act).reshape(size // 8, 8, hid), axis=0)

    gout = lax.fori_loop(0, blk // group, back, jnp.zeros((8, hid), F32))
    gout = jnp.sum(gout, axis=0, keepdims=True)

    width = hid // 8
    for r in range(8):
        extra[r:r + 1, :] = gout[:, r * width:(r + 1) * width]
    row = lax.broadcasted_iota(jnp.int32, (8, width), 0)
    extra[8:16, :] = jnp.where(row == 0, numer, jnp.where(row == 1, total, 0.0))

    def extra_to_z(i):
        return remote(extra, extra_z.at[z], ez_send, ez_recv, at_z(wrap(z + i, depth)))

    def extra_to_plane(i):
        to = {"region": wrap(mine + i, planes)}
        return remote(extra_zsum, extra_plane.at[mine], ep_send, ep_recv, to)

    each(1, depth, lambda i: extra_to_z(i).start())
    extra_z[z] = extra[...]

    wide = group_cols // 2
    turns = hid // wide

    def turn(n):
        return pl.ds(pl.multiple_of(n * wide, wide), wide)

    def to_sibling(n):
        return remote(
            grad.at[:, 1 - core, :, :, turn(n)], sib_grad.at[:, :, :, turn(n)], gs_send, gs_recv.at[n], sibling
        )

    def grads(n):
        part = jnp.dot(first_t[...], pre[:, turn(n)], preferred_element_type=F32)
        grad[:, :, :, :, turn(n)] = part.reshape(depth, 2, 2, 16, wide).astype(BF16)
        to_sibling(n).start()

    each(0, turns, grads)

    def to_u(n, h):
        uu = h * per_half + n // 2
        inside = pl.ds(pl.multiple_of((n % 2) * wide, wide), wide)
        return remote(
            chip_grad.at[:, h, :, turn(n)], u_in.at[u, :, :, inside],
            gu_send, gu_recv, at_uv(uu, v),
        )

    def join(n):
        to_sibling(n).wait_recv()
        mine_part = grad[:, core, :, :, turn(n)].astype(F32)
        chip_grad[:, :, :, turn(n)] = (mine_part + sib_grad[:, :, :, turn(n)].astype(F32)).astype(BF16)
        for h in range(2):

            @pl.when(h * per_half + n // 2 != u)
            def _():
                to_u(n, h).start()

    each(0, turns, join)

    def to_v(i):
        vv = wrap(v + i, side)
        part = u_sum.at[:, :, pl.ds(pl.multiple_of(vv * tile_cols, tile_cols), tile_cols)]
        return remote(part, v_in.at[v], gv_send, gv_recv, at_uv(u, vv))

    arrived(u_in.at[0:side - 1], gu_recv, sibling)

    own_group = span(u, 0, side)

    def sum_u(i):
        acc = chip_grad[pl.ds(i * zs, zs), u // per_half, :, own_group].astype(F32)
        for k in range(1, side):
            acc = acc + u_in[wrap(u + k, side), pl.ds(i * zs, zs)].astype(F32)
        u_sum[pl.ds(i * zs, zs)] = acc.astype(BF16)

    each(0, 4, sum_u)
    for i in range(1, side):
        to_v(i).start()

    arrived(extra_z.at[0:depth - 1], ez_recv, sibling)
    extra_zsum[...] = jnp.sum(extra_z[...], axis=0)
    each(1, planes, lambda i: extra_to_plane(i).start())
    extra_plane[mine] = extra_zsum[...]

    def to_z(i):
        where = wrap(z + i, depth)
        return remote(plane_sum.at[where], z_in.at[z], gz_send, gz_recv, at_z(where))

    arrived(v_in.at[0:side - 1], gv_recv, sibling)
    own_cols = pl.ds(pl.multiple_of(v * tile_cols, tile_cols), tile_cols)
    acc = u_sum[:, :, own_cols].astype(F32)
    for k in range(1, side):
        acc = acc + v_in[wrap(v + k, side)].astype(F32)
    plane_sum[...] = acc.astype(BF16)
    each(1, depth, lambda i: to_z(i).start())
    z_in[z] = plane_sum[z]

    arrived(extra_plane.at[0:planes - 1], ep_recv, sibling)
    extra_psum[...] = jnp.sum(extra_plane[...], axis=0)
    extra_swap = remote(extra_psum, extra_sib, es_send, es_recv, sibling)
    extra_swap.start()
    extra_swap.wait_recv()
    sums_all = extra_psum[...] + extra_sib[...]
    inverse = 1.0 / sums_all[9:10, :]
    gout_out[...] = sums_all[0:8, :] * inverse
    loss_out[...] = sums_all[8:9, 0:1] * inverse[:, 0:1]

    arrived(z_in.at[0:depth - 1], gz_recv, sibling)
    own_rows[...] = jnp.sum(z_in[...].astype(F32), axis=0) * inverse[0:1, 0:1]

    def out_tile(p):
        py, px = p // side, p % side
        uu = py + core * (px - py)
        vv = px + core * (py - px)
        return grad_out.at[pl.ds(pl.multiple_of((uu // per_half) * 16, 16), 16), span(uu, vv, 1)]

    def share(i):
        to = {"region": wrap(mine + i, planes)}
        return remote(own_rows, out_tile(mine), ga_send, ga_recv, to)

    each(1, planes, lambda i: share(i).start())
    own_out = pltpu.make_async_copy(own_rows, out_tile(mine), local_sem.at[1])
    own_out.start()

    left(tile_w.at[0:depth - 1, core], fz_send, sibling)
    left(tile_w.at[0:depth - 1, core], az_send, sibling)
    left(tile_w.at[:, core], fs_send, sibling)
    left(plane_feats.at[0:planes - 1], fp_send, sibling)
    left(part_proj.at[0:planes - 1], pp_send, sibling)
    left(window.at[0:4], halo_send, sibling)
    left(weight_part(0, depth, core, u, 0, side - 1), p1_send, sibling)
    left(weights.at[0:(side - 1) * depth // side, core], p2_send, sibling)
    left(weights.at[:, core], sb_send, sibling)
    left(sib_grad, gs_send, sibling)
    left(u_in.at[0:side - 1], gu_send, sibling)
    left(v_in.at[0:side - 1], gv_send, sibling)
    left(z_in.at[0:depth - 1], gz_send, sibling)
    left(extra_z.at[0:depth - 1], ez_send, sibling)
    left(extra_plane.at[0:planes - 1], ep_send, sibling)
    extra_swap.wait_send()
    own_out.wait()
    arrived(part_proj.at[0:planes - 1], ga_recv, sibling)
    left(part_proj.at[0:planes - 1], ga_send, sibling)


def shards(tiles, tile_block, neighbors, counts, flows, w_anchor, w_dest, w_hidden, w_out):
    planes, shard_count = lax.axis_size("region"), lax.axis_size("shard")
    side = 4 if planes == 16 else 2
    depth = shard_count // 2
    blk, slots = neighbors.shape
    feat, hid = tiles.shape[1], w_hidden.shape[1]
    pairs = blk * slots
    group_cols = hid // (side // 2)
    tile_cols = group_cols // side
    turns = hid // (group_cols // 2)
    width = hid // 8
    vmem = pl.BlockSpec(memory_space=pltpu.VMEM)
    hbm = pl.BlockSpec(memory_space=pltpu.HBM)
    dma = lambda n: pltpu.SemaphoreType.DMA((n,))
    one = pltpu.SemaphoreType.DMA
    scratch = [
        pltpu.VMEM(tiles.shape, BF16),
        pltpu.VMEM((1, tile_block.shape[0]), jnp.int32),
        pltpu.VMEM((blk, slots), jnp.int32),
        pltpu.SMEM((blk,), jnp.int32),
        pltpu.VMEM((blk, slots), jnp.int32),
        pltpu.VMEM((hid,), BF16),
        pltpu.VMEM((depth, 2, 2, 16, hid), BF16),
        pltpu.VMEM((blk, feat), BF16),
        pltpu.VMEM((depth, 2, 16, tile_cols), BF16),
        pltpu.VMEM((planes, blk, feat), BF16),
        pltpu.VMEM((planes, blk, tile_cols), F32),
        pltpu.VMEM((2, blk, hid), F32),
        pltpu.VMEM((5, blk, hid), F32),
        pltpu.VMEM((256, hid), BF16),
        pltpu.VMEM((pairs, 128), BF16),
        pltpu.VMEM((hid, pairs), BF16),
        pltpu.VMEM((pairs, hid), F32),
        pltpu.VMEM((pairs, hid), BF16),
        pltpu.VMEM((depth, 2, 2, 16, hid), BF16),
        pltpu.VMEM((depth, 2, 16, hid), BF16),
        pltpu.VMEM((depth, 2, 16, hid), BF16),
        pltpu.VMEM((side, depth, 16, group_cols), BF16),
        pltpu.VMEM((depth, 16, group_cols), BF16),
        pltpu.VMEM((side, depth, 16, tile_cols), BF16),
        pltpu.VMEM((depth, 16, tile_cols), BF16),
        pltpu.VMEM((depth, 16, tile_cols), BF16),
        pltpu.VMEM((16, tile_cols), F32),
        pltpu.VMEM((16, width), F32),
        pltpu.VMEM((depth, 16, width), F32),
        pltpu.VMEM((16, width), F32),
        pltpu.VMEM((planes, 16, width), F32),
        pltpu.VMEM((16, width), F32),
        pltpu.VMEM((16, width), F32),
        one, one, one, dma(4), one, one, one, one, one, one,
        one, dma(4), one, dma(4), one, dma(4 * side), one, one,
        one, dma(turns), one, one, one, one, one, one,
        one, one, one, one, one, one, one, one, dma(6), dma(4),
    ]
    grad, gout, loss = pl.pallas_call(
        functools.partial(step_kernel, (side, depth, blk, slots, hid)),
        out_shape=(
            jax.ShapeDtypeStruct((w_hidden.shape[0], hid), F32),
            jax.ShapeDtypeStruct((8, width), F32),
            jax.ShapeDtypeStruct((1, 1), F32),
        ),
        in_specs=[hbm] * 9,
        out_specs=(hbm, vmem, vmem),
        scratch_shapes=scratch,
        compiler_params=pltpu.CompilerParams(
            collective_id=0, has_side_effects=True, vmem_limit_bytes=62 * 2 ** 20
        ),
        cost_estimate=pl.CostEstimate(
            flops=4 * pairs * hid * hid, bytes_accessed=2 * tiles.size, transcendentals=pairs
        ),
    )(tiles, tile_block.reshape(1, -1), neighbors, counts, flows, w_anchor, w_dest, w_hidden, w_out)
    return grad, gout.reshape(hid), loss.reshape(())


def solution(mesh):
    return jax.shard_map(
        shards,
        mesh=mesh,
        in_specs=(
            P(("region", "shard"), None),
            P(("region", "shard")),
            P(("region", "shard"), None),
            P(("region", "shard")),
            P(("region", "shard"), None),
            P("shard", None),
            P("shard", None),
            P("shard", None),
            P(),
        ),
        out_specs=(P("shard", None), P(), P()),
        check_vma=False,
    )
```

```python
import functools

import jax
import jax.numpy as jnp
from jax import lax
from jax.experimental import pallas as pl
from jax.experimental.pallas import tpu as pltpu
from jax.sharding import PartitionSpec as P

MESH = pl.DeviceIdType.MESH
BF16 = jnp.bfloat16
F32 = jnp.float32


def remote(src, dst, send, recv, where):
    return pltpu.make_async_remote_copy(
        src_ref=src, dst_ref=dst, send_sem=send, recv_sem=recv, device_id=where, device_id_type=MESH
    )


def arrived(ref, sem, where):
    remote(ref, ref, sem, sem, where).wait_recv()


def left(ref, sem, where):
    remote(ref, ref, sem, sem, where).wait_send()


def step_kernel(
    dims,
    tiles_hbm, tile_block_hbm, neighbors_hbm, counts_hbm, flows_hbm, anchor_hbm, dest_hbm, hidden_hbm, out_hbm,
    grad_out, gout_out, loss_out,
    tiles, tile_block, neighbors, counts, flows, w_out,
    weights, features, tile_w, plane_feats, part_proj, own_proj, window, proj, onehot, first, first_t, lanes, out_weight, active, pre, grad, sib_grad, chip_grad, u_in, u_sum, v_in,
    plane_sum, z_in, own_rows, extra, extra_z, extra_zsum, extra_plane, extra_psum, extra_sib,
    halo_send, halo_recv, fz_send, fz_recv, fs_send, fs_recv, fp_send, fp_recv, pp_send, pp_recv,
    az_send, az_recv, p1_send, p1_recv, p2_send, p2_recv, sb_send, sb_recv,
    gs_send, gs_recv, gu_send, gu_recv, gv_send, gv_recv, gz_send, gz_recv,
    ga_send, ga_recv, ez_send, ez_recv, ep_send, ep_recv, es_send, es_recv, load_sem, local_sem,
):
    side, depth, blk, slots, hid = dims
    planes = side * side
    pos = lax.axis_index("shard")
    mine = lax.axis_index("region")
    z, core = pos // 2, pos % 2
    shards = 2 * depth
    feat = tiles.shape[1]
    y, x = mine // side, mine % side
    u = y + core * (x - y)
    v = x + core * (y - x)
    per_half = side // 2
    group_cols = hid // per_half
    tile_cols = group_cols // side

    def wrap(i, n):
        return lax.rem(i + 2 * n, n)

    def at_z(where):
        return {"shard": where * 2 + core}

    def at_uv(uu, vv):
        return {"region": (uu * side + vv) * (1 - core) + (vv * side + uu) * core}

    sibling = {"shard": z * 2 + (1 - core)}
    cross = {"shard": wrap(pos + 2 * core - 1, shards)}

    def each(first, last, act):
        def body(i, c):
            act(i)
            return c

        lax.fori_loop(first, last, body, 0)

    loads = [
        pltpu.make_async_copy(tiles_hbm, tiles, load_sem.at[0]),
        pltpu.make_async_copy(tile_block_hbm, tile_block, load_sem.at[1]),
        pltpu.make_async_copy(neighbors_hbm, neighbors, load_sem.at[2]),
        pltpu.make_async_copy(counts_hbm, counts, load_sem.at[3]),
        pltpu.make_async_copy(flows_hbm, flows, load_sem.at[4]),
        pltpu.make_async_copy(out_hbm, w_out, load_sem.at[5]),
    ]
    barrier = pltpu.get_barrier_semaphore()

    def greet(where):
        pl.semaphore_signal(barrier, inc=1, device_id=where, device_id_type=MESH)

    def greet_z(i):
        greet(at_z(wrap(z + depth // 2 + i, depth)))
        greet(at_z(wrap(z + depth // 2 - i, depth)))

    greet(at_z(wrap(z + depth // 2, depth)))
    each(1, depth // 2, greet_z)
    each(1, planes, lambda i: greet({"region": wrap(mine + i, planes)}))
    greet(cross)
    greet(sibling)
    for copy in loads:
        copy.start()

    def span(uu, first, count):
        at = (uu % per_half) * group_cols + first * tile_cols
        return pl.ds(pl.multiple_of(at, tile_cols), count * tile_cols)

    def weight_part(where, count, cc, uu, first, tiles_of):
        return weights.at[pl.ds(where, count), cc, uu // per_half, :, span(uu, first, tiles_of)]

    half_planes = planes // 2
    matrix = mine // half_planes
    first_cols = pl.ds(pl.multiple_of((mine % half_planes) * tile_cols, tile_cols), tile_cols)
    hid_tile = hidden_hbm.at[pl.ds(pl.multiple_of((u // per_half) * 16, 16), 16), span(u, v, 1)]

    def weight_slot(where):
        return weights.at[where, core, u // per_half, :, span(u, v, 1)]

    zs = depth // 4
    first_block = z // zs

    def first_to_z(i, source):
        to = at_z(wrap(z + i, depth))
        return remote(source.at[:, first_cols], tile_w.at[z, core], fz_send, fz_recv.at[first_block], to)

    def hid_to_z(i):
        to = at_z(wrap(z + i, depth))
        return remote(hid_tile, weight_slot(z), az_send, az_recv.at[first_block], to)

    def keep_first(source):
        return pltpu.make_async_copy(source.at[:, first_cols], tile_w.at[z, core], local_sem.at[2])

    def near_first(start):
        def both_ways(i):
            start(i)
            start(depth - i)

        each(1, depth // 2, both_ways)
        start(depth // 2)

    pl.semaphore_wait(barrier, planes - 1 + depth - 1 + 2)
    for k, source in enumerate((anchor_hbm, dest_hbm)):

        @pl.when(matrix == k)
        def _():
            near_first(lambda i: first_to_z(i, source).start())
            keep_first(source).start()

    near_first(lambda i: hid_to_z(i).start())
    keep_tile = pltpu.make_async_copy(hid_tile, weight_slot(z), local_sem.at[0])
    keep_tile.start()

    loads[0].wait()
    loads[1].wait()
    member = tile_block[...] == lax.broadcasted_iota(jnp.int32, (blk, tile_block.shape[1]), 0)
    sums = jnp.dot(member.astype(BF16), tiles[...], preferred_element_type=F32)
    scale = lax.rsqrt(jnp.mean(sums * sums, axis=-1, keepdims=True) + 1e-05)
    features[...] = (sums * scale).astype(BF16)
    plane_feats[mine] = features[...]

    def feats_to(i):
        p = wrap(mine + i, planes)
        return remote(features, plane_feats.at[mine], fp_send, fp_recv, {"region": p})

    each(1, planes, lambda i: feats_to(i).start())

    shift = mine * (blk * shards) + (pos - 2) * blk
    for copy in loads[2:]:
        copy.wait()
    place = (neighbors[...] - shift).astype(F32).T
    flow = flows[...].astype(F32).T
    lane16 = lax.broadcasted_iota(jnp.int32, (slots, blk), 1)
    count = jnp.zeros((1, blk), jnp.int32)
    for b in range(blk):
        count = jnp.where(lax.broadcasted_iota(jnp.int32, (1, blk), 1) == b, counts[b], count)
    valid = lax.broadcasted_iota(jnp.int32, (slots, blk), 0) < count
    lane = lax.broadcasted_iota(jnp.int32, (slots, 128), 1).astype(F32)
    for b in range(blk):
        here = (lane == place[:, b:b + 1]) | (lane == 5 * blk + b)
        onehot[b * slots:(b + 1) * slots, :] = jnp.where(here, 1.0, 0.0).astype(BF16)
    anchor_total = jnp.sum(flow, axis=0, keepdims=True)
    proj[...] = jnp.zeros_like(proj)
    keep_tile.wait()

    keep_first(anchor_hbm).wait()

    def block_at(n):
        return wrap(first_block + (0, 1, -1, 2)[n], 4)

    def along_v(b, i):
        tile = weight_part(b * zs, zs, core, u, v, 1)
        return remote(
            tile, tile, p1_send, p1_recv.at[b], at_uv(u, wrap(v + i, side))
        )

    def along_u(b, i):
        part = weight_part(b * zs, zs, core, u, 0, side)
        return remote(
            part, part, p2_send, p2_recv.at[b * side + i], at_uv(wrap(u + i, side), v)
        )

    def from_u(b, i):
        uu = wrap(u - i, side)
        part = weight_part(b * zs, zs, core, uu, 0, side)
        return remote(part, part, p2_send, p2_recv.at[b * side + i], at_uv(uu, v))

    def hand(b, i):
        part = weight_part(b * zs, zs, core, wrap(u - i, side), 0, side)
        return remote(part, part, sb_send, sb_recv, sibling)

    def hand_first(b):
        part = tile_w.at[pl.ds(b * zs, zs), core]
        return remote(part, part, fs_send, fs_recv, sibling)

    def first_block_in(n):
        b = block_at(n)
        others = zs - 1 if n == 0 else zs
        if others:
            arrived(tile_w.at[pl.ds(b * zs, others), core], fz_recv.at[b], sibling)
        hand_first(b).start()

    def hid_block_in(n):
        b = block_at(n)
        others = zs - 1 if n == 0 else zs
        if others:
            arrived(weight_part(b * zs, others, core, u, v, 1), az_recv.at[b], sibling)
        for i in range(1, side):
            along_v(b, i).start()

    def v_in_block(n):
        b = block_at(n)
        arrived(weight_part(b * zs, zs, core, u, 0, side - 1), p1_recv.at[b], sibling)
        for i in range(1, side):
            along_u(b, i).start()
        hand(b, 0).start()

    def u_in_block(n):
        b = block_at(n)
        for i in range(1, side):
            from_u(b, i).wait_recv()
            hand(b, i).start()

    first_block_in(0)
    hid_block_in(0)
    first_block_in(1)
    v_in_block(0)
    first_block_in(2)
    first_block_in(3)
    hid_block_in(1)

    arrived(plane_feats.at[0:planes - 1], fp_recv, sibling)
    arrived(tile_w.at[:, 1 - core], fs_recv, sibling)
    part_proj[...] = jnp.dot(
        plane_feats[...].reshape(planes * blk, feat), tile_w[...].reshape(feat, tile_cols),
        preferred_element_type=F32,
    ).reshape(planes, blk, tile_cols)

    def proj_tile(p):
        at = pl.multiple_of((p % half_planes) * tile_cols, tile_cols)
        return own_proj.at[p // half_planes, :, pl.ds(at, tile_cols)]

    def proj_to(i):
        p = wrap(mine + i, planes)
        return remote(part_proj.at[p], proj_tile(mine), pp_send, pp_recv, {"region": p})

    each(1, planes, lambda i: proj_to(i).start())
    keep_proj = pltpu.make_async_copy(part_proj.at[mine], proj_tile(mine), local_sem.at[3])
    keep_proj.start()

    hid_block_in(2)
    v_in_block(1)
    hid_block_in(3)
    v_in_block(2)
    u_in_block(0)
    keep_proj.wait()
    arrived(part_proj.at[0:planes - 1], pp_recv, sibling)

    def halo(by):
        return remote(
            own_proj.at[1], window.at[2 - by], halo_send, halo_recv,
            {"shard": wrap(pos + by, shards)},
        )

    for by in (-2, -1, 1, 2):
        halo(by).start()
    window[2] = own_proj[1]
    v_in_block(3)
    u_in_block(1)
    u_in_block(2)
    u_in_block(3)
    arrived(window.at[0:4], halo_recv, sibling)

    rows = 5 * blk
    dest = window[...].reshape(rows, hid)
    dest_top = dest.astype(BF16)
    proj[0:rows] = dest_top
    proj[128:128 + rows] = (dest - dest_top.astype(F32)).astype(BF16)
    anchor = own_proj[0]
    anchor_top = anchor.astype(BF16)
    proj[rows:rows + blk] = anchor_top
    proj[128 + rows:128 + rows + blk] = (anchor - anchor_top.astype(F32)).astype(BF16)

    group = 4
    size = group * slots
    wide = group_cols // 2
    turns = hid // wide

    def turn(n):
        return pl.ds(pl.multiple_of(n * wide, wide), wide)

    def hidden(n):
        both = jnp.concatenate([onehot[...], onehot[...]], axis=1)
        part = jnp.maximum(jnp.dot(both, proj[:, turn(n)], preferred_element_type=F32), 0.0).astype(BF16)
        first[:, turn(n)] = part
        first_t[turn(n), :] = part.T

    each(0, turns, hidden)
    arrived(weights.at[:, 1 - core], sb_recv, sibling)

    out_weight[...] = w_out[...].astype(F32).reshape(1, hid)

    def score(n):
        act = jnp.maximum(
            jnp.dot(first[...], weights[:, :, :, :, turn(n)].reshape(hid, wide), preferred_element_type=F32), 0.0
        )
        active[:, turn(n)] = act
        part = act * out_weight[:, turn(n)]
        lanes[...] += sum(part[:, k:k + 128] for k in range(0, wide, 128))

    lanes[...] = jnp.zeros_like(lanes)
    each(0, turns, score)
    col = jnp.sum(lanes[...], axis=1, keepdims=True)
    scores = jnp.zeros((slots, blk), F32)
    for b in range(blk):
        scores = jnp.where(lane16 == b, col[b * slots:(b + 1) * slots], scores)
    weight = out_weight[...]

    top = jnp.max(jnp.where(valid, scores, -jnp.inf), axis=0, keepdims=True)
    expo = jnp.where(valid, jnp.exp(scores - top), 0.0)
    mass = jnp.sum(expo, axis=0, keepdims=True)
    probs = expo / mass
    logp = scores - top - jnp.log(mass)
    sgrad = jnp.where(valid, probs * anchor_total - flow, 0.0)
    numer = -jnp.sum(jnp.where(valid, flow * logp, 0.0))
    total = jnp.sum(anchor_total)

    def pair_grads(i):
        return jnp.concatenate(
            [
                jnp.sum(jnp.where(lane16 == i * group + a, sgrad, 0.0), axis=1, keepdims=True)
                for a in range(group)
            ],
            axis=0,
        )

    def back(i):
        at = pl.multiple_of(i * size, size)
        pre[pl.ds(at, size), :] = jnp.where(active[pl.ds(at, size), :] > 0, pair_grads(i) * weight, 0.0).astype(BF16)

    each(0, blk // group, back)

    def to_sibling(n):
        return remote(
            grad.at[:, 1 - core, :, :, turn(n)], sib_grad.at[:, :, :, turn(n)], gs_send, gs_recv.at[n], sibling
        )

    def grads(n):
        part = jnp.dot(first_t[...], pre[:, turn(n)], preferred_element_type=F32)
        grad[:, :, :, :, turn(n)] = part.reshape(depth, 2, 2, 16, wide).astype(BF16)
        to_sibling(n).start()

    def to_u(n, h):
        uu = h * per_half + n // 2
        inside = pl.ds(pl.multiple_of((n % 2) * wide, wide), wide)
        return remote(
            chip_grad.at[:, h, :, turn(n)], u_in.at[u, :, :, inside],
            gu_send, gu_recv, at_uv(uu, v),
        )

    def join(n):
        to_sibling(n).wait_recv()
        mine_part = grad[:, core, :, :, turn(n)].astype(F32)
        chip_grad[:, :, :, turn(n)] = (mine_part + sib_grad[:, :, :, turn(n)].astype(F32)).astype(BF16)
        for h in range(2):

            @pl.when(h * per_half + n // 2 != u)
            def _():
                to_u(n, h).start()

    behind = 2

    def step(n):
        pl.when(n < turns)(lambda: grads(n))
        pl.when(n >= behind)(lambda: join(n - behind))

    each(0, turns + behind, step)

    def output_grad(i, acc):
        at = pl.multiple_of(i * size, size)
        return acc + jnp.sum((pair_grads(i) * active[pl.ds(at, size), :]).reshape(size // 8, 8, hid), axis=0)

    gout = lax.fori_loop(0, blk // group, output_grad, jnp.zeros((8, hid), F32))
    gout = jnp.sum(gout, axis=0, keepdims=True)
    width = hid // 8
    for r in range(8):
        extra[r:r + 1, :] = gout[:, r * width:(r + 1) * width]
    row = lax.broadcasted_iota(jnp.int32, (8, width), 0)
    extra[8:16, :] = jnp.where(row == 0, numer, jnp.where(row == 1, total, 0.0))

    def extra_to_z(i):
        return remote(extra, extra_z.at[z], ez_send, ez_recv, at_z(wrap(z + i, depth)))

    def extra_to_plane(i):
        to = {"region": wrap(mine + i, planes)}
        return remote(extra_zsum, extra_plane.at[mine], ep_send, ep_recv, to)

    each(1, depth, lambda i: extra_to_z(i).start())
    extra_z[z] = extra[...]

    def to_v(i):
        vv = wrap(v + i, side)
        part = u_sum.at[:, :, pl.ds(pl.multiple_of(vv * tile_cols, tile_cols), tile_cols)]
        return remote(part, v_in.at[v], gv_send, gv_recv, at_uv(u, vv))

    arrived(u_in.at[0:side - 1], gu_recv, sibling)

    own_group = span(u, 0, side)

    def sum_u(i):
        acc = chip_grad[pl.ds(i * zs, zs), u // per_half, :, own_group].astype(F32)
        for k in range(1, side):
            acc = acc + u_in[wrap(u + k, side), pl.ds(i * zs, zs)].astype(F32)
        u_sum[pl.ds(i * zs, zs)] = acc.astype(BF16)

    each(0, 4, sum_u)
    for i in range(1, side):
        to_v(i).start()

    def to_z(i):
        where = wrap(z + i, depth)
        return remote(plane_sum.at[where], z_in.at[z], gz_send, gz_recv, at_z(where))

    arrived(v_in.at[0:side - 1], gv_recv, sibling)
    own_cols = pl.ds(pl.multiple_of(v * tile_cols, tile_cols), tile_cols)
    acc = u_sum[:, :, own_cols].astype(F32)
    for k in range(1, side):
        acc = acc + v_in[wrap(v + k, side)].astype(F32)
    plane_sum[...] = acc.astype(BF16)
    to_z(depth // 2).start()

    def to_both(i):
        to_z(depth // 2 + i).start()
        to_z(depth // 2 - i).start()

    each(1, depth // 2, to_both)
    z_in[z] = plane_sum[z]

    arrived(extra_z.at[0:depth - 1], ez_recv, sibling)
    extra_zsum[...] = jnp.sum(extra_z[...], axis=0)
    each(1, planes, lambda i: extra_to_plane(i).start())
    extra_plane[mine] = extra_zsum[...]

    arrived(extra_plane.at[0:planes - 1], ep_recv, sibling)
    extra_psum[...] = jnp.sum(extra_plane[...], axis=0)
    extra_swap = remote(extra_psum, extra_sib, es_send, es_recv, sibling)
    extra_swap.start()
    extra_swap.wait_recv()
    sums_all = extra_psum[...] + extra_sib[...]
    inverse = 1.0 / sums_all[9:10, :]
    gout_out[...] = sums_all[0:8, :] * inverse
    loss_out[...] = sums_all[8:9, 0:1] * inverse[:, 0:1]

    arrived(z_in.at[0:depth - 1], gz_recv, sibling)
    own_rows[...] = jnp.sum(z_in[...].astype(F32), axis=0) * inverse[0:1, 0:1]

    def out_tile(p):
        py, px = p // side, p % side
        uu = py + core * (px - py)
        vv = px + core * (py - px)
        return grad_out.at[pl.ds(pl.multiple_of((uu // per_half) * 16, 16), 16), span(uu, vv, 1)]

    far_first = sorted(range(1, planes), key=lambda i: -sum(min(d, side - d) for d in divmod(i, side)))
    for i in far_first:
        to = at_uv(wrap(u + i // side, side), wrap(v + i % side, side))
        remote(own_rows, out_tile(mine), ga_send, ga_recv, to).start()
    own_out = pltpu.make_async_copy(own_rows, out_tile(mine), local_sem.at[1])
    own_out.start()

    left(tile_w.at[0:depth - 1, core], fz_send, sibling)
    left(tile_w.at[0:depth - 1, core], az_send, sibling)
    left(tile_w.at[:, core], fs_send, sibling)
    left(plane_feats.at[0:planes - 1], fp_send, sibling)
    left(part_proj.at[0:planes - 1], pp_send, sibling)
    left(window.at[0:4], halo_send, sibling)
    left(weight_part(0, depth, core, u, 0, side - 1), p1_send, sibling)
    left(weights.at[0:(side - 1) * depth // side, core], p2_send, sibling)
    left(weights.at[:, core], sb_send, sibling)
    left(sib_grad, gs_send, sibling)
    left(u_in.at[0:side - 1], gu_send, sibling)
    left(v_in.at[0:side - 1], gv_send, sibling)
    left(z_in.at[0:depth - 1], gz_send, sibling)
    left(extra_z.at[0:depth - 1], ez_send, sibling)
    left(extra_plane.at[0:planes - 1], ep_send, sibling)
    extra_swap.wait_send()
    own_out.wait()
    arrived(part_proj.at[0:planes - 1], ga_recv, sibling)
    left(part_proj.at[0:planes - 1], ga_send, sibling)


def shards(tiles, tile_block, neighbors, counts, flows, w_anchor, w_dest, w_hidden, w_out):
    planes, shard_count = lax.axis_size("region"), lax.axis_size("shard")
    side = 4 if planes == 16 else 2
    depth = shard_count // 2
    blk, slots = neighbors.shape
    feat, hid = tiles.shape[1], w_hidden.shape[1]
    pairs = blk * slots
    group_cols = hid // (side // 2)
    tile_cols = group_cols // side
    turns = hid // (group_cols // 2)
    width = hid // 8
    vmem = pl.BlockSpec(memory_space=pltpu.VMEM)
    hbm = pl.BlockSpec(memory_space=pltpu.HBM)
    dma = lambda n: pltpu.SemaphoreType.DMA((n,))
    one = pltpu.SemaphoreType.DMA
    scratch = [
        pltpu.VMEM(tiles.shape, BF16),
        pltpu.VMEM((1, tile_block.shape[0]), jnp.int32),
        pltpu.VMEM((blk, slots), jnp.int32),
        pltpu.SMEM((blk,), jnp.int32),
        pltpu.VMEM((blk, slots), jnp.int32),
        pltpu.VMEM((hid,), BF16),
        pltpu.VMEM((depth, 2, 2, 16, hid), BF16),
        pltpu.VMEM((blk, feat), BF16),
        pltpu.VMEM((depth, 2, 16, tile_cols), BF16),
        pltpu.VMEM((planes, blk, feat), BF16),
        pltpu.VMEM((planes, blk, tile_cols), F32),
        pltpu.VMEM((2, blk, hid), F32),
        pltpu.VMEM((5, blk, hid), F32),
        pltpu.VMEM((256, hid), BF16),
        pltpu.VMEM((pairs, 128), BF16),
        pltpu.VMEM((pairs, hid), BF16),
        pltpu.VMEM((hid, pairs), BF16),
        pltpu.VMEM((pairs, 128), F32),
        pltpu.VMEM((1, hid), F32),
        pltpu.VMEM((pairs, hid), F32),
        pltpu.VMEM((pairs, hid), BF16),
        pltpu.VMEM((depth, 2, 2, 16, hid), BF16),
        pltpu.VMEM((depth, 2, 16, hid), BF16),
        pltpu.VMEM((depth, 2, 16, hid), BF16),
        pltpu.VMEM((side, depth, 16, group_cols), BF16),
        pltpu.VMEM((depth, 16, group_cols), BF16),
        pltpu.VMEM((side, depth, 16, tile_cols), BF16),
        pltpu.VMEM((depth, 16, tile_cols), BF16),
        pltpu.VMEM((depth, 16, tile_cols), BF16),
        pltpu.VMEM((16, tile_cols), F32),
        pltpu.VMEM((16, width), F32),
        pltpu.VMEM((depth, 16, width), F32),
        pltpu.VMEM((16, width), F32),
        pltpu.VMEM((planes, 16, width), F32),
        pltpu.VMEM((16, width), F32),
        pltpu.VMEM((16, width), F32),
        one, one, one, dma(4), one, one, one, one, one, one,
        one, dma(4), one, dma(4), one, dma(4 * side), one, one,
        one, dma(turns), one, one, one, one, one, one,
        one, one, one, one, one, one, one, one, dma(6), dma(4),
    ]
    grad, gout, loss = pl.pallas_call(
        functools.partial(step_kernel, (side, depth, blk, slots, hid)),
        out_shape=(
            jax.ShapeDtypeStruct((w_hidden.shape[0], hid), F32),
            jax.ShapeDtypeStruct((8, width), F32),
            jax.ShapeDtypeStruct((1, 1), F32),
        ),
        in_specs=[hbm] * 9,
        out_specs=(hbm, vmem, vmem),
        scratch_shapes=scratch,
        compiler_params=pltpu.CompilerParams(
            collective_id=0, has_side_effects=True, vmem_limit_bytes=62 * 2 ** 20
        ),
        cost_estimate=pl.CostEstimate(
            flops=4 * pairs * hid * hid, bytes_accessed=2 * tiles.size, transcendentals=pairs
        ),
    )(tiles, tile_block.reshape(1, -1), neighbors, counts, flows, w_anchor, w_dest, w_hidden, w_out)
    return grad, gout.reshape(hid), loss.reshape(())


def solution(mesh):
    return jax.shard_map(
        shards,
        mesh=mesh,
        in_specs=(
            P(("region", "shard"), None),
            P(("region", "shard")),
            P(("region", "shard"), None),
            P(("region", "shard")),
            P(("region", "shard"), None),
            P("shard", None),
            P("shard", None),
            P("shard", None),
            P(),
        ),
        out_specs=(P("shard", None), P(), P()),
        check_vma=False,
    )
```

```python
import functools

import jax
import jax.numpy as jnp
from jax import lax
from jax.experimental import pallas as pl
from jax.experimental.pallas import tpu as pltpu
from jax.sharding import PartitionSpec as P

MESH = pl.DeviceIdType.MESH
BF16 = jnp.bfloat16
F32 = jnp.float32


def remote(src, dst, send, recv, where):
    return pltpu.make_async_remote_copy(
        src_ref=src, dst_ref=dst, send_sem=send, recv_sem=recv, device_id=where, device_id_type=MESH
    )


def arrived(ref, sem, where):
    remote(ref, ref, sem, sem, where).wait_recv()


def left(ref, sem, where):
    remote(ref, ref, sem, sem, where).wait_send()


def step_kernel(
    dims,
    tiles_hbm, tile_block_hbm, neighbors_hbm, counts_hbm, flows_hbm, anchor_hbm, dest_hbm, hidden_hbm, out_hbm,
    grad_out, gout_out, loss_out,
    tiles, tile_block, neighbors, counts, flows, w_out,
    weights, features, tile_w, plane_feats, part_proj, own_proj, window, proj, onehot, first, first_t, lanes, out_weight, active, pre, grad, sib_grad, chip_grad, u_in, u_sum, v_in,
    plane_sum, z_in, own_rows, extra, extra_z, extra_zsum, extra_plane, extra_psum, extra_sib,
    halo_send, halo_recv, fz_send, fz_recv, fz_pass, fs_send, fs_recv, fp_send, fp_recv, pp_send, pp_recv,
    az_send, az_recv, az_pass, p1_send, p1_recv, p2_send, p2_recv, sb_send, sb_recv,
    gs_send, gs_recv, gu_send, gu_recv, gv_send, gv_recv, gz_send, gz_recv,
    ga_send, ga_recv, ez_send, ez_recv, ep_send, ep_recv, es_send, es_recv, load_sem, local_sem,
):
    side, depth, blk, slots, hid = dims
    planes = side * side
    pos = lax.axis_index("shard")
    mine = lax.axis_index("region")
    z, core = pos // 2, pos % 2
    shards = 2 * depth
    feat = tiles.shape[1]
    y, x = mine // side, mine % side
    u = y + core * (x - y)
    v = x + core * (y - x)
    per_half = side // 2
    group_cols = hid // per_half
    tile_cols = group_cols // side

    def wrap(i, n):
        return lax.rem(i + 2 * n, n)

    def at_z(where):
        return {"shard": where * 2 + core}

    def at_uv(uu, vv):
        return {"region": (uu * side + vv) * (1 - core) + (vv * side + uu) * core}

    sibling = {"shard": z * 2 + (1 - core)}
    cross = {"shard": wrap(pos + 2 * core - 1, shards)}

    def each(first, last, act):
        def body(i, c):
            act(i)
            return c

        lax.fori_loop(first, last, body, 0)

    loads = [
        pltpu.make_async_copy(tiles_hbm, tiles, load_sem.at[0]),
        pltpu.make_async_copy(tile_block_hbm, tile_block, load_sem.at[1]),
        pltpu.make_async_copy(neighbors_hbm, neighbors, load_sem.at[2]),
        pltpu.make_async_copy(counts_hbm, counts, load_sem.at[3]),
        pltpu.make_async_copy(flows_hbm, flows, load_sem.at[4]),
        pltpu.make_async_copy(out_hbm, w_out, load_sem.at[5]),
    ]
    barrier = pltpu.get_barrier_semaphore()

    def greet(where):
        pl.semaphore_signal(barrier, inc=1, device_id=where, device_id_type=MESH)

    zs = depth // 4
    first_block = z // zs

    def greet_z(i):
        greet(at_z(wrap(z + zs - i, depth)))
        greet(at_z(wrap(z + i - zs, depth)))

    each(0, zs, greet_z)
    each(1, planes, lambda i: greet({"region": wrap(mine + i, planes)}))
    greet(cross)
    greet(sibling)
    for copy in loads:
        copy.start()

    def span(uu, first, count):
        at = (uu % per_half) * group_cols + first * tile_cols
        return pl.ds(pl.multiple_of(at, tile_cols), count * tile_cols)

    def weight_part(where, count, cc, uu, first, tiles_of):
        return weights.at[pl.ds(where, count), cc, uu // per_half, :, span(uu, first, tiles_of)]

    half_planes = planes // 2
    matrix = mine // half_planes
    first_cols = pl.ds(pl.multiple_of((mine % half_planes) * tile_cols, tile_cols), tile_cols)
    hid_tile = hidden_hbm.at[pl.ds(pl.multiple_of((u // per_half) * 16, 16), 16), span(u, v, 1)]

    def weight_slot(where):
        return weights.at[where, core, u // per_half, :, span(u, v, 1)]

    def first_to_z(by, source, far=None):
        sem = fz_recv.at[first_block] if far is None else fz_pass.at[far]
        return remote(source.at[:, first_cols], tile_w.at[z, core], fz_send, sem, at_z(wrap(z + by, depth)))

    def hid_to_z(by, far=None):
        sem = az_recv.at[first_block] if far is None else az_pass.at[far]
        return remote(hid_tile, weight_slot(z), az_send, sem, at_z(wrap(z + by, depth)))

    def keep_first(source):
        return pltpu.make_async_copy(source.at[:, first_cols], tile_w.at[z, core], local_sem.at[2])

    def spread_z(copy_to):
        copy_to(zs, 0).start()
        copy_to(-zs, 1).start()

        def both_ways(i):
            copy_to(zs - i).start()
            copy_to(i - zs).start()

        each(1, zs, both_ways)

    def pass_on(slot_of, send, recv, passed):
        for far, sign in ((0, 1), (1, -1)):
            slot = slot_of(wrap(z - sign * zs, depth))
            arrived(slot, passed.at[far], sibling)
            sem = recv.at[wrap(first_block - sign, 4)]

            def onward(i):
                remote(slot, slot, send, sem, at_z(wrap(z + sign * (zs - i), depth))).start()

            each(far, zs, onward)

    pl.semaphore_wait(barrier, planes - 1 + 2 * zs + 2)
    for k, source in enumerate((anchor_hbm, dest_hbm)):

        @pl.when(matrix == k)
        def _():
            spread_z(lambda by, far=None: first_to_z(by, source, far))
            keep_first(source).start()

    spread_z(hid_to_z)
    keep_tile = pltpu.make_async_copy(hid_tile, weight_slot(z), local_sem.at[0])
    keep_tile.start()

    loads[0].wait()
    loads[1].wait()
    member = tile_block[...] == lax.broadcasted_iota(jnp.int32, (blk, tile_block.shape[1]), 0)
    sums = jnp.dot(member.astype(BF16), tiles[...], preferred_element_type=F32)
    scale = lax.rsqrt(jnp.mean(sums * sums, axis=-1, keepdims=True) + 1e-05)
    features[...] = (sums * scale).astype(BF16)
    plane_feats[mine] = features[...]

    def feats_to(i):
        p = wrap(mine + i, planes)
        return remote(features, plane_feats.at[mine], fp_send, fp_recv, {"region": p})

    each(1, planes, lambda i: feats_to(i).start())
    pass_on(lambda where: tile_w.at[where, core], fz_send, fz_recv, fz_pass)
    pass_on(weight_slot, az_send, az_recv, az_pass)

    shift = mine * (blk * shards) + (pos - 2) * blk
    for copy in loads[2:]:
        copy.wait()
    place = (neighbors[...] - shift).astype(F32).T
    flow = flows[...].astype(F32).T
    lane16 = lax.broadcasted_iota(jnp.int32, (slots, blk), 1)
    count = jnp.zeros((1, blk), jnp.int32)
    for b in range(blk):
        count = jnp.where(lax.broadcasted_iota(jnp.int32, (1, blk), 1) == b, counts[b], count)
    valid = lax.broadcasted_iota(jnp.int32, (slots, blk), 0) < count
    lane = lax.broadcasted_iota(jnp.int32, (slots, 128), 1).astype(F32)
    for b in range(blk):
        here = (lane == place[:, b:b + 1]) | (lane == 5 * blk + b)
        onehot[b * slots:(b + 1) * slots, :] = jnp.where(here, 1.0, 0.0).astype(BF16)
    anchor_total = jnp.sum(flow, axis=0, keepdims=True)
    proj[...] = jnp.zeros_like(proj)
    keep_tile.wait()

    keep_first(anchor_hbm).wait()

    def block_at(n):
        return wrap(first_block + (0, 1, -1, 2)[n], 4)

    def along_v(b, i):
        tile = weight_part(b * zs, zs, core, u, v, 1)
        return remote(
            tile, tile, p1_send, p1_recv.at[b], at_uv(u, wrap(v + i, side))
        )

    def along_u(b, i):
        part = weight_part(b * zs, zs, core, u, 0, side)
        return remote(
            part, part, p2_send, p2_recv.at[b * side + i], at_uv(wrap(u + i, side), v)
        )

    def from_u(b, i):
        uu = wrap(u - i, side)
        part = weight_part(b * zs, zs, core, uu, 0, side)
        return remote(part, part, p2_send, p2_recv.at[b * side + i], at_uv(uu, v))

    def hand(b, i):
        part = weight_part(b * zs, zs, core, wrap(u - i, side), 0, side)
        return remote(part, part, sb_send, sb_recv, sibling)

    def hand_first(b):
        part = tile_w.at[pl.ds(b * zs, zs), core]
        return remote(part, part, fs_send, fs_recv, sibling)

    def first_block_in(n):
        b = block_at(n)
        others = zs if n == 3 else zs - 1
        if others:
            arrived(tile_w.at[pl.ds(b * zs, others), core], fz_recv.at[b], sibling)
        hand_first(b).start()

    def hid_block_in(n):
        b = block_at(n)
        others = zs if n == 3 else zs - 1
        if others:
            arrived(weight_part(b * zs, others, core, u, v, 1), az_recv.at[b], sibling)
        for i in range(1, side):
            along_v(b, i).start()

    def v_in_block(n):
        b = block_at(n)
        arrived(weight_part(b * zs, zs, core, u, 0, side - 1), p1_recv.at[b], sibling)
        for i in range(1, side):
            along_u(b, i).start()
        hand(b, 0).start()

    def u_in_block(n):
        b = block_at(n)
        for i in range(1, side):
            from_u(b, i).wait_recv()
            hand(b, i).start()

    first_block_in(0)
    hid_block_in(0)
    first_block_in(1)
    v_in_block(0)
    first_block_in(2)
    first_block_in(3)
    hid_block_in(1)

    arrived(plane_feats.at[0:planes - 1], fp_recv, sibling)
    arrived(tile_w.at[:, 1 - core], fs_recv, sibling)
    part_proj[...] = jnp.dot(
        plane_feats[...].reshape(planes * blk, feat), tile_w[...].reshape(feat, tile_cols),
        preferred_element_type=F32,
    ).reshape(planes, blk, tile_cols)

    def proj_tile(p):
        at = pl.multiple_of((p % half_planes) * tile_cols, tile_cols)
        return own_proj.at[p // half_planes, :, pl.ds(at, tile_cols)]

    def proj_to(i):
        p = wrap(mine + i, planes)
        return remote(part_proj.at[p], proj_tile(mine), pp_send, pp_recv, {"region": p})

    each(1, planes, lambda i: proj_to(i).start())
    keep_proj = pltpu.make_async_copy(part_proj.at[mine], proj_tile(mine), local_sem.at[3])
    keep_proj.start()

    hid_block_in(2)
    v_in_block(1)
    hid_block_in(3)
    v_in_block(2)
    u_in_block(0)
    keep_proj.wait()
    arrived(part_proj.at[0:planes - 1], pp_recv, sibling)

    def halo(by):
        return remote(
            own_proj.at[1], window.at[2 - by], halo_send, halo_recv,
            {"shard": wrap(pos + by, shards)},
        )

    for by in (-2, -1, 1, 2):
        halo(by).start()
    window[2] = own_proj[1]
    v_in_block(3)
    u_in_block(1)
    u_in_block(2)
    u_in_block(3)
    arrived(window.at[0:4], halo_recv, sibling)

    rows = 5 * blk
    dest = window[...].reshape(rows, hid)
    dest_top = dest.astype(BF16)
    proj[0:rows] = dest_top
    proj[128:128 + rows] = (dest - dest_top.astype(F32)).astype(BF16)
    anchor = own_proj[0]
    anchor_top = anchor.astype(BF16)
    proj[rows:rows + blk] = anchor_top
    proj[128 + rows:128 + rows + blk] = (anchor - anchor_top.astype(F32)).astype(BF16)

    group = 4
    size = group * slots
    wide = group_cols // 2
    turns = hid // wide

    def turn(n):
        return pl.ds(pl.multiple_of(n * wide, wide), wide)

    def hidden(n):
        both = jnp.concatenate([onehot[...], onehot[...]], axis=1)
        part = jnp.maximum(jnp.dot(both, proj[:, turn(n)], preferred_element_type=F32), 0.0).astype(BF16)
        first[:, turn(n)] = part
        first_t[turn(n), :] = part.T

    each(0, turns, hidden)
    arrived(weights.at[:, 1 - core], sb_recv, sibling)

    out_weight[...] = w_out[...].astype(F32).reshape(1, hid)

    def score(n):
        act = jnp.maximum(
            jnp.dot(first[...], weights[:, :, :, :, turn(n)].reshape(hid, wide), preferred_element_type=F32), 0.0
        )
        active[:, turn(n)] = act
        part = act * out_weight[:, turn(n)]
        lanes[...] += sum(part[:, k:k + 128] for k in range(0, wide, 128))

    lanes[...] = jnp.zeros_like(lanes)
    each(0, turns, score)
    col = jnp.sum(lanes[...], axis=1, keepdims=True)
    scores = jnp.zeros((slots, blk), F32)
    for b in range(blk):
        scores = jnp.where(lane16 == b, col[b * slots:(b + 1) * slots], scores)
    weight = out_weight[...]

    top = jnp.max(jnp.where(valid, scores, -jnp.inf), axis=0, keepdims=True)
    expo = jnp.where(valid, jnp.exp(scores - top), 0.0)
    mass = jnp.sum(expo, axis=0, keepdims=True)
    probs = expo / mass
    logp = scores - top - jnp.log(mass)
    sgrad = jnp.where(valid, probs * anchor_total - flow, 0.0)
    numer = -jnp.sum(jnp.where(valid, flow * logp, 0.0))
    total = jnp.sum(anchor_total)

    def pair_grads(i):
        return jnp.concatenate(
            [
                jnp.sum(jnp.where(lane16 == i * group + a, sgrad, 0.0), axis=1, keepdims=True)
                for a in range(group)
            ],
            axis=0,
        )

    def back(i):
        at = pl.multiple_of(i * size, size)
        pre[pl.ds(at, size), :] = jnp.where(active[pl.ds(at, size), :] > 0, pair_grads(i) * weight, 0.0).astype(BF16)

    each(0, blk // group, back)

    def to_sibling(n):
        return remote(
            grad.at[:, 1 - core, :, :, turn(n)], sib_grad.at[:, :, :, turn(n)], gs_send, gs_recv.at[n], sibling
        )

    def grads(n):
        part = jnp.dot(first_t[...], pre[:, turn(n)], preferred_element_type=F32)
        grad[:, :, :, :, turn(n)] = part.reshape(depth, 2, 2, 16, wide).astype(BF16)
        to_sibling(n).start()

    def to_u(n, h):
        uu = h * per_half + n // 2
        inside = pl.ds(pl.multiple_of((n % 2) * wide, wide), wide)
        return remote(
            chip_grad.at[:, h, :, turn(n)], u_in.at[u, :, :, inside],
            gu_send, gu_recv, at_uv(uu, v),
        )

    def join(n):
        to_sibling(n).wait_recv()
        mine_part = grad[:, core, :, :, turn(n)].astype(F32)
        chip_grad[:, :, :, turn(n)] = (mine_part + sib_grad[:, :, :, turn(n)].astype(F32)).astype(BF16)
        for h in range(2):

            @pl.when(h * per_half + n // 2 != u)
            def _():
                to_u(n, h).start()

    behind = 2

    def step(n):
        pl.when(n < turns)(lambda: grads(n))
        pl.when(n >= behind)(lambda: join(n - behind))

    each(0, turns + behind, step)

    def output_grad(i, acc):
        at = pl.multiple_of(i * size, size)
        return acc + jnp.sum((pair_grads(i) * active[pl.ds(at, size), :]).reshape(size // 8, 8, hid), axis=0)

    gout = lax.fori_loop(0, blk // group, output_grad, jnp.zeros((8, hid), F32))
    gout = jnp.sum(gout, axis=0, keepdims=True)
    width = hid // 8
    for r in range(8):
        extra[r:r + 1, :] = gout[:, r * width:(r + 1) * width]
    row = lax.broadcasted_iota(jnp.int32, (8, width), 0)
    extra[8:16, :] = jnp.where(row == 0, numer, jnp.where(row == 1, total, 0.0))

    def extra_to_z(i):
        return remote(extra, extra_z.at[z], ez_send, ez_recv, at_z(wrap(z + i, depth)))

    def extra_to_plane(i):
        to = {"region": wrap(mine + i, planes)}
        return remote(extra_zsum, extra_plane.at[mine], ep_send, ep_recv, to)

    each(1, depth, lambda i: extra_to_z(i).start())
    extra_z[z] = extra[...]

    def to_v(i):
        vv = wrap(v + i, side)
        part = u_sum.at[:, :, pl.ds(pl.multiple_of(vv * tile_cols, tile_cols), tile_cols)]
        return remote(part, v_in.at[v], gv_send, gv_recv, at_uv(u, vv))

    arrived(u_in.at[0:side - 1], gu_recv, sibling)

    own_group = span(u, 0, side)

    def sum_u(i):
        acc = chip_grad[pl.ds(i * zs, zs), u // per_half, :, own_group].astype(F32)
        for k in range(1, side):
            acc = acc + u_in[wrap(u + k, side), pl.ds(i * zs, zs)].astype(F32)
        u_sum[pl.ds(i * zs, zs)] = acc.astype(BF16)

    each(0, 4, sum_u)
    for i in range(1, side):
        to_v(i).start()

    def to_z(i):
        where = wrap(z + i, depth)
        return remote(plane_sum.at[where], z_in.at[z], gz_send, gz_recv, at_z(where))

    arrived(v_in.at[0:side - 1], gv_recv, sibling)
    own_cols = pl.ds(pl.multiple_of(v * tile_cols, tile_cols), tile_cols)
    acc = u_sum[:, :, own_cols].astype(F32)
    for k in range(1, side):
        acc = acc + v_in[wrap(v + k, side)].astype(F32)
    plane_sum[...] = acc.astype(BF16)
    to_z(depth // 2).start()

    def to_both(i):
        to_z(depth // 2 + i).start()
        to_z(depth // 2 - i).start()

    each(1, depth // 2, to_both)
    z_in[z] = plane_sum[z]

    arrived(extra_z.at[0:depth - 1], ez_recv, sibling)
    extra_zsum[...] = jnp.sum(extra_z[...], axis=0)
    each(1, planes, lambda i: extra_to_plane(i).start())
    extra_plane[mine] = extra_zsum[...]

    arrived(extra_plane.at[0:planes - 1], ep_recv, sibling)
    extra_psum[...] = jnp.sum(extra_plane[...], axis=0)
    extra_swap = remote(extra_psum, extra_sib, es_send, es_recv, sibling)
    extra_swap.start()
    extra_swap.wait_recv()
    sums_all = extra_psum[...] + extra_sib[...]
    inverse = 1.0 / sums_all[9:10, :]
    gout_out[...] = sums_all[0:8, :] * inverse
    loss_out[...] = sums_all[8:9, 0:1] * inverse[:, 0:1]

    arrived(z_in.at[0:depth - 1], gz_recv, sibling)
    own_rows[...] = jnp.sum(z_in[...].astype(F32), axis=0) * inverse[0:1, 0:1]

    def out_tile(p):
        py, px = p // side, p % side
        uu = py + core * (px - py)
        vv = px + core * (py - px)
        return grad_out.at[pl.ds(pl.multiple_of((uu // per_half) * 16, 16), 16), span(uu, vv, 1)]

    far_first = sorted(range(1, planes), key=lambda i: -sum(min(d, side - d) for d in divmod(i, side)))
    for i in far_first:
        to = at_uv(wrap(u + i // side, side), wrap(v + i % side, side))
        remote(own_rows, out_tile(mine), ga_send, ga_recv, to).start()
    own_out = pltpu.make_async_copy(own_rows, out_tile(mine), local_sem.at[1])
    own_out.start()

    left(tile_w.at[0:depth - 1, core], fz_send, sibling)
    left(tile_w.at[0:depth - 1, core], az_send, sibling)
    left(tile_w.at[:, core], fs_send, sibling)
    left(plane_feats.at[0:planes - 1], fp_send, sibling)
    left(part_proj.at[0:planes - 1], pp_send, sibling)
    left(window.at[0:4], halo_send, sibling)
    left(weight_part(0, depth, core, u, 0, side - 1), p1_send, sibling)
    left(weights.at[0:(side - 1) * depth // side, core], p2_send, sibling)
    left(weights.at[:, core], sb_send, sibling)
    left(sib_grad, gs_send, sibling)
    left(u_in.at[0:side - 1], gu_send, sibling)
    left(v_in.at[0:side - 1], gv_send, sibling)
    left(z_in.at[0:depth - 1], gz_send, sibling)
    left(extra_z.at[0:depth - 1], ez_send, sibling)
    left(extra_plane.at[0:planes - 1], ep_send, sibling)
    extra_swap.wait_send()
    own_out.wait()
    arrived(part_proj.at[0:planes - 1], ga_recv, sibling)
    left(part_proj.at[0:planes - 1], ga_send, sibling)


def shards(tiles, tile_block, neighbors, counts, flows, w_anchor, w_dest, w_hidden, w_out):
    planes, shard_count = lax.axis_size("region"), lax.axis_size("shard")
    side = 4 if planes == 16 else 2
    depth = shard_count // 2
    blk, slots = neighbors.shape
    feat, hid = tiles.shape[1], w_hidden.shape[1]
    pairs = blk * slots
    group_cols = hid // (side // 2)
    tile_cols = group_cols // side
    turns = hid // (group_cols // 2)
    width = hid // 8
    vmem = pl.BlockSpec(memory_space=pltpu.VMEM)
    hbm = pl.BlockSpec(memory_space=pltpu.HBM)
    dma = lambda n: pltpu.SemaphoreType.DMA((n,))
    one = pltpu.SemaphoreType.DMA
    scratch = [
        pltpu.VMEM(tiles.shape, BF16),
        pltpu.VMEM((1, tile_block.shape[0]), jnp.int32),
        pltpu.VMEM((blk, slots), jnp.int32),
        pltpu.SMEM((blk,), jnp.int32),
        pltpu.VMEM((blk, slots), jnp.int32),
        pltpu.VMEM((hid,), BF16),
        pltpu.VMEM((depth, 2, 2, 16, hid), BF16),
        pltpu.VMEM((blk, feat), BF16),
        pltpu.VMEM((depth, 2, 16, tile_cols), BF16),
        pltpu.VMEM((planes, blk, feat), BF16),
        pltpu.VMEM((planes, blk, tile_cols), F32),
        pltpu.VMEM((2, blk, hid), F32),
        pltpu.VMEM((5, blk, hid), F32),
        pltpu.VMEM((256, hid), BF16),
        pltpu.VMEM((pairs, 128), BF16),
        pltpu.VMEM((pairs, hid), BF16),
        pltpu.VMEM((hid, pairs), BF16),
        pltpu.VMEM((pairs, 128), F32),
        pltpu.VMEM((1, hid), F32),
        pltpu.VMEM((pairs, hid), F32),
        pltpu.VMEM((pairs, hid), BF16),
        pltpu.VMEM((depth, 2, 2, 16, hid), BF16),
        pltpu.VMEM((depth, 2, 16, hid), BF16),
        pltpu.VMEM((depth, 2, 16, hid), BF16),
        pltpu.VMEM((side, depth, 16, group_cols), BF16),
        pltpu.VMEM((depth, 16, group_cols), BF16),
        pltpu.VMEM((side, depth, 16, tile_cols), BF16),
        pltpu.VMEM((depth, 16, tile_cols), BF16),
        pltpu.VMEM((depth, 16, tile_cols), BF16),
        pltpu.VMEM((16, tile_cols), F32),
        pltpu.VMEM((16, width), F32),
        pltpu.VMEM((depth, 16, width), F32),
        pltpu.VMEM((16, width), F32),
        pltpu.VMEM((planes, 16, width), F32),
        pltpu.VMEM((16, width), F32),
        pltpu.VMEM((16, width), F32),
        one, one, one, dma(4), dma(2), one, one, one, one, one, one,
        one, dma(4), dma(2), one, dma(4), one, dma(4 * side), one, one,
        one, dma(turns), one, one, one, one, one, one,
        one, one, one, one, one, one, one, one, dma(6), dma(4),
    ]
    grad, gout, loss = pl.pallas_call(
        functools.partial(step_kernel, (side, depth, blk, slots, hid)),
        out_shape=(
            jax.ShapeDtypeStruct((w_hidden.shape[0], hid), F32),
            jax.ShapeDtypeStruct((8, width), F32),
            jax.ShapeDtypeStruct((1, 1), F32),
        ),
        in_specs=[hbm] * 9,
        out_specs=(hbm, vmem, vmem),
        scratch_shapes=scratch,
        compiler_params=pltpu.CompilerParams(
            collective_id=0, has_side_effects=True, vmem_limit_bytes=62 * 2 ** 20
        ),
        cost_estimate=pl.CostEstimate(
            flops=4 * pairs * hid * hid, bytes_accessed=2 * tiles.size, transcendentals=pairs
        ),
    )(tiles, tile_block.reshape(1, -1), neighbors, counts, flows, w_anchor, w_dest, w_hidden, w_out)
    return grad, gout.reshape(hid), loss.reshape(())


def solution(mesh):
    return jax.shard_map(
        shards,
        mesh=mesh,
        in_specs=(
            P(("region", "shard"), None),
            P(("region", "shard")),
            P(("region", "shard"), None),
            P(("region", "shard")),
            P(("region", "shard"), None),
            P("shard", None),
            P("shard", None),
            P("shard", None),
            P(),
        ),
        out_specs=(P("shard", None), P(), P()),
        check_vma=False,
    )
```

```python
import functools

import jax
import jax.numpy as jnp
from jax import lax
from jax.experimental import pallas as pl
from jax.experimental.pallas import tpu as pltpu
from jax.sharding import PartitionSpec as P

MESH = pl.DeviceIdType.MESH
BF16 = jnp.bfloat16
F32 = jnp.float32


def remote(src, dst, send, recv, where):
    return pltpu.make_async_remote_copy(
        src_ref=src, dst_ref=dst, send_sem=send, recv_sem=recv, device_id=where, device_id_type=MESH
    )


def arrived(ref, sem, where):
    remote(ref, ref, sem, sem, where).wait_recv()


def left(ref, sem, where):
    remote(ref, ref, sem, sem, where).wait_send()


def step_kernel(
    dims,
    tiles_hbm, tile_block_hbm, neighbors_hbm, counts_hbm, flows_hbm, anchor_hbm, dest_hbm, hidden_hbm, out_hbm,
    grad_out, gout_out, loss_out,
    tiles, tile_block, neighbors, counts, flows, w_out,
    weights, features, tile_w, plane_feats, part_proj, own_proj, window, proj, onehot, first, first_t, lanes, out_weight, active, pre, grad, sib_grad, chip_grad, u_in, u_sum, v_in,
    plane_sum, z_in, own_rows, extra, extra_sib, extra_own, extra_z, extra_zsum, extra_plane, extra_all,
    halo_send, halo_recv, fz_send, fz_recv, fz_pass, fs_send, fs_recv, fp_send, fp_recv, pp_send, pp_recv,
    az_send, az_recv, az_pass, p1_send, p1_recv, p2_send, p2_recv, sb_send, sb_recv,
    gs_send, gs_recv, gu_send, gu_recv, gv_send, gv_recv, gz_send, gz_recv,
    ga_send, ga_recv, ez_send, ez_recv, ep_send, ep_recv, ea_send, ea_recv, es_send, es_recv, load_sem, local_sem,
):
    side, depth, blk, slots, hid = dims
    planes = side * side
    pos = lax.axis_index("shard")
    mine = lax.axis_index("region")
    z, core = pos // 2, pos % 2
    shards = 2 * depth
    feat = tiles.shape[1]
    y, x = mine // side, mine % side
    u = y + core * (x - y)
    v = x + core * (y - x)
    per_half = side // 2
    group_cols = hid // per_half
    tile_cols = group_cols // side

    def wrap(i, n):
        return lax.rem(i + 2 * n, n)

    def at_z(where):
        return {"shard": where * 2 + core}

    def at_uv(uu, vv):
        return {"region": (uu * side + vv) * (1 - core) + (vv * side + uu) * core}

    sibling = {"shard": z * 2 + (1 - core)}
    cross = {"shard": wrap(pos + 2 * core - 1, shards)}

    def each(first, last, act):
        def body(i, c):
            act(i)
            return c

        lax.fori_loop(first, last, body, 0)

    loads = [
        pltpu.make_async_copy(tiles_hbm, tiles, load_sem.at[0]),
        pltpu.make_async_copy(tile_block_hbm, tile_block, load_sem.at[1]),
        pltpu.make_async_copy(neighbors_hbm, neighbors, load_sem.at[2]),
        pltpu.make_async_copy(counts_hbm, counts, load_sem.at[3]),
        pltpu.make_async_copy(flows_hbm, flows, load_sem.at[4]),
        pltpu.make_async_copy(out_hbm, w_out, load_sem.at[5]),
    ]
    barrier = pltpu.get_barrier_semaphore()

    def greet(where):
        pl.semaphore_signal(barrier, inc=1, device_id=where, device_id_type=MESH)

    zs = depth // 4
    first_block = z // zs

    def greet_z(i):
        greet(at_z(wrap(z + zs - i, depth)))
        greet(at_z(wrap(z + i - zs, depth)))

    each(0, zs, greet_z)
    each(1, planes, lambda i: greet({"region": wrap(mine + i, planes)}))
    greet(cross)
    greet(sibling)
    for copy in loads:
        copy.start()

    def span(uu, first, count):
        at = (uu % per_half) * group_cols + first * tile_cols
        return pl.ds(pl.multiple_of(at, tile_cols), count * tile_cols)

    def weight_part(where, count, cc, uu, first, tiles_of):
        return weights.at[pl.ds(where, count), cc, uu // per_half, :, span(uu, first, tiles_of)]

    half_planes = planes // 2
    matrix = mine // half_planes
    first_cols = pl.ds(pl.multiple_of((mine % half_planes) * tile_cols, tile_cols), tile_cols)
    hid_tile = hidden_hbm.at[pl.ds(pl.multiple_of((u // per_half) * 16, 16), 16), span(u, v, 1)]

    def weight_slot(where):
        return weights.at[where, core, u // per_half, :, span(u, v, 1)]

    def first_to_z(by, source, far=None):
        sem = fz_recv.at[first_block] if far is None else fz_pass.at[far]
        return remote(source.at[:, first_cols], tile_w.at[z, core], fz_send, sem, at_z(wrap(z + by, depth)))

    def hid_to_z(by, far=None):
        sem = az_recv.at[first_block] if far is None else az_pass.at[far]
        return remote(hid_tile, weight_slot(z), az_send, sem, at_z(wrap(z + by, depth)))

    def keep_first(source):
        return pltpu.make_async_copy(source.at[:, first_cols], tile_w.at[z, core], local_sem.at[2])

    def spread_z(copy_to):
        copy_to(zs, 0).start()
        copy_to(-zs, 1).start()

        def both_ways(i):
            copy_to(zs - i).start()
            copy_to(i - zs).start()

        each(1, zs, both_ways)

    def pass_on(slot_of, send, recv, passed):
        for far, sign in ((0, 1), (1, -1)):
            slot = slot_of(wrap(z - sign * zs, depth))
            arrived(slot, passed.at[far], sibling)
            sem = recv.at[wrap(first_block - sign, 4)]

            def onward(i):
                remote(slot, slot, send, sem, at_z(wrap(z + sign * (zs - i), depth))).start()

            each(far, zs, onward)

    pl.semaphore_wait(barrier, planes - 1 + 2 * zs + 2)
    for k, source in enumerate((anchor_hbm, dest_hbm)):

        @pl.when(matrix == k)
        def _():
            spread_z(lambda by, far=None: first_to_z(by, source, far))
            keep_first(source).start()

    spread_z(hid_to_z)
    keep_tile = pltpu.make_async_copy(hid_tile, weight_slot(z), local_sem.at[0])
    keep_tile.start()

    loads[0].wait()
    loads[1].wait()
    member = tile_block[...] == lax.broadcasted_iota(jnp.int32, (blk, tile_block.shape[1]), 0)
    sums = jnp.dot(member.astype(BF16), tiles[...], preferred_element_type=F32)
    scale = lax.rsqrt(jnp.mean(sums * sums, axis=-1, keepdims=True) + 1e-05)
    features[...] = (sums * scale).astype(BF16)
    plane_feats[mine] = features[...]

    def feats_to(i):
        p = wrap(mine + i, planes)
        return remote(features, plane_feats.at[mine], fp_send, fp_recv, {"region": p})

    each(1, planes, lambda i: feats_to(i).start())
    pass_on(lambda where: tile_w.at[where, core], fz_send, fz_recv, fz_pass)
    pass_on(weight_slot, az_send, az_recv, az_pass)

    shift = mine * (blk * shards) + (pos - 2) * blk
    for copy in loads[2:]:
        copy.wait()
    place = (neighbors[...] - shift).astype(F32).T
    flow = flows[...].astype(F32).T
    lane16 = lax.broadcasted_iota(jnp.int32, (slots, blk), 1)
    count = jnp.zeros((1, blk), jnp.int32)
    for b in range(blk):
        count = jnp.where(lax.broadcasted_iota(jnp.int32, (1, blk), 1) == b, counts[b], count)
    valid = lax.broadcasted_iota(jnp.int32, (slots, blk), 0) < count
    lane = lax.broadcasted_iota(jnp.int32, (slots, 128), 1).astype(F32)
    for b in range(blk):
        here = (lane == place[:, b:b + 1]) | (lane == 5 * blk + b)
        onehot[b * slots:(b + 1) * slots, :] = jnp.where(here, 1.0, 0.0).astype(BF16)
    anchor_total = jnp.sum(flow, axis=0, keepdims=True)
    proj[...] = jnp.zeros_like(proj)
    keep_tile.wait()

    keep_first(anchor_hbm).wait()

    def block_at(n):
        return wrap(first_block + (0, 1, -1, 2)[n], 4)

    def along_v(b, i):
        tile = weight_part(b * zs, zs, core, u, v, 1)
        return remote(
            tile, tile, p1_send, p1_recv.at[b], at_uv(u, wrap(v + i, side))
        )

    def along_u(b, i):
        part = weight_part(b * zs, zs, core, u, 0, side)
        return remote(
            part, part, p2_send, p2_recv.at[b * side + i], at_uv(wrap(u + i, side), v)
        )

    def from_u(b, i):
        uu = wrap(u - i, side)
        part = weight_part(b * zs, zs, core, uu, 0, side)
        return remote(part, part, p2_send, p2_recv.at[b * side + i], at_uv(uu, v))

    def hand(b, i):
        part = weight_part(b * zs, zs, core, wrap(u - i, side), 0, side)
        return remote(part, part, sb_send, sb_recv, sibling)

    def hand_first(b):
        part = tile_w.at[pl.ds(b * zs, zs), core]
        return remote(part, part, fs_send, fs_recv, sibling)

    def first_block_in(n):
        b = block_at(n)
        others = zs if n == 3 else zs - 1
        if others:
            arrived(tile_w.at[pl.ds(b * zs, others), core], fz_recv.at[b], sibling)
        hand_first(b).start()

    def hid_block_in(n):
        b = block_at(n)
        others = zs if n == 3 else zs - 1
        if others:
            arrived(weight_part(b * zs, others, core, u, v, 1), az_recv.at[b], sibling)
        for i in range(1, side):
            along_v(b, i).start()

    def v_in_block(n):
        b = block_at(n)
        arrived(weight_part(b * zs, zs, core, u, 0, side - 1), p1_recv.at[b], sibling)
        for i in range(1, side):
            along_u(b, i).start()
        hand(b, 0).start()

    def u_in_block(n):
        b = block_at(n)
        for i in range(1, side):
            from_u(b, i).wait_recv()
            hand(b, i).start()

    first_block_in(0)
    hid_block_in(0)
    first_block_in(1)
    v_in_block(0)
    first_block_in(2)
    first_block_in(3)
    hid_block_in(1)
    hid_block_in(2)

    arrived(plane_feats.at[0:planes - 1], fp_recv, sibling)
    arrived(tile_w.at[:, 1 - core], fs_recv, sibling)
    part_proj[...] = jnp.dot(
        plane_feats[...].reshape(planes * blk, feat), tile_w[...].reshape(feat, tile_cols),
        preferred_element_type=F32,
    ).reshape(planes, blk, tile_cols)

    def proj_tile(p):
        at = pl.multiple_of((p % half_planes) * tile_cols, tile_cols)
        return own_proj.at[p // half_planes, :, pl.ds(at, tile_cols)]

    def proj_to(i):
        p = wrap(mine + i, planes)
        return remote(part_proj.at[p], proj_tile(mine), pp_send, pp_recv, {"region": p})

    each(1, planes, lambda i: proj_to(i).start())
    keep_proj = pltpu.make_async_copy(part_proj.at[mine], proj_tile(mine), local_sem.at[3])
    keep_proj.start()

    hid_block_in(3)
    v_in_block(1)
    v_in_block(2)
    u_in_block(0)
    keep_proj.wait()
    arrived(part_proj.at[0:planes - 1], pp_recv, sibling)

    def halo(by):
        return remote(
            own_proj.at[1], window.at[2 - by], halo_send, halo_recv,
            {"shard": wrap(pos + by, shards)},
        )

    for by in (-2, -1, 1, 2):
        halo(by).start()
    window[2] = own_proj[1]
    v_in_block(3)
    u_in_block(1)
    u_in_block(2)
    u_in_block(3)
    arrived(window.at[0:4], halo_recv, sibling)

    rows = 5 * blk
    dest = window[...].reshape(rows, hid)
    dest_top = dest.astype(BF16)
    proj[0:rows] = dest_top
    proj[128:128 + rows] = (dest - dest_top.astype(F32)).astype(BF16)
    anchor = own_proj[0]
    anchor_top = anchor.astype(BF16)
    proj[rows:rows + blk] = anchor_top
    proj[128 + rows:128 + rows + blk] = (anchor - anchor_top.astype(F32)).astype(BF16)

    group = 4
    size = group * slots
    wide = group_cols // 2
    turns = hid // wide

    def turn(n):
        return pl.ds(pl.multiple_of(n * wide, wide), wide)

    def hidden(n):
        both = jnp.concatenate([onehot[...], onehot[...]], axis=1)
        part = jnp.maximum(jnp.dot(both, proj[:, turn(n)], preferred_element_type=F32), 0.0).astype(BF16)
        first[:, turn(n)] = part
        first_t[turn(n), :] = part.T

    each(0, turns, hidden)
    arrived(weights.at[:, 1 - core], sb_recv, sibling)

    out_weight[...] = w_out[...].astype(F32).reshape(1, hid)

    def score(n):
        act = jnp.maximum(
            jnp.dot(first[...], weights[:, :, :, :, turn(n)].reshape(hid, wide), preferred_element_type=F32), 0.0
        )
        active[:, turn(n)] = act
        part = act * out_weight[:, turn(n)]
        lanes[...] += sum(part[:, k:k + 128] for k in range(0, wide, 128))

    lanes[...] = jnp.zeros_like(lanes)
    each(0, turns, score)
    col = jnp.sum(lanes[...], axis=1, keepdims=True)
    scores = jnp.zeros((slots, blk), F32)
    for b in range(blk):
        scores = jnp.where(lane16 == b, col[b * slots:(b + 1) * slots], scores)
    weight = out_weight[...]

    top = jnp.max(jnp.where(valid, scores, -jnp.inf), axis=0, keepdims=True)
    expo = jnp.where(valid, jnp.exp(scores - top), 0.0)
    mass = jnp.sum(expo, axis=0, keepdims=True)
    probs = expo / mass
    logp = scores - top - jnp.log(mass)
    sgrad = jnp.where(valid, probs * anchor_total - flow, 0.0)
    numer = -jnp.sum(jnp.where(valid, flow * logp, 0.0))
    total = jnp.sum(anchor_total)

    def pair_grads(i):
        return jnp.concatenate(
            [
                jnp.sum(jnp.where(lane16 == i * group + a, sgrad, 0.0), axis=1, keepdims=True)
                for a in range(group)
            ],
            axis=0,
        )

    def back(i):
        at = pl.multiple_of(i * size, size)
        pre[pl.ds(at, size), :] = jnp.where(active[pl.ds(at, size), :] > 0, pair_grads(i) * weight, 0.0).astype(BF16)

    each(0, blk // group, back)

    def to_sibling(n):
        return remote(
            grad.at[:, 1 - core, :, :, turn(n)], sib_grad.at[:, :, :, turn(n)], gs_send, gs_recv.at[n], sibling
        )

    def grads(n):
        part = jnp.dot(first_t[...], pre[:, turn(n)], preferred_element_type=F32)
        grad[:, :, :, :, turn(n)] = part.reshape(depth, 2, 2, 16, wide).astype(BF16)
        to_sibling(n).start()

    def to_u(n, h):
        uu = h * per_half + n // 2
        inside = pl.ds(pl.multiple_of((n % 2) * wide, wide), wide)
        return remote(
            chip_grad.at[:, h, :, turn(n)], u_in.at[u, :, :, inside],
            gu_send, gu_recv, at_uv(uu, v),
        )

    def join(n):
        to_sibling(n).wait_recv()
        mine_part = grad[:, core, :, :, turn(n)].astype(F32)
        chip_grad[:, :, :, turn(n)] = (mine_part + sib_grad[:, :, :, turn(n)].astype(F32)).astype(BF16)
        for h in range(2):

            @pl.when(h * per_half + n // 2 != u)
            def _():
                to_u(n, h).start()

    behind = 2

    def step(n):
        pl.when(n < turns)(lambda: grads(n))
        pl.when(n >= behind)(lambda: join(n - behind))

    each(0, turns + behind, step)

    def output_grad(i, acc):
        at = pl.multiple_of(i * size, size)
        return acc + jnp.sum((pair_grads(i) * active[pl.ds(at, size), :]).reshape(size // 8, 8, hid), axis=0)

    gout = lax.fori_loop(0, blk // group, output_grad, jnp.zeros((8, hid), F32))
    gout = jnp.sum(gout, axis=0, keepdims=True)
    width = hid // 8
    for r in range(8):
        extra[0, r:r + 1, :] = gout[:, r * width:(r + 1) * width]
    row = lax.broadcasted_iota(jnp.int32, (8, width), 0)
    extra[1] = jnp.where(row == 0, numer, jnp.where(row == 1, total, 0.0))

    def extra_to_z(i):
        return remote(extra_own, extra_z.at[z], ez_send, ez_recv, at_z(wrap(z + i, depth)))

    def extra_to_plane(i):
        to = {"region": wrap(mine + i, planes)}
        return remote(extra_zsum, extra_plane.at[mine], ep_send, ep_recv, to)

    extra_half = remote(extra.at[1 - core], extra_sib, ea_send, ea_recv, sibling)
    extra_half.start()
    extra_half.wait_recv()
    extra_own[...] = extra[core] + extra_sib[...]
    each(1, depth, lambda i: extra_to_z(i).start())
    extra_z[z] = extra_own[...]

    def to_v(b, i):
        vv = wrap(v + i, side)
        zz = pl.ds(b * zs, zs)
        part = u_sum.at[zz, :, pl.ds(pl.multiple_of(vv * tile_cols, tile_cols), tile_cols)]
        return remote(part, v_in.at[v, zz], gv_send, gv_recv.at[b], at_uv(u, vv))

    arrived(u_in.at[0:side - 1], gu_recv, sibling)

    own_group = span(u, 0, side)

    def far_block(i):
        return wrap(first_block + 2 - i + (i // 2) * 3 - (i // 3) * 2, 4)

    def sum_u(i):
        b = far_block(i)
        part = pl.ds(b * zs, zs)
        acc = chip_grad[part, u // per_half, :, own_group].astype(F32)
        for k in range(1, side):
            acc = acc + u_in[wrap(u + k, side), part].astype(F32)
        u_sum[part] = acc.astype(BF16)
        for k in range(1, side):
            to_v(b, k).start()

    each(0, 4, sum_u)

    own_cols = pl.ds(pl.multiple_of(v * tile_cols, tile_cols), tile_cols)

    def sum_v(i):
        b = far_block(i)
        part = pl.ds(b * zs, zs)
        arrived(v_in.at[0:side - 1, part], gv_recv.at[b], sibling)
        acc = u_sum[part, :, own_cols].astype(F32)
        for k in range(1, side):
            acc = acc + v_in[wrap(v + k, side), part].astype(F32)
        plane_sum[part] = acc.astype(BF16)
        for k in range(zs):
            where = b * zs + k

            @pl.when(where != z)
            def _():
                remote(plane_sum.at[where], z_in.at[z], gz_send, gz_recv, at_z(where)).start()

    each(0, 4, sum_v)
    z_in[z] = plane_sum[z]

    arrived(extra_z.at[0:depth - 1], ez_recv, sibling)
    extra_zsum[...] = jnp.sum(extra_z[...], axis=0)
    each(1, planes, lambda i: extra_to_plane(i).start())
    extra_plane[mine] = extra_zsum[...]

    arrived(extra_plane.at[0:planes - 1], ep_recv, sibling)
    extra_all[core] = jnp.sum(extra_plane[...], axis=0)
    extra_swap = remote(extra_all.at[core], extra_all.at[core], es_send, es_recv, sibling)
    extra_swap.start()
    extra_swap.wait_recv()
    inverse = 1.0 / extra_all[1, 1:2, :]
    gout_out[...] = extra_all[0] * inverse
    loss_out[...] = extra_all[1, 0:1, 0:1] * inverse[:, 0:1]

    arrived(z_in.at[0:depth - 1], gz_recv, sibling)
    own_rows[...] = jnp.sum(z_in[...].astype(F32), axis=0) * inverse[0:1, 0:1]

    def out_tile(p):
        py, px = p // side, p % side
        uu = py + core * (px - py)
        vv = px + core * (py - px)
        return grad_out.at[pl.ds(pl.multiple_of((uu // per_half) * 16, 16), 16), span(uu, vv, 1)]

    far_first = sorted(range(1, planes), key=lambda i: -sum(min(d, side - d) for d in divmod(i, side)))
    for i in far_first:
        to = at_uv(wrap(u + i // side, side), wrap(v + i % side, side))
        remote(own_rows, out_tile(mine), ga_send, ga_recv, to).start()
    own_out = pltpu.make_async_copy(own_rows, out_tile(mine), local_sem.at[1])
    own_out.start()

    left(tile_w.at[0:depth - 1, core], fz_send, sibling)
    left(tile_w.at[0:depth - 1, core], az_send, sibling)
    left(tile_w.at[:, core], fs_send, sibling)
    left(plane_feats.at[0:planes - 1], fp_send, sibling)
    left(part_proj.at[0:planes - 1], pp_send, sibling)
    left(window.at[0:4], halo_send, sibling)
    left(weight_part(0, depth, core, u, 0, side - 1), p1_send, sibling)
    left(weights.at[0:(side - 1) * depth // side, core], p2_send, sibling)
    left(weights.at[:, core], sb_send, sibling)
    left(sib_grad, gs_send, sibling)
    left(u_in.at[0:side - 1], gu_send, sibling)
    left(v_in.at[0:side - 1], gv_send, sibling)
    left(z_in.at[0:depth - 1], gz_send, sibling)
    left(extra_z.at[0:depth - 1], ez_send, sibling)
    left(extra_plane.at[0:planes - 1], ep_send, sibling)
    extra_half.wait_send()
    extra_swap.wait_send()
    own_out.wait()
    arrived(part_proj.at[0:planes - 1], ga_recv, sibling)
    left(part_proj.at[0:planes - 1], ga_send, sibling)


def shards(tiles, tile_block, neighbors, counts, flows, w_anchor, w_dest, w_hidden, w_out):
    planes, shard_count = lax.axis_size("region"), lax.axis_size("shard")
    side = 4 if planes == 16 else 2
    depth = shard_count // 2
    blk, slots = neighbors.shape
    feat, hid = tiles.shape[1], w_hidden.shape[1]
    pairs = blk * slots
    group_cols = hid // (side // 2)
    tile_cols = group_cols // side
    turns = hid // (group_cols // 2)
    width = hid // 8
    vmem = pl.BlockSpec(memory_space=pltpu.VMEM)
    hbm = pl.BlockSpec(memory_space=pltpu.HBM)
    dma = lambda n: pltpu.SemaphoreType.DMA((n,))
    one = pltpu.SemaphoreType.DMA
    scratch = [
        pltpu.VMEM(tiles.shape, BF16),
        pltpu.VMEM((1, tile_block.shape[0]), jnp.int32),
        pltpu.VMEM((blk, slots), jnp.int32),
        pltpu.SMEM((blk,), jnp.int32),
        pltpu.VMEM((blk, slots), jnp.int32),
        pltpu.VMEM((hid,), BF16),
        pltpu.VMEM((depth, 2, 2, 16, hid), BF16),
        pltpu.VMEM((blk, feat), BF16),
        pltpu.VMEM((depth, 2, 16, tile_cols), BF16),
        pltpu.VMEM((planes, blk, feat), BF16),
        pltpu.VMEM((planes, blk, tile_cols), F32),
        pltpu.VMEM((2, blk, hid), F32),
        pltpu.VMEM((5, blk, hid), F32),
        pltpu.VMEM((256, hid), BF16),
        pltpu.VMEM((pairs, 128), BF16),
        pltpu.VMEM((pairs, hid), BF16),
        pltpu.VMEM((hid, pairs), BF16),
        pltpu.VMEM((pairs, 128), F32),
        pltpu.VMEM((1, hid), F32),
        pltpu.VMEM((pairs, hid), F32),
        pltpu.VMEM((pairs, hid), BF16),
        pltpu.VMEM((depth, 2, 2, 16, hid), BF16),
        pltpu.VMEM((depth, 2, 16, hid), BF16),
        pltpu.VMEM((depth, 2, 16, hid), BF16),
        pltpu.VMEM((side, depth, 16, group_cols), BF16),
        pltpu.VMEM((depth, 16, group_cols), BF16),
        pltpu.VMEM((side, depth, 16, tile_cols), BF16),
        pltpu.VMEM((depth, 16, tile_cols), BF16),
        pltpu.VMEM((depth, 16, tile_cols), BF16),
        pltpu.VMEM((16, tile_cols), F32),
        pltpu.VMEM((2, 8, width), F32),
        pltpu.VMEM((8, width), F32),
        pltpu.VMEM((8, width), F32),
        pltpu.VMEM((depth, 8, width), F32),
        pltpu.VMEM((8, width), F32),
        pltpu.VMEM((planes, 8, width), F32),
        pltpu.VMEM((2, 8, width), F32),
        one, one, one, dma(4), dma(2), one, one, one, one, one, one,
        one, dma(4), dma(2), one, dma(4), one, dma(4 * side), one, one,
        one, dma(turns), one, one, one, dma(4), one, one,
        one, one, one, one, one, one, one, one, one, one, dma(6), dma(4),
    ]
    grad, gout, loss = pl.pallas_call(
        functools.partial(step_kernel, (side, depth, blk, slots, hid)),
        out_shape=(
            jax.ShapeDtypeStruct((w_hidden.shape[0], hid), F32),
            jax.ShapeDtypeStruct((8, width), F32),
            jax.ShapeDtypeStruct((1, 1), F32),
        ),
        in_specs=[hbm] * 9,
        out_specs=(hbm, vmem, vmem),
        scratch_shapes=scratch,
        compiler_params=pltpu.CompilerParams(
            collective_id=0, has_side_effects=True, vmem_limit_bytes=62 * 2 ** 20
        ),
        cost_estimate=pl.CostEstimate(
            flops=4 * pairs * hid * hid, bytes_accessed=2 * tiles.size, transcendentals=pairs
        ),
    )(tiles, tile_block.reshape(1, -1), neighbors, counts, flows, w_anchor, w_dest, w_hidden, w_out)
    return grad, gout.reshape(hid), loss.reshape(())


def solution(mesh):
    return jax.shard_map(
        shards,
        mesh=mesh,
        in_specs=(
            P(("region", "shard"), None),
            P(("region", "shard")),
            P(("region", "shard"), None),
            P(("region", "shard")),
            P(("region", "shard"), None),
            P("shard", None),
            P("shard", None),
            P("shard", None),
            P(),
        ),
        out_specs=(P("shard", None), P(), P()),
        check_vma=False,
    )
```

```python
import functools

import jax
import jax.numpy as jnp
from jax import lax
from jax.experimental import pallas as pl
from jax.experimental.pallas import tpu as pltpu
from jax.sharding import PartitionSpec as P

MESH = pl.DeviceIdType.MESH
BF16 = jnp.bfloat16
F32 = jnp.float32


def remote(src, dst, send, recv, where):
    return pltpu.make_async_remote_copy(
        src_ref=src, dst_ref=dst, send_sem=send, recv_sem=recv, device_id=where, device_id_type=MESH
    )


def arrived(ref, sem, where):
    remote(ref, ref, sem, sem, where).wait_recv()


def left(ref, sem, where):
    remote(ref, ref, sem, sem, where).wait_send()


def step_kernel(
    dims,
    tiles_hbm, tile_block_hbm, neighbors_hbm, counts_hbm, flows_hbm, anchor_hbm, dest_hbm, hidden_hbm, out_hbm,
    grad_out, gout_out, loss_out,
    tiles, tile_block, neighbors, counts, flows, w_out,
    weights, features, tile_w, plane_feats, part_proj, own_proj, window, proj, onehot, first, first_t, lanes, active, pre, grad, sib_grad, chip_grad, u_in, u_sum, v_in,
    plane_sum, z_in, own_rows, extra, extra_sib, extra_own, extra_z, extra_zsum, extra_plane, extra_all,
    halo_send, halo_recv, fz_send, fz_recv, fz_pass, fs_send, fs_recv, fp_send, fp_recv, pp_send, pp_recv,
    az_send, az_recv, az_pass, p1_send, p1_recv, p2_send, p2_recv, sb_send, sb_recv,
    gs_send, gs_recv, gu_send, gu_recv, gv_send, gv_recv, gz_send, gz_recv,
    ga_send, ga_recv, ez_send, ez_recv, ep_send, ep_recv, ea_send, ea_recv, es_send, es_recv, load_sem, local_sem,
):
    side, depth, blk, slots, hid = dims
    planes = side * side
    pos = lax.axis_index("shard")
    mine = lax.axis_index("region")
    z, core = pos // 2, pos % 2
    shards = 2 * depth
    feat = tiles.shape[1]
    y, x = mine // side, mine % side
    u = y + core * (x - y)
    v = x + core * (y - x)
    per_half = side // 2
    group_cols = hid // per_half
    tile_cols = group_cols // side

    def wrap(i, n):
        return lax.rem(i + 2 * n, n)

    def at_z(where):
        return {"shard": where * 2 + core}

    def at_uv(uu, vv):
        return {"region": (uu * side + vv) * (1 - core) + (vv * side + uu) * core}

    sibling = {"shard": z * 2 + (1 - core)}
    cross = {"shard": wrap(pos + 2 * core - 1, shards)}

    def each(first, last, act):
        def body(i, c):
            act(i)
            return c

        lax.fori_loop(first, last, body, 0)

    loads = [
        pltpu.make_async_copy(tiles_hbm, tiles, load_sem.at[0]),
        pltpu.make_async_copy(tile_block_hbm, tile_block, load_sem.at[1]),
        pltpu.make_async_copy(neighbors_hbm, neighbors, load_sem.at[2]),
        pltpu.make_async_copy(counts_hbm, counts, load_sem.at[3]),
        pltpu.make_async_copy(flows_hbm, flows, load_sem.at[4]),
        pltpu.make_async_copy(out_hbm, w_out, load_sem.at[5]),
    ]
    barrier = pltpu.get_barrier_semaphore()

    def greet(where):
        pl.semaphore_signal(barrier, inc=1, device_id=where, device_id_type=MESH)

    zs = depth // 4
    first_block = z // zs

    def greet_z(i):
        greet(at_z(wrap(z + zs - i, depth)))
        greet(at_z(wrap(z + i - zs, depth)))

    each(0, zs, greet_z)
    each(1, planes, lambda i: greet({"region": wrap(mine + i, planes)}))
    greet(cross)
    greet(sibling)
    for copy in loads:
        copy.start()

    def span(uu, first, count):
        at = (uu % per_half) * group_cols + first * tile_cols
        return pl.ds(pl.multiple_of(at, tile_cols), count * tile_cols)

    def weight_part(where, count, cc, uu, first, tiles_of):
        return weights.at[pl.ds(where, count), cc, uu // per_half, :, span(uu, first, tiles_of)]

    half_planes = planes // 2
    matrix = mine // half_planes
    first_cols = pl.ds(pl.multiple_of((mine % half_planes) * tile_cols, tile_cols), tile_cols)
    hid_tile = hidden_hbm.at[pl.ds(pl.multiple_of((u // per_half) * 16, 16), 16), span(u, v, 1)]

    def weight_slot(where):
        return weights.at[where, core, u // per_half, :, span(u, v, 1)]

    def first_to_z(by, source, far=None):
        sem = fz_recv.at[first_block] if far is None else fz_pass.at[far]
        return remote(source.at[:, first_cols], tile_w.at[z, core], fz_send, sem, at_z(wrap(z + by, depth)))

    def hid_to_z(by, far=None):
        sem = az_recv.at[first_block] if far is None else az_pass.at[far]
        return remote(hid_tile, weight_slot(z), az_send, sem, at_z(wrap(z + by, depth)))

    def keep_first(source):
        return pltpu.make_async_copy(source.at[:, first_cols], tile_w.at[z, core], local_sem.at[2])

    def spread_z(copy_to):
        copy_to(zs, 0).start()
        copy_to(-zs, 1).start()

        def both_ways(i):
            copy_to(zs - i).start()
            copy_to(i - zs).start()

        each(1, zs, both_ways)

    def pass_on(slot_of, send, recv, passed):
        for far, sign in ((0, 1), (1, -1)):
            slot = slot_of(wrap(z - sign * zs, depth))
            arrived(slot, passed.at[far], sibling)
            sem = recv.at[wrap(first_block - sign, 4)]

            def onward(i):
                remote(slot, slot, send, sem, at_z(wrap(z + sign * (zs - i), depth))).start()

            each(far, zs, onward)

    pl.semaphore_wait(barrier, planes - 1 + 2 * zs + 2)
    for k, source in enumerate((anchor_hbm, dest_hbm)):

        @pl.when(matrix == k)
        def _():
            spread_z(lambda by, far=None: first_to_z(by, source, far))
            keep_first(source).start()

    spread_z(hid_to_z)
    keep_tile = pltpu.make_async_copy(hid_tile, weight_slot(z), local_sem.at[0])
    keep_tile.start()

    loads[0].wait()
    loads[1].wait()
    member = tile_block[...] == lax.broadcasted_iota(jnp.int32, (blk, tile_block.shape[1]), 0)
    sums = jnp.dot(member.astype(BF16), tiles[...], preferred_element_type=F32)
    scale = lax.rsqrt(jnp.mean(sums * sums, axis=-1, keepdims=True) + 1e-05)
    features[...] = (sums * scale).astype(BF16)
    plane_feats[mine] = features[...]

    def feats_to(i):
        p = wrap(mine + i, planes)
        return remote(features, plane_feats.at[mine], fp_send, fp_recv, {"region": p})

    each(1, planes, lambda i: feats_to(i).start())
    pass_on(lambda where: tile_w.at[where, core], fz_send, fz_recv, fz_pass)
    pass_on(weight_slot, az_send, az_recv, az_pass)

    shift = mine * (blk * shards) + (pos - 2) * blk
    for copy in loads[2:]:
        copy.wait()
    place = (neighbors[...] - shift).astype(F32).T
    flow = flows[...].astype(F32).T
    lane16 = lax.broadcasted_iota(jnp.int32, (slots, blk), 1)
    count = jnp.zeros((1, blk), jnp.int32)
    for b in range(blk):
        count = jnp.where(lax.broadcasted_iota(jnp.int32, (1, blk), 1) == b, counts[b], count)
    valid = lax.broadcasted_iota(jnp.int32, (slots, blk), 0) < count
    lane = lax.broadcasted_iota(jnp.int32, (slots, 128), 1).astype(F32)
    for b in range(blk):
        here = (lane == place[:, b:b + 1]) | (lane == 5 * blk + b)
        onehot[b * slots:(b + 1) * slots, :] = jnp.where(here, 1.0, 0.0).astype(BF16)
    anchor_total = jnp.sum(flow, axis=0, keepdims=True)
    proj[...] = jnp.zeros_like(proj)
    keep_tile.wait()

    keep_first(anchor_hbm).wait()

    def block_at(n):
        return wrap(first_block + (0, 1, -1, 2)[n], 4)

    def along_v(b, i):
        tile = weight_part(b * zs, zs, core, u, v, 1)
        return remote(
            tile, tile, p1_send, p1_recv.at[b], at_uv(u, wrap(v + i, side))
        )

    def along_u(b, i):
        part = weight_part(b * zs, zs, core, u, 0, side)
        return remote(
            part, part, p2_send, p2_recv.at[b * side + i], at_uv(wrap(u + i, side), v)
        )

    def from_u(b, i):
        uu = wrap(u - i, side)
        part = weight_part(b * zs, zs, core, uu, 0, side)
        return remote(part, part, p2_send, p2_recv.at[b * side + i], at_uv(uu, v))

    def hand(b, i):
        part = weight_part(b * zs, zs, core, wrap(u - i, side), 0, side)
        return remote(part, part, sb_send, sb_recv, sibling)

    def hand_first(b):
        part = tile_w.at[pl.ds(b * zs, zs), core]
        return remote(part, part, fs_send, fs_recv, sibling)

    def first_block_in(n):
        b = block_at(n)
        others = zs if n == 3 else zs - 1
        if others:
            arrived(tile_w.at[pl.ds(b * zs, others), core], fz_recv.at[b], sibling)
        hand_first(b).start()

    def hid_block_in(n):
        b = block_at(n)
        others = zs if n == 3 else zs - 1
        if others:
            arrived(weight_part(b * zs, others, core, u, v, 1), az_recv.at[b], sibling)
        for i in range(1, side):
            along_v(b, i).start()

    def v_in_block(n):
        b = block_at(n)
        arrived(weight_part(b * zs, zs, core, u, 0, side - 1), p1_recv.at[b], sibling)
        for i in range(1, side):
            along_u(b, i).start()
        hand(b, 0).start()

    def u_in_block(n):
        b = block_at(n)
        for i in range(1, side):
            from_u(b, i).wait_recv()
            hand(b, i).start()

    first_block_in(0)
    hid_block_in(0)
    first_block_in(1)
    v_in_block(0)
    first_block_in(2)
    first_block_in(3)
    hid_block_in(1)
    hid_block_in(2)

    arrived(plane_feats.at[0:planes - 1], fp_recv, sibling)
    arrived(tile_w.at[:, 1 - core], fs_recv, sibling)
    part_proj[...] = jnp.dot(
        plane_feats[...].reshape(planes * blk, feat), tile_w[...].reshape(feat, tile_cols),
        preferred_element_type=F32,
    ).reshape(planes, blk, tile_cols)

    def proj_tile(p):
        at = pl.multiple_of((p % half_planes) * tile_cols, tile_cols)
        return own_proj.at[p // half_planes, :, pl.ds(at, tile_cols)]

    def proj_to(i):
        p = wrap(mine + i, planes)
        return remote(part_proj.at[p], proj_tile(mine), pp_send, pp_recv, {"region": p})

    each(1, planes, lambda i: proj_to(i).start())
    keep_proj = pltpu.make_async_copy(part_proj.at[mine], proj_tile(mine), local_sem.at[3])
    keep_proj.start()

    hid_block_in(3)
    v_in_block(1)
    v_in_block(2)
    u_in_block(0)
    keep_proj.wait()
    arrived(part_proj.at[0:planes - 1], pp_recv, sibling)

    def halo(by):
        return remote(
            own_proj.at[1], window.at[2 - by], halo_send, halo_recv,
            {"shard": wrap(pos + by, shards)},
        )

    for by in (-2, -1, 1, 2):
        halo(by).start()
    window[2] = own_proj[1]
    v_in_block(3)
    u_in_block(1)
    u_in_block(2)
    u_in_block(3)
    arrived(window.at[0:4], halo_recv, sibling)

    rows = 5 * blk
    dest = window[...].reshape(rows, hid)
    dest_top = dest.astype(BF16)
    proj[0:rows] = dest_top
    proj[128:128 + rows] = (dest - dest_top.astype(F32)).astype(BF16)
    anchor = own_proj[0]
    anchor_top = anchor.astype(BF16)
    proj[rows:rows + blk] = anchor_top
    proj[128 + rows:128 + rows + blk] = (anchor - anchor_top.astype(F32)).astype(BF16)

    group = 4
    size = group * slots
    wide = group_cols // 2
    turns = hid // wide

    def turn(n):
        return pl.ds(pl.multiple_of(n * wide, wide), wide)

    def hidden(n):
        both = jnp.concatenate([onehot[...], onehot[...]], axis=1)
        part = jnp.maximum(jnp.dot(both, proj[:, turn(n)], preferred_element_type=F32), 0.0).astype(BF16)
        first[:, turn(n)] = part
        first_t[turn(n), :] = part.T

    each(0, turns, hidden)
    arrived(weights.at[:, 1 - core], sb_recv, sibling)

    def score(n):
        act = jnp.maximum(
            jnp.dot(first[...], weights[:, :, :, :, turn(n)].reshape(hid, wide), preferred_element_type=F32), 0.0
        )
        active[:, turn(n)] = act
        part = act * w_out[:, turn(n)]
        lanes[...] += sum(part[:, k:k + 128] for k in range(0, wide, 128))

    lanes[...] = jnp.zeros_like(lanes)
    each(0, turns, score)
    col = jnp.sum(lanes[...], axis=1, keepdims=True)
    scores = jnp.zeros((slots, blk), F32)
    for b in range(blk):
        scores = jnp.where(lane16 == b, col[b * slots:(b + 1) * slots], scores)
    weight = w_out[...]

    top = jnp.max(jnp.where(valid, scores, -jnp.inf), axis=0, keepdims=True)
    expo = jnp.where(valid, jnp.exp(scores - top), 0.0)
    mass = jnp.sum(expo, axis=0, keepdims=True)
    probs = expo / mass
    logp = scores - top - jnp.log(mass)
    sgrad = jnp.where(valid, probs * anchor_total - flow, 0.0)
    numer = -jnp.sum(jnp.where(valid, flow * logp, 0.0))
    total = jnp.sum(anchor_total)

    def pair_grads(i):
        return jnp.concatenate(
            [
                jnp.sum(jnp.where(lane16 == i * group + a, sgrad, 0.0), axis=1, keepdims=True)
                for a in range(group)
            ],
            axis=0,
        )

    def back(i):
        at = pl.multiple_of(i * size, size)
        pre[pl.ds(at, size), :] = jnp.where(active[pl.ds(at, size), :] > 0, pair_grads(i) * weight, 0.0).astype(BF16)

    each(0, blk // group, back)

    def to_sibling(n):
        return remote(
            grad.at[:, 1 - core, :, :, turn(n)], sib_grad.at[:, :, :, turn(n)], gs_send, gs_recv.at[n], sibling
        )

    def grads(n):
        part = jnp.dot(first_t[...], pre[:, turn(n)], preferred_element_type=F32)
        grad[:, :, :, :, turn(n)] = part.reshape(depth, 2, 2, 16, wide).astype(BF16)
        to_sibling(n).start()

    def to_u(n, h):
        uu = h * per_half + n // 2
        inside = pl.ds(pl.multiple_of((n % 2) * wide, wide), wide)
        return remote(
            chip_grad.at[:, h, :, turn(n)], u_in.at[u, :, :, inside],
            gu_send, gu_recv, at_uv(uu, v),
        )

    def join(n):
        to_sibling(n).wait_recv()
        mine_part = grad[:, core, :, :, turn(n)].astype(F32)
        chip_grad[:, :, :, turn(n)] = (mine_part + sib_grad[:, :, :, turn(n)].astype(F32)).astype(BF16)
        for h in range(2):

            @pl.when(h * per_half + n // 2 != u)
            def _():
                to_u(n, h).start()

    behind = 2

    def step(n):
        pl.when(n < turns)(lambda: grads(n))
        pl.when(n >= behind)(lambda: join(n - behind))

    each(0, turns + behind, step)

    def output_grad(i, acc):
        at = pl.multiple_of(i * size, size)
        return acc + jnp.sum((pair_grads(i) * active[pl.ds(at, size), :]).reshape(size // 8, 8, hid), axis=0)

    gout = lax.fori_loop(0, blk // group, output_grad, jnp.zeros((8, hid), F32))
    gout = jnp.sum(gout, axis=0, keepdims=True)
    width = hid // 8
    for r in range(8):
        extra[0, r:r + 1, :] = gout[:, r * width:(r + 1) * width]
    row = lax.broadcasted_iota(jnp.int32, (8, width), 0)
    extra[1] = jnp.where(row == 0, numer, jnp.where(row == 1, total, 0.0))

    def extra_to_z(i):
        return remote(extra_own, extra_z.at[z], ez_send, ez_recv, at_z(wrap(z + i, depth)))

    def extra_to_plane(i):
        to = {"region": wrap(mine + i, planes)}
        return remote(extra_zsum, extra_plane.at[mine], ep_send, ep_recv, to)

    extra_half = remote(extra.at[1 - core], extra_sib, ea_send, ea_recv, sibling)
    extra_half.start()
    extra_half.wait_recv()
    extra_own[...] = extra[core] + extra_sib[...]
    each(1, depth, lambda i: extra_to_z(i).start())
    extra_z[z] = extra_own[...]

    def to_v(b, i):
        vv = wrap(v + i, side)
        zz = pl.ds(b * zs, zs)
        part = u_sum.at[zz, :, pl.ds(pl.multiple_of(vv * tile_cols, tile_cols), tile_cols)]
        return remote(part, v_in.at[v, zz], gv_send, gv_recv.at[b], at_uv(u, vv))

    arrived(u_in.at[0:side - 1], gu_recv, sibling)

    own_group = span(u, 0, side)

    def far_block(i):
        return wrap(first_block + 2 - i + (i // 2) * 3 - (i // 3) * 2, 4)

    def sum_u(i):
        b = far_block(i)
        part = pl.ds(b * zs, zs)
        acc = chip_grad[part, u // per_half, :, own_group].astype(F32)
        for k in range(1, side):
            acc = acc + u_in[wrap(u + k, side), part].astype(F32)
        u_sum[part] = acc.astype(BF16)
        for k in range(1, side):
            to_v(b, k).start()

    each(0, 4, sum_u)

    own_cols = pl.ds(pl.multiple_of(v * tile_cols, tile_cols), tile_cols)

    def sum_v(i):
        b = far_block(i)
        part = pl.ds(b * zs, zs)
        arrived(v_in.at[0:side - 1, part], gv_recv.at[b], sibling)
        acc = u_sum[part, :, own_cols].astype(F32)
        for k in range(1, side):
            acc = acc + v_in[wrap(v + k, side), part].astype(F32)
        plane_sum[part] = acc.astype(BF16)
        for k in range(zs):
            where = b * zs + k

            @pl.when(where != z)
            def _():
                remote(plane_sum.at[where], z_in.at[z], gz_send, gz_recv, at_z(where)).start()

    each(0, 4, sum_v)
    z_in[z] = plane_sum[z]

    arrived(extra_z.at[0:depth - 1], ez_recv, sibling)
    extra_zsum[...] = jnp.sum(extra_z[...], axis=0)
    each(1, planes, lambda i: extra_to_plane(i).start())
    extra_plane[mine] = extra_zsum[...]

    arrived(extra_plane.at[0:planes - 1], ep_recv, sibling)
    extra_all[core] = jnp.sum(extra_plane[...], axis=0)
    extra_swap = remote(extra_all.at[core], extra_all.at[core], es_send, es_recv, sibling)
    extra_swap.start()
    extra_swap.wait_recv()
    inverse = 1.0 / extra_all[1, 1:2, :]
    gout_out[...] = extra_all[0] * inverse
    loss_out[...] = extra_all[1, 0:1, 0:1] * inverse[:, 0:1]

    arrived(z_in.at[0:depth - 1], gz_recv, sibling)
    own_rows[...] = jnp.sum(z_in[...].astype(F32), axis=0) * inverse[0:1, 0:1]

    def out_tile(p):
        py, px = p // side, p % side
        uu = py + core * (px - py)
        vv = px + core * (py - px)
        return grad_out.at[pl.ds(pl.multiple_of((uu // per_half) * 16, 16), 16), span(uu, vv, 1)]

    far_first = sorted(range(1, planes), key=lambda i: -sum(min(d, side - d) for d in divmod(i, side)))
    for i in far_first:
        to = at_uv(wrap(u + i // side, side), wrap(v + i % side, side))
        remote(own_rows, out_tile(mine), ga_send, ga_recv, to).start()
    own_out = pltpu.make_async_copy(own_rows, out_tile(mine), local_sem.at[1])
    own_out.start()

    left(tile_w.at[0:depth - 1, core], fz_send, sibling)
    left(tile_w.at[0:depth - 1, core], az_send, sibling)
    left(tile_w.at[:, core], fs_send, sibling)
    left(plane_feats.at[0:planes - 1], fp_send, sibling)
    left(part_proj.at[0:planes - 1], pp_send, sibling)
    left(window.at[0:4], halo_send, sibling)
    left(weight_part(0, depth, core, u, 0, side - 1), p1_send, sibling)
    left(weights.at[0:(side - 1) * depth // side, core], p2_send, sibling)
    left(weights.at[:, core], sb_send, sibling)
    left(sib_grad, gs_send, sibling)
    left(u_in.at[0:side - 1], gu_send, sibling)
    left(v_in.at[0:side - 1], gv_send, sibling)
    left(z_in.at[0:depth - 1], gz_send, sibling)
    left(extra_z.at[0:depth - 1], ez_send, sibling)
    left(extra_plane.at[0:planes - 1], ep_send, sibling)
    extra_half.wait_send()
    extra_swap.wait_send()
    own_out.wait()
    arrived(part_proj.at[0:planes - 1], ga_recv, sibling)
    left(part_proj.at[0:planes - 1], ga_send, sibling)


def shards(tiles, tile_block, neighbors, counts, flows, w_anchor, w_dest, w_hidden, w_out):
    planes, shard_count = lax.axis_size("region"), lax.axis_size("shard")
    side = 4 if planes == 16 else 2
    depth = shard_count // 2
    blk, slots = neighbors.shape
    feat, hid = tiles.shape[1], w_hidden.shape[1]
    pairs = blk * slots
    group_cols = hid // (side // 2)
    tile_cols = group_cols // side
    turns = hid // (group_cols // 2)
    width = hid // 8
    vmem = pl.BlockSpec(memory_space=pltpu.VMEM)
    hbm = pl.BlockSpec(memory_space=pltpu.HBM)
    dma = lambda n: pltpu.SemaphoreType.DMA((n,))
    one = pltpu.SemaphoreType.DMA
    scratch = [
        pltpu.VMEM(tiles.shape, BF16),
        pltpu.VMEM((1, tile_block.shape[0]), jnp.int32),
        pltpu.VMEM((blk, slots), jnp.int32),
        pltpu.SMEM((blk,), jnp.int32),
        pltpu.VMEM((blk, slots), jnp.int32),
        pltpu.VMEM((1, hid), F32),
        pltpu.VMEM((depth, 2, 2, 16, hid), BF16),
        pltpu.VMEM((blk, feat), BF16),
        pltpu.VMEM((depth, 2, 16, tile_cols), BF16),
        pltpu.VMEM((planes, blk, feat), BF16),
        pltpu.VMEM((planes, blk, tile_cols), F32),
        pltpu.VMEM((2, blk, hid), F32),
        pltpu.VMEM((5, blk, hid), F32),
        pltpu.VMEM((256, hid), BF16),
        pltpu.VMEM((pairs, 128), BF16),
        pltpu.VMEM((pairs, hid), BF16),
        pltpu.VMEM((hid, pairs), BF16),
        pltpu.VMEM((pairs, 128), F32),
        pltpu.VMEM((pairs, hid), F32),
        pltpu.VMEM((pairs, hid), BF16),
        pltpu.VMEM((depth, 2, 2, 16, hid), BF16),
        pltpu.VMEM((depth, 2, 16, hid), BF16),
        pltpu.VMEM((depth, 2, 16, hid), BF16),
        pltpu.VMEM((side, depth, 16, group_cols), BF16),
        pltpu.VMEM((depth, 16, group_cols), BF16),
        pltpu.VMEM((side, depth, 16, tile_cols), BF16),
        pltpu.VMEM((depth, 16, tile_cols), BF16),
        pltpu.VMEM((depth, 16, tile_cols), BF16),
        pltpu.VMEM((16, tile_cols), F32),
        pltpu.VMEM((2, 8, width), F32),
        pltpu.VMEM((8, width), F32),
        pltpu.VMEM((8, width), F32),
        pltpu.VMEM((depth, 8, width), F32),
        pltpu.VMEM((8, width), F32),
        pltpu.VMEM((planes, 8, width), F32),
        pltpu.VMEM((2, 8, width), F32),
        one, one, one, dma(4), dma(2), one, one, one, one, one, one,
        one, dma(4), dma(2), one, dma(4), one, dma(4 * side), one, one,
        one, dma(turns), one, one, one, dma(4), one, one,
        one, one, one, one, one, one, one, one, one, one, dma(6), dma(4),
    ]
    grad, gout, loss = pl.pallas_call(
        functools.partial(step_kernel, (side, depth, blk, slots, hid)),
        out_shape=(
            jax.ShapeDtypeStruct((w_hidden.shape[0], hid), F32),
            jax.ShapeDtypeStruct((8, width), F32),
            jax.ShapeDtypeStruct((1, 1), F32),
        ),
        in_specs=[hbm] * 9,
        out_specs=(hbm, vmem, vmem),
        scratch_shapes=scratch,
        compiler_params=pltpu.CompilerParams(
            collective_id=0, has_side_effects=True, vmem_limit_bytes=62 * 2 ** 20
        ),
        cost_estimate=pl.CostEstimate(
            flops=4 * pairs * hid * hid, bytes_accessed=2 * tiles.size, transcendentals=pairs
        ),
    )(tiles, tile_block.reshape(1, -1), neighbors, counts, flows, w_anchor, w_dest, w_hidden, w_out.astype(F32).reshape(1, -1))
    return grad, gout.reshape(hid), loss.reshape(())


def solution(mesh):
    return jax.shard_map(
        shards,
        mesh=mesh,
        in_specs=(
            P(("region", "shard"), None),
            P(("region", "shard")),
            P(("region", "shard"), None),
            P(("region", "shard")),
            P(("region", "shard"), None),
            P("shard", None),
            P("shard", None),
            P("shard", None),
            P(),
        ),
        out_specs=(P("shard", None), P(), P()),
        check_vma=False,
    )
```
